32 devices in a mesh: ty: 2 (over y), tx: 16 (over z, x, core).
Axes of the slice: x: 2, y: 2, z: 4, core: 2. Of those that a mesh axis runs over, the one named last changes fastest.
Arguments:
- tracer_start: float32 [48, 32, 2048], P(None, 'ty', 'tx'), may hold values from -6 to 6
- observed: bfloat16 [48, 32, 2048], P(None, 'ty', 'tx'), may hold values from -6 to 6
- east_speed: bfloat16 [48, 32, 2048], P(None, 'ty', 'tx'), may hold values from -4 to 4
- north_speed: bfloat16 [48, 32, 2048], P(None, 'ty', 'tx'), may hold values from -4 to 4
- mixing: bfloat16 [48, 32, 2048], P(None, 'ty', 'tx'), may hold values from 0.019897461 to 0.19921875
- vertical_mixing: bfloat16 [47, 32, 2048], P(None, 'ty', 'tx'), may hold values from 0.19921875 to 5
- relax_rate: bfloat16 [48, 32, 2048], P(None, 'ty', 'tx'), may hold values from 0.049804688 to 0.5
- level_count: int32 [32, 2048], P('ty', 'tx'), may hold values from 0 to 48, as said below
- face_east: int32 [32, 2048], P('ty', 'tx'), may hold values from 0 to 48, as said below
- face_north: int32 [32, 2048], P('ty', 'tx'), may hold values from 0 to 48, as said below
Outputs:
- adjoint_start: float32 [48, 32, 2048], P(None, 'ty', 'tx')
- mixing_gradient: float32 [48, 32, 2048], P(None, 'ty', 'tx')
The draws below stay inside these ranges and needn't reach their ends.
Inputs may be any that keep to these rules, and one draw needn't show every extreme that they name: Levels 0 to level_count - 1 of a column are water; 0 marks land. `face_east`: the smaller of the level counts of a column and of the next column east, the last column's next being the first. `face_north`: the smaller of the level counts of a column and of the next row's column north, the last row's next being the first.
All inputs are finite; a program needn't handle non-finite values.
Results may differ from the reference program's by a relative error of at most 0.0006.
Values sent between devices are 32-bit elements; how exact they have to be, the bound alone decides.
No kernel may reach another device: no remote copies, remote signals or barrier semaphores. Data moves between devices by JAX's collectives and lax.ppermute only.
A program may use at most 64 MiB of HBM per device.

```python
import math
import jax
import jax.numpy as jnp
from jax import lax

L = 48
NY = 32
NX = 2048


def level_tables(key):
    base = jax.random.fold_in(key, 11)
    key_land, key_depth = jax.random.split(base)
    land_cells = jax.random.randint(key_land, (NY, NX), 0, 5) == 0
    depths = jax.random.randint(key_depth, (NY, NX), 1, L + 1)
    counts = jnp.where(land_cells, 0, depths).astype(jnp.int32)
    counts = counts.at[0, 0].set(L).at[0, 1].set(L).at[1, 0].set(L).at[0, 2].set(0)
    east_levels = jnp.minimum(counts, jnp.roll(counts, -1, axis=1))
    north_levels = jnp.minimum(counts, jnp.roll(counts, -1, axis=0))
    return (counts, east_levels.astype(jnp.int32), north_levels.astype(jnp.int32))


def draw_level_count(key, part):
    return level_tables(key)[0]


def draw_face_east(key, part):
    return level_tables(key)[1]


def draw_face_north(key, part):
    return level_tables(key)[2]


def block_levels(rng, extent, cuts, smallest, largest):
    level = 1.0
    for position, blocks in cuts:
        draws = jax.random.uniform(jax.random.fold_in(jax.random.fold_in(rng, 6), position), (blocks,), jnp.float32, smallest / len(cuts), largest / len(cuts))
        level = level * jnp.repeat(jnp.exp(draws), extent[position] // blocks).reshape((-1,) + (1,) * (len(extent) - 1 - position))
    return level


def bell_draw(own_key, shape, deviation, limit, cuts=(), dtype=jnp.bfloat16):
    drawn = jax.random.normal(own_key, shape, jnp.float32) * deviation
    if len(cuts) > 0:
        drawn = block_levels(own_key, shape, cuts, -0.22, 0.18) * drawn
    return jnp.clip(drawn, min=-limit, max=limit).astype(dtype)


def setup_inputs(seed: int = 0) -> dict:
    keys = jax.random.split(jax.random.key(seed), 11)
    tracer_start = bell_draw(keys[0], (L, NY, NX), 1.0, 6.0, ((1, 2), (2, 16)), jnp.float32)
    observed = bell_draw(keys[1], (L, NY, NX), 1.0, 6.0, ((1, 2), (2, 16)))
    east_speed = bell_draw(keys[2], (L, NY, NX), 0.3, 4.0, ((1, 2), (2, 16)))
    north_speed = bell_draw(keys[3], (L, NY, NX), 0.3, 4.0, ((1, 2), (2, 16)))
    mixing = jnp.clip(jnp.exp(math.log(0.19921875) - 2.3038113 * jax.random.uniform(keys[4], (L, NY, NX), jnp.float32) ** block_levels(keys[4], (L, NY, NX), ((1, 2), (2, 16)), -0.2, 0.2)), 0.019897461, 0.19921875).astype(jnp.bfloat16)
    vertical_mixing = jnp.clip(jnp.exp(math.log(5.0) - 3.2227897 * jax.random.uniform(keys[5], (L - 1, NY, NX), jnp.float32) ** block_levels(keys[5], (L - 1, NY, NX), ((1, 2), (2, 16)), -0.2, 0.2)), 0.19921875, 5.0).astype(jnp.bfloat16)
    relax_rate = jnp.clip(jnp.exp(math.log(0.5) - 2.306499 * jax.random.uniform(keys[6], (L, NY, NX), jnp.float32) ** block_levels(keys[6], (L, NY, NX), ((1, 2), (2, 16)), -0.2, 0.2)), 0.049804688, 0.5).astype(jnp.bfloat16)
    level_count = draw_level_count(jax.random.fold_in(keys[10], 71), 0)
    face_east = draw_face_east(jax.random.fold_in(keys[10], 71), 0)
    face_north = draw_face_north(jax.random.fold_in(keys[10], 71), 0)
    return {"tracer_start": tracer_start, "observed": observed, "east_speed": east_speed, "north_speed": north_speed, "mixing": mixing, "vertical_mixing": vertical_mixing, "relax_rate": relax_rate, "level_count": level_count, "face_east": face_east, "face_north": face_north}


def solve_columns(rhs, level_links):
    levels = rhs.shape[0]
    nothing = jnp.zeros_like(rhs[0])
    ratios = []
    carries = []
    last_ratio = nothing
    last_carry = nothing
    for height in range(levels):
        upper_link = level_links[height - 1] if height > 0 else nothing
        lower_link = level_links[height] if height < levels - 1 else nothing
        divisor = 1.0 + upper_link + lower_link - upper_link * last_ratio
        last_carry = (rhs[height] + upper_link * last_carry) / divisor
        last_ratio = lower_link / divisor
        ratios.append(last_ratio)
        carries.append(last_carry)
    result = [carries[-1]]
    for height in range(levels - 2, -1, -1):
        result.append(carries[height] + ratios[height] * result[-1])
    return jnp.stack(result[::-1], axis=0)


def mask_levels(level_total, counts):
    heights = lax.broadcasted_iota(jnp.int32, (level_total,) + counts.shape, 0)
    return (heights < counts[None]).astype(jnp.float32)


def reference(tracer_start, observed, east_speed, north_speed, mixing, vertical_mixing, relax_rate, level_count, face_east, face_north):
    water = mask_levels(L, level_count)
    open_east = mask_levels(L, face_east)
    open_north = mask_levels(L, face_north)
    diffusion = mixing.astype(jnp.float32)
    speed_east = east_speed.astype(jnp.float32)
    speed_north = north_speed.astype(jnp.float32)
    east_minus = open_east * (0.5 * speed_east - diffusion)
    east_plus = open_east * (0.5 * speed_east + diffusion)
    north_minus = open_north * (0.5 * speed_north - diffusion)
    north_plus = open_north * (0.5 * speed_north + diffusion)
    level_links = vertical_mixing.astype(jnp.float32) * water[:-1] * water[1:]
    sink_rate = water * relax_rate.astype(jnp.float32)

    def advance(state):
        flux_east = east_plus * state + east_minus * jnp.roll(state, -1, 2)
        flux_north = north_plus * state + north_minus * jnp.roll(state, -1, 1)
        spread = (flux_east - jnp.roll(flux_east, 1, 2)) + (flux_north - jnp.roll(flux_north, 1, 1))
        return solve_columns(state - spread - sink_rate * jnp.tanh(state), level_links)

    def retreat(adjoint, state):
        solved = solve_columns(adjoint, level_links)
        grad_east = jnp.roll(solved, -1, 2) - solved
        grad_north = jnp.roll(solved, -1, 1) - solved
        squeeze = jnp.tanh(state)
        new_adjoint = solved * (1.0 - sink_rate * (1.0 - squeeze * squeeze))
        new_adjoint = new_adjoint + east_plus * grad_east + jnp.roll(east_minus * grad_east, 1, 2)
        new_adjoint = new_adjoint + north_plus * grad_north + jnp.roll(north_minus * grad_north, 1, 1)
        kappa_part = -(open_east * grad_east * (jnp.roll(state, -1, 2) - state) + open_north * grad_north * (jnp.roll(state, -1, 1) - state))
        return new_adjoint, kappa_part

    middle = advance(tracer_start)
    final_state = advance(middle)
    adjoint = water * (final_state - observed.astype(jnp.float32))
    adjoint, late_part = retreat(adjoint, middle)
    adjoint, early_part = retreat(adjoint, tracer_start)
    return adjoint, late_part + early_part
```

```python
import functools

import jax
import jax.numpy as jnp
from jax import lax
from jax.experimental import pallas as pl
from jax.experimental.pallas import tpu as pltpu
from jax.sharding import PartitionSpec as P

F32 = jnp.float32
VMEM = pl.BlockSpec(memory_space=pltpu.VMEM)
GROUP = 8
NAMES = ("s", "es", "ns", "mix", "relax", "vm", "obs")


def call(kernel, outs, scratch, *args):
    return pl.pallas_call(
        kernel,
        out_shape=[jax.ShapeDtypeStruct(shape, F32) for shape in outs],
        in_specs=[VMEM] * len(args),
        out_specs=[VMEM] * len(outs),
        scratch_shapes=[pltpu.VMEM(shape, F32) for shape in scratch],
        compiler_params=pltpu.CompilerParams(vmem_limit_bytes=16 << 20),
    )(*args)


def iota(shape, dim):
    return lax.broadcasted_iota(jnp.int32, shape, dim)


def roll(x, shift, axis):
    if isinstance(shift, int):
        shift = shift % x.shape[axis]
        if shift == 0:
            return x
    return pltpu.roll(x, shift, axis)


def odd_column():
    return lax.rem(lax.axis_index("tx"), 2) == 1


def level_of(ref, name, level):
    if name == "vm":
        level = jnp.minimum(level, ref.shape[0] - 1)
    return ref[level].astype(F32)


def edge_rows(block):
    return jnp.where(iota((8, block.shape[1]), 0) < 4, block[:8], block[-8:])


def near(shape):
    sub = iota(shape, 0)
    return (sub < 2) | (sub >= 6)


def pack_rows(get):
    tile = {name: edge_rows(get(name)) for name in NAMES[:6]}
    shape = tile["s"].shape
    sub = iota(shape, 0)
    first = jnp.where(near(shape), tile["s"], roll(tile["ns"], 4, 0))
    first = jnp.where(sub == 5, roll(tile["vm"], 5, 0), first)
    second = jnp.where((sub == 3) | (sub == 4), roll(tile["es"], 4, 0), tile["mix"])
    second = jnp.where((sub == 1) | (sub == 2), roll(tile["relax"], 2, 0), second)
    second = jnp.where(sub == 5, roll(tile["vm"], 6, 0), second)
    return first, second


def unpack_rows(first, second):
    sub = iota(first.shape, 0)
    return {
        "s": first,
        "ns": roll(first, 4, 0),
        "mix": second,
        "es": roll(second, 4, 0),
        "relax": roll(second, 6, 0),
        "vm": jnp.where(sub == 0, roll(first, 3, 0), roll(second, 2, 0)),
    }


def pack_kernel(s, es, ns, mix, relax, vm, obs, count, rows, corners, one, two, planes):
    refs = dict(zip(NAMES, (s, es, ns, mix, relax, vm, obs)))
    levels = s.shape[0]
    per_plane = 128 // GROUP
    plane_count = levels // per_plane
    shape = s.shape[1:]
    group = iota(shape, 1) // GROUP

    for a, name in enumerate(NAMES):
        def columns(p, carry, a=a, name=name):
            acc = jnp.zeros(shape, F32)
            for g in range(per_plane):
                x = level_of(refs[name], name, p * per_plane + g)
                acc = jnp.where(group == g, roll(x, GROUP * g + 4, 1), acc)
            planes[a * plane_count + p] = acc
            return carry

        lax.fori_loop(0, plane_count, columns, 0)
    total = len(NAMES) * plane_count
    count_plane = count[...].astype(F32)
    planes[total] = roll(count_plane, 4, 1)
    if (total + 1) % 2:
        planes[total + 1] = jnp.zeros(shape, F32)

    odd = odd_column()
    low = iota(shape, 1) % GROUP < 4
    for h in range(one.shape[0]):
        x, y = planes[2 * h], planes[2 * h + 1]
        to_east = jnp.where(low, x, roll(y, 4, 1))
        to_west = jnp.where(low, roll(x, -4, 1), y)
        one[h] = jnp.where(odd, to_west, to_east)
        two[h] = jnp.where(odd, to_east, to_west)

    small = (8, shape[1])
    small_group = iota(small, 1) // GROUP
    half = per_plane // 2

    def rims(p, carry):
        acc = jnp.zeros(small, F32)
        for m in range(half):
            level = p * half + m
            pair = pack_rows(lambda name: level_of(refs[name], name, level))
            for q in range(2):
                rows[2 * level + q] = pair[q]
                g = 2 * m + q
                acc = jnp.where(small_group == g, roll(pair[q], GROUP * g + 4, 1), acc)
        corners[p] = acc
        return carry

    lax.fori_loop(0, levels // half, rims, 0)
    count_rows = edge_rows(count_plane)
    rows[2 * levels] = count_rows
    corners[levels // half] = roll(count_rows, 4, 1)


def shift_up(x, axis):
    return roll(x, -1, axis)


def shift_down(x, axis):
    return roll(x, 1, axis)


def extend(main, side, rows=None, corners=None):
    top = jnp.concatenate([main, side], axis=1)
    if rows is None:
        return top
    return jnp.concatenate([top, jnp.concatenate([rows, corners], axis=1)], axis=0)


def solve_inward(levels, get, inv_q, carries):
    half = levels // 2
    inv, q = inv_q

    def step(t, carry):
        new = []
        for k, last in ((t, carry[0]), (levels - 1 - t, carry[1])):
            c = get(k) * inv(k) + q(k) * last
            carries[k] = c
            new.append(c)
        return tuple(new)

    zero = jnp.zeros(carries.shape[1:], F32)
    return lax.fori_loop(0, half, step, (zero, zero), unroll=2)


def solve_outward(levels, ends, ratio, join, carries, use):
    half = levels // 2
    high, low = ends
    upper = (high + ratio(half - 1) * low) * join
    lower = (low + ratio(half) * high) * join

    def step(t, carry):
        t = half - 1 - t
        new = []
        for k, last in ((t, carry[0]), (levels - 1 - t, carry[1])):
            x = carries[k] + ratio(k) * last
            use(k, x)
            new.append(x)
        return tuple(new)

    lax.fori_loop(0, half, step, (lower, upper), unroll=2)


def merge_halos(odd, from_one, from_two, planes):
    low = iota(from_one.shape[1:], 1) % GROUP < 4
    for h in range(from_one.shape[0]):
        a, b = from_one[h], from_two[h]
        west = jnp.where(odd, a, b)
        east = jnp.where(odd, b, a)
        planes[2 * h] = jnp.where(low, west, roll(east, 4, 1))
        planes[2 * h + 1] = jnp.where(low, roll(west, -4, 1), east)


def forward_kernel(
    s, es, ns, mix, relax, vm, obs, count, from_one, from_two, rows_n, rows_s, corner_one_n,
    corner_one_s, corner_two_n, corner_two_s,
    ep_out, em_out, np_out, nm_out, sink_out, inv_out, q_out, r_out, middle_out, solved_out,
    counts_out, join_out, start_out, send,
    planes, corners, rhs, links, carries,
):
    refs = dict(zip(NAMES, (s, es, ns, mix, relax, vm, obs)))
    levels = s.shape[0]
    half = levels // 2
    per_plane = 128 // GROUP
    plane_count = levels // per_plane
    odd = odd_column()
    merge_halos(odd, from_one, from_two, planes)
    small = (8, s.shape[2])
    low = iota(small, 1) % GROUP < 4
    north = iota(small, 0) < 4

    def rows_at(index):
        return rows_n[index], rows_s[index]

    def merge_first(n, s_):
        sub = iota(n.shape, 0)
        return jnp.where((sub < 2) | (sub == 4) | (sub == 5), n, s_)

    def merge_second(n, s_):
        sub = iota(n.shape, 0)
        return jnp.where((sub == 0) | (sub == 4) | (sub == 2), n, s_)

    def corner_plane(p):
        out = []
        for one_ref, two_ref in ((corner_one_n, corner_two_n), (corner_one_s, corner_two_s)):
            a, b = one_ref[p], two_ref[p]
            west = jnp.where(odd, a, b)
            east = jnp.where(odd, b, a)
            out.append(jnp.where(low, west, east))
        return out

    total = levels * 2 // per_plane
    first_group = (iota(small, 1) // GROUP) % 2 == 0
    for p in range(total):
        n, s_ = corner_plane(p)
        corners[p] = jnp.where(first_group, merge_first(n, s_), merge_second(n, s_))
    n, s_ = corner_plane(total)
    corners[total] = jnp.where(north, n, s_)

    last = len(NAMES) * plane_count
    count_ext = extend(
        count[...].astype(F32),
        roll(planes[last], 124, 1),
        jnp.where(north, rows_n[2 * levels], rows_s[2 * levels]),
        roll(corners[total], 124, 1),
    )
    east_count = jnp.minimum(count_ext, shift_up(count_ext, 1))
    north_count = jnp.minimum(count_ext, shift_up(count_ext, 0))
    counts_out[0] = count_ext
    counts_out[1] = east_count
    counts_out[2] = north_count

    def side_of(name, k):
        p = NAMES.index(name) * plane_count + k // per_plane
        return roll(planes[p], 124 - GROUP * (k % per_plane), 1)

    def load(k):
        pair = []
        for j, merge in enumerate((merge_first, merge_second)):
            index = 2 * k + j
            line = merge(rows_n[index], rows_s[index])
            corner = roll(corners[index // per_plane], 124 - GROUP * (index % per_plane), 1)
            pair.append(jnp.concatenate([line, corner], axis=1))
        rim = unpack_rows(*pair)
        return {
            name: jnp.concatenate(
                [extend(level_of(refs[name], name, k), side_of(name, k)), rim[name]], axis=0
            )
            for name in NAMES[:6]
        }

    def prepare(k, carry):
        x = load(k)
        level = k.astype(F32)
        state = x["s"]
        open_east = level < east_count
        open_north = level < north_count
        ep = jnp.where(open_east, 0.5 * x["es"] + x["mix"], 0.0)
        em = jnp.where(open_east, 0.5 * x["es"] - x["mix"], 0.0)
        np_ = jnp.where(open_north, 0.5 * x["ns"] + x["mix"], 0.0)
        nm = jnp.where(open_north, 0.5 * x["ns"] - x["mix"], 0.0)
        sink = jnp.where(level < count_ext, x["relax"], 0.0)
        link = jnp.where(level + 1.0 < count_ext, x["vm"], 0.0)
        ep_out[k] = ep
        em_out[k] = em
        np_out[k] = np_
        nm_out[k] = nm
        sink_out[k] = sink
        links[k] = link
        start_out[k] = state
        rhs[k] = advance(state, ep, em, np_, nm, sink)
        return carry

    def advance(state, ep, em, np_, nm, sink):
        fe = ep * state + em * shift_up(state, 1)
        fn = np_ * state + nm * shift_up(state, 0)
        spread = (fe - shift_down(fe, 1)) + (fn - shift_down(fn, 0))
        return state - spread - sink * jnp.tanh(state)

    lax.fori_loop(0, levels, prepare, 0)

    def factor(t, carry):
        (r_top, c_top), (r_low, c_low) = carry
        k = t
        above = jnp.where(k > 0, links[jnp.maximum(k - 1, 0)], 0.0)
        below = links[k]
        inv = 1.0 / (1.0 + above + below - above * r_top)
        q = above * inv
        r_top = below * inv
        c_top = rhs[k] * inv + q * c_top
        inv_out[k] = inv
        q_out[k] = q
        r_out[k] = r_top
        carries[k] = c_top
        k = levels - 1 - t
        above = links[k - 1]
        below = links[k]
        inv = 1.0 / (1.0 + above + below - below * r_low)
        q = below * inv
        r_low = above * inv
        c_low = rhs[k] * inv + q * c_low
        inv_out[k] = inv
        q_out[k] = q
        r_out[k] = r_low
        carries[k] = c_low
        return (r_top, c_top), (r_low, c_low)

    zero = jnp.zeros(rhs.shape[1:], F32)
    (r_top, c_top), (r_low, c_low) = lax.fori_loop(
        0, half, factor, ((zero, zero), (zero, zero)), unroll=2
    )
    join = 1.0 / (1.0 - r_top * r_low)
    join_out[...] = join

    def to_second(k, x):
        middle_out[k] = x
        value = advance(x, ep_out[k], em_out[k], np_out[k], nm_out[k], sink_out[k])
        rhs[k, :16] = value[:16]

    solve_outward(levels, (c_top, c_low), lambda k: r_out[k], join, carries, to_second)

    main = carries.at[:, :16]
    inv_q = (lambda k: inv_out[k, :16], lambda k: q_out[k, :16])
    ratio = lambda k: r_out[k, :16]
    ends = solve_inward(levels, lambda k: rhs[k, :16], inv_q, main)

    def to_adjoint(k, x):
        seen = extend(level_of(refs["obs"], "obs", k), side_of("obs", k))
        rhs[k, :16] = jnp.where(k.astype(F32) < count_ext[:16], x - seen, 0.0)

    solve_outward(levels, ends, ratio, join[:16], main, to_adjoint)
    ends = solve_inward(levels, lambda k: rhs[k, :16], inv_q, main)

    def to_solved(k, x):
        solved_out[k] = x

    solve_outward(levels, ends, ratio, join[:16], main, to_solved)

    group = iota(small, 1) // GROUP
    for p in range(send.shape[0] - half):
        acc = jnp.zeros(small, F32)
        for g in range(min(per_plane, half - p * per_plane)):
            t = p * per_plane + g
            x = edge_rows(solved_out[t])
            y = edge_rows(solved_out[levels - 1 - t])
            both = jnp.where(near(x.shape), x, roll(y, 4, 0))
            send[t] = both[:, :128]
            acc = jnp.where(
                group == g, roll(both[:, 128:], GROUP * g + 4, 1), acc
            )
        send[half + p] = acc


def backward_kernel(
    ep, em, np_, nm, sink, inv, q, r, middle, solved, counts, join, start, rows_n, rows_s,
    adjoint_out, gradient_out, carries,
):
    levels = solved.shape[0]
    half = levels // 2
    per_plane = 128 // GROUP
    small = (8, 128)
    sub = iota(small, 0)
    from_north = (sub < 2) | (sub == 4) | (sub == 5)

    def rims(t):
        line = jnp.where(from_north, rows_n[t], rows_s[t])
        p = half + t // per_plane
        corner = jnp.where(from_north, rows_n[p], rows_s[p])
        corner = roll(corner, 124 - GROUP * (t % per_plane), 1)
        both = jnp.concatenate([line, corner], axis=1)
        return both, roll(both, 4, 0)

    def pull(k, x, state):
        ge = shift_up(x, 1) - x
        gn = shift_up(x, 0) - x
        squeeze = jnp.tanh(state)
        result = x * (1.0 - sink[k] * (1.0 - squeeze * squeeze))
        result = result + ep[k] * ge + shift_down(em[k] * ge, 1)
        result = result + np_[k] * gn + shift_down(nm[k] * gn, 0)
        level = k.astype(F32)
        part = jnp.where(level < counts[1], ge * (shift_up(state, 1) - state), 0.0)
        part = part + jnp.where(level < counts[2], gn * (shift_up(state, 0) - state), 0.0)
        return result, part

    def late(t, carry):
        new = []
        for k, rim, last in zip((t, levels - 1 - t), rims(t), carry):
            x = jnp.concatenate([solved[k], rim], axis=0)
            result, part = pull(k, x, middle[k])
            gradient_out[k] = -part[:16, :128]
            c = result * inv[k] + q[k] * last
            carries[k] = c
            new.append(c)
        return tuple(new)

    zero = jnp.zeros(carries.shape[1:], F32)
    ends = lax.fori_loop(0, half, late, (zero, zero))

    def early(k, x):
        result, part = pull(k, x, start[k])
        adjoint_out[k] = result[:16, :128]
        gradient_out[k] = gradient_out[k] - part[:16, :128]

    solve_outward(levels, ends, lambda k: r[k], join[...], carries, early)


def ring(axis, distance):
    count = lax.axis_size(axis)
    return [(i, (i + distance) % count) for i in range(count)]


def both_ways(x):
    from_north = lax.ppermute(x, "ty", ring("ty", -1))
    if lax.axis_size("ty") == 2:
        return from_north, from_north
    return from_north, lax.ppermute(x, "ty", ring("ty", 1))


def swap(x, phase, rise):
    ny, nx = lax.axis_size("ty"), lax.axis_size("tx")
    route = []
    for j in range(ny):
        for i in range(nx):
            partner = (i + 1) % nx if i % 2 == phase else (i - 1) % nx
            route.append((j * nx + i, ((j + rise) % ny) * nx + partner))
    return lax.ppermute(x, ("ty", "tx"), route)


def diagonal(x, phase):
    from_north = swap(x, phase, -1)
    if lax.axis_size("ty") == 2:
        return from_north, from_north
    return from_north, swap(x, phase, 1)


def per_device(
    tracer_start,
    observed,
    east_speed,
    north_speed,
    mixing,
    vertical_mixing,
    relax_rate,
    level_count,
    face_east,
    face_north,
):
    levels, ny, nx = tracer_start.shape
    per_plane = 128 // GROUP
    plane_count = levels // per_plane
    pairs = (len(NAMES) * plane_count + 2) // 2
    fields = (
        tracer_start, east_speed, north_speed, mixing, relax_rate, vertical_mixing, observed,
        level_count,
    )
    corner_planes = 2 * levels // per_plane + 1
    rows, corners, one, two = call(
        pack_kernel,
        [
            (2 * levels + 1, 8, nx),
            (corner_planes, 8, nx),
            (pairs, ny, nx),
            (pairs, ny, nx),
        ],
        [(2 * pairs, ny, nx)],
        *fields,
    )
    rows_n, rows_s = both_ways(rows)
    from_two = swap(two, 1, 0)
    corner_two_n, corner_two_s = diagonal(corners, 1)
    from_one = swap(one, 0, 0)
    corner_one_n, corner_one_s = diagonal(corners, 0)
    ext = (levels, ny + 8, 2 * nx)
    half = levels // 2
    outs = call(
        forward_kernel,
        [ext] * 9 + [(levels, ny, 2 * nx), (3,) + ext[1:], ext[1:], ext]
        + [(half + -(-half // per_plane), 8, nx)],
        [(2 * pairs, ny, nx), (corner_planes, 8, nx), ext, ext, ext],
        *fields, from_one, from_two, rows_n, rows_s,
        corner_one_n, corner_one_s, corner_two_n, corner_two_s,
    )
    ep, em, np_, nm, sink, inv, q, r, middle, solved, counts, join, start, send = outs
    sent_n, sent_s = both_ways(send)
    adjoint, gradient = call(
        backward_kernel,
        [(levels, ny, nx)] * 2,
        [ext],
        ep, em, np_, nm, sink, inv, q, r, middle, solved, counts, join, start, sent_n, sent_s,
    )
    return adjoint, gradient


def solution(mesh):
    block = P(None, "ty", "tx")
    plane = P("ty", "tx")
    return jax.shard_map(
        per_device,
        mesh=mesh,
        in_specs=(block,) * 7 + (plane,) * 3,
        out_specs=(block, block),
        check_vma=False,
    )
```

```python
import functools

import jax
import jax.numpy as jnp
from jax import lax
from jax.experimental import pallas as pl
from jax.experimental.pallas import tpu as pltpu
from jax.sharding import PartitionSpec as P

F32 = jnp.float32
VMEM = pl.BlockSpec(memory_space=pltpu.VMEM)
HBM = pl.BlockSpec(memory_space=pltpu.HBM)
UNROLL = 8
GROUP = 8
NAMES = ("s", "es", "ns", "mix", "relax", "vm", "obs")


def call(kernel, outs, scratch, *args, space=VMEM):
    def typed(x):
        return x if isinstance(x, jax.ShapeDtypeStruct) else jax.ShapeDtypeStruct(x, F32)

    return pl.pallas_call(
        kernel,
        out_shape=[typed(x) for x in outs],
        in_specs=[space] * len(args),
        out_specs=[VMEM] * len(outs),
        scratch_shapes=[pltpu.VMEM(x, F32) if isinstance(x, tuple) else x for x in scratch],
        compiler_params=pltpu.CompilerParams(vmem_limit_bytes=16 << 20),
    )(*args)


def iota(shape, dim):
    return lax.broadcasted_iota(jnp.int32, shape, dim)


def roll(x, shift, axis):
    if isinstance(shift, int):
        shift = shift % x.shape[axis]
        if shift == 0:
            return x
    return pltpu.roll(x, shift, axis)


def odd_column():
    return lax.rem(lax.axis_index("tx"), 2) == 1


def level_of(ref, name, level):
    if name == "vm":
        level = jnp.minimum(level, ref.shape[0] - 1)
    return ref[level].astype(F32)


def edge_rows(block):
    return jnp.where(iota((8, block.shape[1]), 0) < 4, block[:8], block[-8:])


def near(shape):
    sub = iota(shape, 0)
    return (sub < 2) | (sub >= 6)


def pack_rows(get):
    tile = {name: edge_rows(get(name)) for name in NAMES[:6]}
    shape = tile["s"].shape
    sub = iota(shape, 0)
    first = jnp.where(near(shape), tile["s"], roll(tile["ns"], 4, 0))
    first = jnp.where(sub == 5, roll(tile["vm"], 5, 0), first)
    second = jnp.where((sub == 3) | (sub == 4), roll(tile["es"], 4, 0), tile["mix"])
    second = jnp.where((sub == 1) | (sub == 2), roll(tile["relax"], 2, 0), second)
    second = jnp.where(sub == 5, roll(tile["vm"], 6, 0), second)
    return first, second


def unpack_rows(first, second):
    sub = iota(first.shape, 0)
    return {
        "s": first,
        "ns": roll(first, 4, 0),
        "mix": second,
        "es": roll(second, 4, 0),
        "relax": roll(second, 6, 0),
        "vm": jnp.where(sub == 0, roll(first, 3, 0), roll(second, 2, 0)),
    }


def pack_kernel(*args):
    fields = args[:8]
    s, es, ns, mix, relax, vm, obs, count = kept = args[8:16]
    rows, corners, one, two, planes, arrived = args[16:]
    copies = [pltpu.make_async_copy(fields[i], kept[i], arrived.at[i]) for i in range(8)]
    for copy in copies:
        copy.start()
    refs = dict(zip(NAMES, (s, es, ns, mix, relax, vm, obs)))
    levels = s.shape[0]
    per_plane = 128 // GROUP
    plane_count = levels // per_plane
    shape = s.shape[1:]
    group = iota(shape, 1) // GROUP

    for a, name in enumerate(NAMES):
        copies[a].wait()

        def columns(p, carry, a=a, name=name):
            acc = jnp.zeros(shape, F32)
            for g in range(per_plane):
                x = level_of(refs[name], name, p * per_plane + g)
                acc = jnp.where(group == g, roll(x, GROUP * g + 4, 1), acc)
            planes[a * plane_count + p] = acc
            return carry

        lax.fori_loop(0, plane_count, columns, 0)
    total = len(NAMES) * plane_count
    copies[7].wait()
    count_plane = count[...].astype(F32)
    planes[total] = roll(count_plane, 4, 1)
    if (total + 1) % 2:
        planes[total + 1] = jnp.zeros(shape, F32)

    odd = odd_column()
    low = iota(shape, 1) % GROUP < 4
    for h in range(one.shape[0]):
        x, y = planes[2 * h], planes[2 * h + 1]
        to_east = jnp.where(low, x, roll(y, 4, 1))
        to_west = jnp.where(low, roll(x, -4, 1), y)
        one[h] = jnp.where(odd, to_west, to_east)
        two[h] = jnp.where(odd, to_east, to_west)

    small = (8, shape[1])
    small_group = iota(small, 1) // GROUP
    half = per_plane // 2

    def rims(p, carry):
        acc = jnp.zeros(small, F32)
        for m in range(half):
            level = p * half + m
            pair = pack_rows(lambda name: level_of(refs[name], name, level))
            for q in range(2):
                rows[2 * level + q] = pair[q]
                g = 2 * m + q
                acc = jnp.where(small_group == g, roll(pair[q], GROUP * g + 4, 1), acc)
        corners[p] = acc
        return carry

    lax.fori_loop(0, levels // half, rims, 0)
    count_rows = edge_rows(count_plane)
    rows[2 * levels] = count_rows
    corners[levels // half] = roll(count_rows, 4, 1)


def shift_up(x, axis):
    return roll(x, -1, axis)


def shift_down(x, axis):
    return roll(x, 1, axis)


def extend(main, side, rows=None, corners=None):
    top = jnp.concatenate([main, side], axis=1)
    if rows is None:
        return top
    return jnp.concatenate([top, jnp.concatenate([rows, corners], axis=1)], axis=0)


def solve_inward(levels, get, inv_q, carries):
    half = levels // 2
    inv, q = inv_q

    def step(t, carry):
        new = []
        for k, last in ((t, carry[0]), (levels - 1 - t, carry[1])):
            c = get(k) * inv(k) + q(k) * last
            carries[k] = c
            new.append(c)
        return tuple(new)

    zero = jnp.zeros(carries.shape[1:], F32)
    return lax.fori_loop(0, half, step, (zero, zero), unroll=UNROLL)


def solve_outward(levels, ends, ratio, join, carries, use):
    half = levels // 2
    high, low = ends
    upper = (high + ratio(half - 1) * low) * join
    lower = (low + ratio(half) * high) * join

    def step(t, carry):
        t = half - 1 - t
        new = []
        for k, last in ((t, carry[0]), (levels - 1 - t, carry[1])):
            x = carries[k] + ratio(k) * last
            use(k, x)
            new.append(x)
        return tuple(new)

    lax.fori_loop(0, half, step, (lower, upper), unroll=UNROLL)


def merge_halos(odd, from_one, from_two, planes):
    low = iota(from_one.shape[1:], 1) % GROUP < 4
    for h in range(from_one.shape[0]):
        a, b = from_one[h], from_two[h]
        west = jnp.where(odd, a, b)
        east = jnp.where(odd, b, a)
        planes[2 * h] = jnp.where(low, west, roll(east, 4, 1))
        planes[2 * h + 1] = jnp.where(low, roll(west, -4, 1), east)


def forward_kernel(
    s, es, ns, mix, relax, vm, obs, count, from_one, from_two, rows_n, rows_s, corner_one_n,
    corner_one_s, corner_two_n, corner_two_s,
    ep_out, em_out, np_out, nm_out, sink_out, inv_out, q_out, r_out, middle_out, solved_out,
    counts_out, join_out, start_out, send,
    planes, corners, rhs, links, carries,
):
    refs = dict(zip(NAMES, (s, es, ns, mix, relax, vm, obs)))
    levels = s.shape[0]
    half = levels // 2
    per_plane = 128 // GROUP
    plane_count = levels // per_plane
    odd = odd_column()
    merge_halos(odd, from_one, from_two, planes)
    small = (8, s.shape[2])
    low = iota(small, 1) % GROUP < 4
    north = iota(small, 0) < 4

    def rows_at(index):
        return rows_n[index], rows_s[index]

    def merge_first(n, s_):
        sub = iota(n.shape, 0)
        return jnp.where((sub < 2) | (sub == 4) | (sub == 5), n, s_)

    def merge_second(n, s_):
        sub = iota(n.shape, 0)
        return jnp.where((sub == 0) | (sub == 4) | (sub == 2), n, s_)

    def corner_plane(p):
        out = []
        for one_ref, two_ref in ((corner_one_n, corner_two_n), (corner_one_s, corner_two_s)):
            a, b = one_ref[p], two_ref[p]
            west = jnp.where(odd, a, b)
            east = jnp.where(odd, b, a)
            out.append(jnp.where(low, west, east))
        return out

    total = levels * 2 // per_plane
    first_group = (iota(small, 1) // GROUP) % 2 == 0
    for p in range(total):
        n, s_ = corner_plane(p)
        corners[p] = jnp.where(first_group, merge_first(n, s_), merge_second(n, s_))
    n, s_ = corner_plane(total)
    corners[total] = jnp.where(north, n, s_)

    last = len(NAMES) * plane_count
    count_ext = extend(
        count[...].astype(F32),
        roll(planes[last], 124, 1),
        jnp.where(north, rows_n[2 * levels], rows_s[2 * levels]),
        roll(corners[total], 124, 1),
    )
    east_count = jnp.minimum(count_ext, shift_up(count_ext, 1))
    north_count = jnp.minimum(count_ext, shift_up(count_ext, 0))
    counts_out[0] = count_ext
    counts_out[1] = east_count
    counts_out[2] = north_count

    def side_of(name, k):
        p = NAMES.index(name) * plane_count + k // per_plane
        return roll(planes[p], 124 - GROUP * (k % per_plane), 1)

    def load(k):
        pair = []
        for j, merge in enumerate((merge_first, merge_second)):
            index = 2 * k + j
            line = merge(rows_n[index], rows_s[index])
            corner = roll(corners[index // per_plane], 124 - GROUP * (index % per_plane), 1)
            pair.append(jnp.concatenate([line, corner], axis=1))
        rim = unpack_rows(*pair)
        return {
            name: jnp.concatenate(
                [extend(level_of(refs[name], name, k), side_of(name, k)), rim[name]], axis=0
            )
            for name in NAMES[:6]
        }

    def prepare(k, carry):
        x = load(k)
        level = k.astype(F32)
        state = x["s"]
        open_east = level < east_count
        open_north = level < north_count
        ep = jnp.where(open_east, 0.5 * x["es"] + x["mix"], 0.0)
        em = jnp.where(open_east, 0.5 * x["es"] - x["mix"], 0.0)
        np_ = jnp.where(open_north, 0.5 * x["ns"] + x["mix"], 0.0)
        nm = jnp.where(open_north, 0.5 * x["ns"] - x["mix"], 0.0)
        sink = jnp.where(level < count_ext, x["relax"], 0.0)
        link = jnp.where(level + 1.0 < count_ext, x["vm"], 0.0)
        ep_out[k] = ep
        em_out[k] = em
        np_out[k] = np_
        nm_out[k] = nm
        sink_out[k] = sink
        links[k] = link
        start_out[k] = state
        rhs[k] = advance(state, ep, em, np_, nm, sink)
        return carry

    def advance(state, ep, em, np_, nm, sink):
        fe = ep * state + em * shift_up(state, 1)
        fn = np_ * state + nm * shift_up(state, 0)
        spread = (fe - shift_down(fe, 1)) + (fn - shift_down(fn, 0))
        return state - spread - sink * jnp.tanh(state)

    lax.fori_loop(0, levels, prepare, 0, unroll=UNROLL)

    def factor(t, carry):
        (r_top, c_top), (r_low, c_low) = carry
        k = t
        above = jnp.where(k > 0, links[jnp.maximum(k - 1, 0)], 0.0)
        below = links[k]
        inv = 1.0 / (1.0 + above + below - above * r_top)
        q = above * inv
        r_top = below * inv
        c_top = rhs[k] * inv + q * c_top
        inv_out[k] = inv
        q_out[k] = q
        r_out[k] = r_top
        carries[k] = c_top
        k = levels - 1 - t
        above = links[k - 1]
        below = links[k]
        inv = 1.0 / (1.0 + above + below - below * r_low)
        q = below * inv
        r_low = above * inv
        c_low = rhs[k] * inv + q * c_low
        inv_out[k] = inv
        q_out[k] = q
        r_out[k] = r_low
        carries[k] = c_low
        return (r_top, c_top), (r_low, c_low)

    zero = jnp.zeros(rhs.shape[1:], F32)
    (r_top, c_top), (r_low, c_low) = lax.fori_loop(
        0, half, factor, ((zero, zero), (zero, zero)), unroll=UNROLL
    )
    join = 1.0 / (1.0 - r_top * r_low)
    join_out[...] = join

    def to_second(k, x):
        middle_out[k] = x
        value = advance(x, ep_out[k], em_out[k], np_out[k], nm_out[k], sink_out[k])
        rhs[k, :16] = value[:16]

    solve_outward(levels, (c_top, c_low), lambda k: r_out[k], join, carries, to_second)

    main = carries.at[:, :16]
    inv_q = (lambda k: inv_out[k, :16], lambda k: q_out[k, :16])
    ratio = lambda k: r_out[k, :16]
    ends = solve_inward(levels, lambda k: rhs[k, :16], inv_q, main)

    def to_adjoint(k, x):
        seen = extend(level_of(refs["obs"], "obs", k), side_of("obs", k))
        rhs[k, :16] = jnp.where(k.astype(F32) < count_ext[:16], x - seen, 0.0)

    solve_outward(levels, ends, ratio, join[:16], main, to_adjoint)
    ends = solve_inward(levels, lambda k: rhs[k, :16], inv_q, main)

    def to_solved(k, x):
        solved_out[k] = x

    solve_outward(levels, ends, ratio, join[:16], main, to_solved)

    group = iota(small, 1) // GROUP
    for p in range(send.shape[0] - half):
        acc = jnp.zeros(small, F32)
        for g in range(min(per_plane, half - p * per_plane)):
            t = p * per_plane + g
            x = edge_rows(solved_out[t])
            y = edge_rows(solved_out[levels - 1 - t])
            both = jnp.where(near(x.shape), x, roll(y, 4, 0))
            send[t] = both[:, :128]
            acc = jnp.where(
                group == g, roll(both[:, 128:], GROUP * g + 4, 1), acc
            )
        send[half + p] = acc


def backward_kernel(
    ep, em, np_, nm, sink, inv, q, r, middle, solved, counts, join, start, rows_n, rows_s,
    adjoint_out, gradient_out, carries,
):
    levels = solved.shape[0]
    half = levels // 2
    per_plane = 128 // GROUP
    small = (8, 128)
    sub = iota(small, 0)
    from_north = (sub < 2) | (sub == 4) | (sub == 5)

    def rims(t):
        line = jnp.where(from_north, rows_n[t], rows_s[t])
        p = half + t // per_plane
        corner = jnp.where(from_north, rows_n[p], rows_s[p])
        corner = roll(corner, 124 - GROUP * (t % per_plane), 1)
        both = jnp.concatenate([line, corner], axis=1)
        return both, roll(both, 4, 0)

    def pull(k, x, state):
        ge = shift_up(x, 1) - x
        gn = shift_up(x, 0) - x
        squeeze = jnp.tanh(state)
        result = x * (1.0 - sink[k] * (1.0 - squeeze * squeeze))
        result = result + ep[k] * ge + shift_down(em[k] * ge, 1)
        result = result + np_[k] * gn + shift_down(nm[k] * gn, 0)
        level = k.astype(F32)
        part = jnp.where(level < counts[1], ge * (shift_up(state, 1) - state), 0.0)
        part = part + jnp.where(level < counts[2], gn * (shift_up(state, 0) - state), 0.0)
        return result, part

    def late(t, carry):
        new = []
        for k, rim, last in zip((t, levels - 1 - t), rims(t), carry):
            x = jnp.concatenate([solved[k], rim], axis=0)
            result, part = pull(k, x, middle[k])
            gradient_out[k] = -part[:16, :128]
            c = result * inv[k] + q[k] * last
            carries[k] = c
            new.append(c)
        return tuple(new)

    zero = jnp.zeros(carries.shape[1:], F32)
    ends = lax.fori_loop(0, half, late, (zero, zero), unroll=UNROLL // 2)

    def early(k, x):
        result, part = pull(k, x, start[k])
        adjoint_out[k] = result[:16, :128]
        gradient_out[k] = gradient_out[k] - part[:16, :128]

    solve_outward(levels, ends, lambda k: r[k], join[...], carries, early)


def ring(axis, distance):
    count = lax.axis_size(axis)
    return [(i, (i + distance) % count) for i in range(count)]


def both_ways(x):
    from_north = lax.ppermute(x, "ty", ring("ty", -1))
    if lax.axis_size("ty") == 2:
        return from_north, from_north
    return from_north, lax.ppermute(x, "ty", ring("ty", 1))


def swap(x, phase, rise):
    ny, nx = lax.axis_size("ty"), lax.axis_size("tx")
    route = []
    for j in range(ny):
        for i in range(nx):
            partner = (i + 1) % nx if i % 2 == phase else (i - 1) % nx
            route.append((j * nx + i, ((j + rise) % ny) * nx + partner))
    return lax.ppermute(x, ("ty", "tx"), route)


def diagonal(x, phase):
    from_north = swap(x, phase, -1)
    if lax.axis_size("ty") == 2:
        return from_north, from_north
    return from_north, swap(x, phase, 1)


def per_device(
    tracer_start,
    observed,
    east_speed,
    north_speed,
    mixing,
    vertical_mixing,
    relax_rate,
    level_count,
    face_east,
    face_north,
):
    levels, ny, nx = tracer_start.shape
    per_plane = 128 // GROUP
    plane_count = levels // per_plane
    pairs = (len(NAMES) * plane_count + 2) // 2
    fields = (
        tracer_start, east_speed, north_speed, mixing, relax_rate, vertical_mixing, observed,
        level_count,
    )
    corner_planes = 2 * levels // per_plane + 1
    *fields, rows, corners, one, two = call(
        pack_kernel,
        [jax.ShapeDtypeStruct(x.shape, x.dtype) for x in fields]
        + [
            (2 * levels + 1, 8, nx),
            (corner_planes, 8, nx),
            (pairs, ny, nx),
            (pairs, ny, nx),
        ],
        [(2 * pairs, ny, nx), pltpu.SemaphoreType.DMA((8,))],
        *[pltpu.with_memory_space_constraint(x, pltpu.HBM) for x in fields],
        space=HBM,
    )
    rows_n, rows_s = both_ways(rows)
    from_two = swap(two, 1, 0)
    corner_two_n, corner_two_s = diagonal(corners, 1)
    from_one = swap(one, 0, 0)
    corner_one_n, corner_one_s = diagonal(corners, 0)
    ext = (levels, ny + 8, 2 * nx)
    half = levels // 2
    outs = call(
        forward_kernel,
        [ext] * 9 + [(levels, ny, 2 * nx), (3,) + ext[1:], ext[1:], ext]
        + [(half + -(-half // per_plane), 8, nx)],
        [(2 * pairs, ny, nx), (corner_planes, 8, nx), ext, ext, ext],
        *fields, from_one, from_two, rows_n, rows_s,
        corner_one_n, corner_one_s, corner_two_n, corner_two_s,
    )
    ep, em, np_, nm, sink, inv, q, r, middle, solved, counts, join, start, send = outs
    sent_n, sent_s = both_ways(send)
    adjoint, gradient = call(
        backward_kernel,
        [(levels, ny, nx)] * 2,
        [ext],
        ep, em, np_, nm, sink, inv, q, r, middle, solved, counts, join, start, sent_n, sent_s,
    )
    return adjoint, gradient


def solution(mesh):
    block = P(None, "ty", "tx")
    plane = P("ty", "tx")
    return jax.shard_map(
        per_device,
        mesh=mesh,
        in_specs=(block,) * 7 + (plane,) * 3,
        out_specs=(block, block),
        check_vma=False,
    )
```

```python
import functools

import jax
import jax.numpy as jnp
from jax import lax
from jax.experimental import pallas as pl
from jax.experimental.pallas import tpu as pltpu
from jax.sharding import PartitionSpec as P

F32 = jnp.float32
VMEM = pl.BlockSpec(memory_space=pltpu.VMEM)
HBM = pl.BlockSpec(memory_space=pltpu.HBM)
UNROLL = 8
GROUP = 8
NAMES = ("s", "es", "ns", "mix", "relax", "vm", "obs")


def call(kernel, outs, scratch, *args, space=VMEM, cost=None):
    def typed(x):
        return x if isinstance(x, jax.ShapeDtypeStruct) else jax.ShapeDtypeStruct(x, F32)

    return pl.pallas_call(
        kernel,
        out_shape=[typed(x) for x in outs],
        in_specs=[space] * len(args),
        out_specs=[VMEM] * len(outs),
        scratch_shapes=[pltpu.VMEM(x, F32) if isinstance(x, tuple) else x for x in scratch],
        compiler_params=pltpu.CompilerParams(vmem_limit_bytes=16 << 20),
        cost_estimate=cost,
    )(*args)


def iota(shape, dim):
    return lax.broadcasted_iota(jnp.int32, shape, dim)


def roll(x, shift, axis):
    if isinstance(shift, int):
        shift = shift % x.shape[axis]
        if shift == 0:
            return x
    return pltpu.roll(x, shift, axis)


def odd_column():
    return lax.rem(lax.axis_index("tx"), 2) == 1


def level_of(ref, name, level):
    if name == "vm":
        level = jnp.minimum(level, ref.shape[0] - 1)
    return ref[level].astype(F32)


def edge_rows(block):
    return jnp.where(iota((8, block.shape[1]), 0) < 4, block[:8], block[-8:])


def sublane(shape):
    return iota(shape, 0)


def step_count(counts, axis):
    return jnp.minimum(counts, shift_up(counts, axis))


def pair_rows(first, second):
    sub = sublane(first.shape)
    return jnp.where((sub == 1) | (sub == 2), roll(second, 2, 0), first)


def pack_rows(get, counts, level):
    tile = {name: edge_rows(get(name)) for name in NAMES[:6]}
    s = tile["s"]
    sub = sublane(s.shape)
    open_north = level < step_count(counts, 0)
    fn = jnp.where(
        open_north,
        (0.5 * tile["ns"] + tile["mix"]) * s + (0.5 * tile["ns"] - tile["mix"]) * shift_up(s, 0),
        0.0,
    )
    sink = jnp.where(level < counts, tile["relax"], 0.0)
    inner = jnp.where(sub == 0, -fn, jnp.where(sub == 7, shift_down(fn, 0), 0.0))
    base = s - sink * jnp.tanh(s) + inner
    first = pair_rows(s, base)
    first = jnp.where((sub == 3) | (sub == 4), roll(tile["es"], 4, 0), first)
    first = jnp.where((sub == 5) | (sub == 6), roll(tile["mix"], 6, 0), first)
    return first, pair_rows(tile["vm"], tile["ns"])


def unpack_rows(first, second):
    return {
        "s": first,
        "base": roll(first, 6, 0),
        "es": roll(first, 4, 0),
        "mix": roll(first, 2, 0),
        "vm": second,
        "ns": roll(second, 6, 0),
    }


def two_levels(x, y):
    sub = sublane(x.shape)
    return jnp.where((sub >= 3) & (sub <= 6), roll(y, 4, 0), x)


def shift_up(x, axis):
    return roll(x, -1, axis)


def shift_down(x, axis):
    return roll(x, 1, axis)


def rim_kernel(*args):
    fields = args[:8]
    s, es, ns, mix, relax, vm, obs, count = kept = args[8:16]
    rows, corners, arrived = args[16:]
    copies = [pltpu.make_async_copy(fields[i], kept[i], arrived.at[i]) for i in range(8)]
    for copy in copies:
        copy.start()
    for copy in copies:
        copy.wait()
    refs = dict(zip(NAMES, (s, es, ns, mix, relax, vm, obs)))
    levels = s.shape[0]
    per_plane = 128 // GROUP
    small = (8, s.shape[2])
    group = iota(small, 1) // GROUP
    half = per_plane // 2
    count_planes = levels // per_plane
    counts = edge_rows(count[...].astype(F32))

    def rims(p, carry):
        acc = jnp.zeros(small, F32)
        late = jnp.zeros(small, F32)
        for g in range(0, per_plane, 2):
            tiles = []
            for level in (p * per_plane + g, p * per_plane + g + 1):
                tiles.append(
                    pack_rows(
                        lambda name: level_of(refs[name], name, level), counts, level.astype(F32)
                    )
                )
            half_tile = two_levels(tiles[0][1], tiles[1][1])
            h = g // 2
            rows[levels + p * half + h] = half_tile
            late = jnp.where(group == h, roll(half_tile, GROUP * h + 4, 1), late)
            for q in range(2):
                rows[p * per_plane + g + q] = tiles[q][0]
                acc = jnp.where(
                    group == g + q, roll(tiles[q][0], GROUP * (g + q) + 4, 1), acc
                )
        corners[p] = acc
        corners[count_planes + p] = late
        return carry

    lax.fori_loop(0, count_planes, rims, 0)
    rows[levels + levels // 2] = counts
    corners[2 * count_planes] = roll(counts, 4, 1)
    for p in range(2 * count_planes + 1, corners.shape[0]):
        corners[p] = jnp.zeros(small, F32)


def column_kernel(s, es, ns, mix, relax, vm, obs, count, planes):
    refs = dict(zip(NAMES, (s, es, ns, mix, relax, vm, obs)))
    levels = s.shape[0]
    per_plane = 128 // GROUP
    plane_count = levels // per_plane
    shape = s.shape[1:]
    group = iota(shape, 1) // GROUP

    def columns(p, carry):
        for a, name in enumerate(NAMES):
            acc = jnp.zeros(shape, F32)
            for g in range(per_plane):
                x = level_of(refs[name], name, p * per_plane + g)
                acc = jnp.where(group == g, roll(x, GROUP * g + 4, 1), acc)
            planes[a * plane_count + p] = acc
        return carry

    lax.fori_loop(0, plane_count, columns, 0)
    total = len(NAMES) * plane_count
    planes[total] = roll(count[...].astype(F32), 4, 1)
    for p in range(total + 1, planes.shape[0]):
        planes[p] = jnp.zeros(shape, F32)


def merge_rows(north, south):
    return jnp.where(sublane(north.shape) % 2 == 0, north, south)


def halves_kernel(planes, corners_n, corners_s, rows, one, two, rows_out):
    odd = odd_column()
    pairs = planes.shape[0] // 2
    ny = planes.shape[1]

    def put(place, x, y):
        low = iota(x.shape, 1) % GROUP < 4
        to_east = jnp.where(low, x, roll(y, 4, 1))
        to_west = jnp.where(low, roll(x, -4, 1), y)
        one[place] = jnp.where(odd, to_west, to_east)
        two[place] = jnp.where(odd, to_east, to_west)

    for h in range(pairs):
        put(pl.ds(h * ny, ny), planes[2 * h], planes[2 * h + 1])

    count = corners_n.shape[0]
    rows_out[...] = rows[...]
    two[pl.ds(one.shape[0], 8)] = jnp.zeros((8, one.shape[1]), F32)

    def corner(p):
        return merge_rows(corners_n[p], corners_s[p])

    for h in range(count // 2):
        put(pl.ds(pairs * ny + h * 8, 8), corner(2 * h), corner(2 * h + 1))


def extend(main, side, rows=None, corners=None):
    top = jnp.concatenate([main, side], axis=1)
    if rows is None:
        return top
    return jnp.concatenate([top, jnp.concatenate([rows, corners], axis=1)], axis=0)


def solve_inward(levels, get, inv_q, carries):
    half = levels // 2
    inv, q = inv_q

    def step(t, carry):
        new = []
        for k, last in ((t, carry[0]), (levels - 1 - t, carry[1])):
            c = get(k) * inv(k) + q(k) * last
            carries[k] = c
            new.append(c)
        return tuple(new)

    zero = jnp.zeros(carries.shape[1:], F32)
    return lax.fori_loop(0, half, step, (zero, zero), unroll=UNROLL)


def solve_outward(levels, ends, ratio, join, carries, use):
    half = levels // 2
    high, low = ends
    upper = (high + ratio(half - 1) * low) * join
    lower = (low + ratio(half) * high) * join

    def step(t, carry):
        t = half - 1 - t
        new = []
        for k, last in ((t, carry[0]), (levels - 1 - t, carry[1])):
            x = carries[k] + ratio(k) * last
            use(k, x)
            new.append(x)
        return tuple(new)

    lax.fori_loop(0, half, step, (lower, upper), unroll=UNROLL)


def merge_halos(odd, from_one, from_two, planes, start):
    size = planes.shape[1]
    low = iota(planes.shape[1:], 1) % GROUP < 4
    for h in range(planes.shape[0] // 2):
        place = pl.ds(start + h * size, size)
        a, b = from_one[place], from_two[place]
        west = jnp.where(odd, a, b)
        east = jnp.where(odd, b, a)
        planes[2 * h] = jnp.where(low, west, roll(east, 4, 1))
        planes[2 * h + 1] = jnp.where(low, roll(west, -4, 1), east)


def part_of_pull(x, ep, em, damp):
    ge = shift_up(x, 1) - x
    return x * damp + ep * ge + shift_down(em * ge, 1), ge


def forward_kernel(
    s, es, ns, mix, relax, vm, obs, count, from_one, from_two, rows_n, rows_s,
    ep_out, em_out, np_out, nm_out, sink_out, inv_out, q_out, r_out, middle_out, damp_out,
    solved_out, counts_out, join_out, start_out, send,
    planes, corners, rhs, links, carries,
):
    refs = dict(zip(NAMES, (s, es, ns, mix, relax, vm, obs)))
    levels, ny, nx = s.shape
    half = levels // 2
    per_plane = 128 // GROUP
    plane_count = levels // per_plane
    odd = odd_column()
    merge_halos(odd, from_one, from_two, planes, 0)
    merge_halos(odd, from_one, from_two, corners, planes.shape[0] // 2 * planes.shape[1])

    def rim(index):
        return merge_rows(rows_n[index], rows_s[index])

    count_ext = extend(
        count[...].astype(F32),
        roll(planes[len(NAMES) * plane_count], 124, 1),
        rim(levels + half),
        roll(corners[2 * plane_count], 124, 1),
    )
    east_count = step_count(count_ext, 1)
    sub = sublane(count_ext.shape)
    north_count = jnp.where(
        (sub < ny) | (sub == ny + 7), step_count(count_ext, 0), 0.0
    )
    counts_out[0] = count_ext
    counts_out[1] = east_count
    counts_out[2] = north_count

    def side_of(name, k):
        p = NAMES.index(name) * plane_count + k // per_plane
        return roll(planes[p], 124 - GROUP * (k % per_plane), 1)

    def rim_ext(index, plane, group):
        corner = roll(corners[plane], 124 - GROUP * group, 1)
        return jnp.concatenate([rim(index), corner], axis=1)

    def prepare(m, carry):
        later = rim_ext(
            levels + m,
            plane_count + m // (per_plane // 2),
            m % (per_plane // 2),
        )
        for q in range(2):
            k = 2 * m + q
            first = rim_ext(k, k // per_plane, k % per_plane)
            x = unpack_rows(first, roll(later, 4, 0) if q else later)
            for name in NAMES[:4] + NAMES[5:6]:
                x[name] = jnp.concatenate(
                    [extend(level_of(refs[name], name, k), side_of(name, k)), x[name]], axis=0
                )
            level = k.astype(F32)
            state = x["s"]
            open_east = level < east_count
            open_north = level < north_count
            ep = jnp.where(open_east, 0.5 * x["es"] + x["mix"], 0.0)
            em = jnp.where(open_east, 0.5 * x["es"] - x["mix"], 0.0)
            np_ = jnp.where(open_north, 0.5 * x["ns"] + x["mix"], 0.0)
            nm = jnp.where(open_north, 0.5 * x["ns"] - x["mix"], 0.0)
            inner = state[:ny]
            sink = extend(level_of(refs["relax"], "relax", k), side_of("relax", k))
            sink = jnp.where(level < count_ext[:ny], sink, 0.0)
            link = jnp.where(level + 1.0 < count_ext, x["vm"], 0.0)
            squeeze = jnp.tanh(inner)
            base = jnp.concatenate([inner - sink * squeeze, x["base"]], axis=0)
            ep_out[k] = ep
            em_out[k] = em
            np_out[k] = np_
            nm_out[k] = nm
            sink_out[k] = sink
            links[k] = link
            start_out[k] = state
            damp_out[k] = 1.0 - sink * (1.0 - squeeze * squeeze)
            rhs[k] = base - spread(state, ep, em, np_, nm)
        return carry

    def spread(state, ep, em, np_, nm):
        fe = ep * state + em * shift_up(state, 1)
        fn = np_ * state + nm * shift_up(state, 0)
        return (fe - shift_down(fe, 1)) + (fn - shift_down(fn, 0))

    lax.fori_loop(0, half, prepare, 0, unroll=UNROLL // 2)

    def factor(t, carry):
        (r_top, c_top), (r_low, c_low) = carry
        k = t
        above = jnp.where(k > 0, links[jnp.maximum(k - 1, 0)], 0.0)
        below = links[k]
        inv = 1.0 / (1.0 + above + below - above * r_top)
        q = above * inv
        r_top = below * inv
        c_top = rhs[k] * inv + q * c_top
        inv_out[k] = inv
        q_out[k] = q
        r_out[k] = r_top
        carries[k] = c_top
        k = levels - 1 - t
        above = links[k - 1]
        below = links[k]
        inv = 1.0 / (1.0 + above + below - below * r_low)
        q = below * inv
        r_low = above * inv
        c_low = rhs[k] * inv + q * c_low
        inv_out[k] = inv
        q_out[k] = q
        r_out[k] = r_low
        carries[k] = c_low
        return (r_top, c_top), (r_low, c_low)

    zero = jnp.zeros(rhs.shape[1:], F32)
    (r_top, c_top), (r_low, c_low) = lax.fori_loop(
        0, half, factor, ((zero, zero), (zero, zero)), unroll=UNROLL
    )
    join = 1.0 / (1.0 - r_top * r_low)
    join_out[...] = join

    def to_second(k, x):
        middle_out[k] = x
        inner = x[:ny]
        squeeze = jnp.tanh(inner)
        sink = sink_out[k]
        damp_out[levels + k] = 1.0 - sink * (1.0 - squeeze * squeeze)
        flow = spread(x, ep_out[k], em_out[k], np_out[k], nm_out[k])
        rhs[k, :ny] = inner - flow[:ny] - sink * squeeze

    solve_outward(levels, (c_top, c_low), lambda k: r_out[k], join, carries, to_second)

    main = carries.at[:, :ny]
    inv_q = (lambda k: inv_out[k, :ny], lambda k: q_out[k, :ny])
    ratio = lambda k: r_out[k, :ny]
    ends = solve_inward(levels, lambda k: rhs[k, :ny], inv_q, main)

    def to_adjoint(k, x):
        seen = extend(level_of(refs["obs"], "obs", k), side_of("obs", k))
        rhs[k, :ny] = jnp.where(k.astype(F32) < count_ext[:ny], x - seen, 0.0)

    solve_outward(levels, ends, ratio, join[:ny], main, to_adjoint)
    ends = solve_inward(levels, lambda k: rhs[k, :ny], inv_q, main)

    def to_solved(k, x):
        solved_out[k] = x

    solve_outward(levels, ends, ratio, join[:ny], main, to_solved)

    def rim_part(k):
        x = edge_rows(solved_out[k])
        edge = lambda ref: edge_rows(ref[k, :ny])
        part, _ = part_of_pull(x, edge(ep_out), edge(em_out), edge_rows(damp_out[levels + k]))
        gn = shift_up(x, 0) - x
        sub = sublane(x.shape)
        part = part + jnp.where(
            sub == 0,
            edge(np_out) * gn,
            jnp.where(sub == 7, shift_down(edge(nm_out) * gn, 0), 0.0),
        )
        return pair_rows(x, part)

    group = iota((8, nx), 1) // GROUP

    def rims(p, carry):
        acc = jnp.zeros((8, nx), F32)
        for g in range(8):
            t = p * 8 + g
            both = two_levels(rim_part(t), rim_part(levels - 1 - t))
            send[t] = both[:, :nx]
            acc = jnp.where(group == g, roll(both[:, nx:], GROUP * g + 4, 1), acc)
        send[half + p] = acc
        return carry

    lax.fori_loop(0, half // 8, rims, 0)


def inner_kernel(
    ep, em, np_, nm, damp, middle, solved, counts, part_out, late_out,
):
    levels, ny, width = solved.shape
    nx = width // 2
    sub = sublane((ny, width))
    inside = sub < ny - 1

    def inner(k, carry):
        x = solved[k]
        state = middle[k]
        part, ge = part_of_pull(x, ep[k, :ny], em[k, :ny], damp[levels + k])
        gn = jnp.where(inside, shift_up(x, 0) - x, 0.0)
        part_out[k] = part + np_[k, :ny] * gn + shift_down(nm[k, :ny] * gn, 0)
        level = k.astype(F32)
        rise = shift_up(state, 0)[:ny, :nx] - state[:ny, :nx]
        run = (shift_up(state[:ny], 1) - state[:ny])[:, :nx]
        late_out[k] = jnp.where(level < counts[1, :ny, :nx], ge[:, :nx] * run, 0.0) + jnp.where(
            level < counts[2, :ny, :nx], gn[:, :nx] * rise, 0.0
        )
        return carry

    lax.fori_loop(0, levels, inner, 0, unroll=UNROLL)


def backward_kernel(
    ep, em, np_, nm, inv, q, r, middle, damp, solved, counts, join, start, part, late,
    rows_n, rows_s,
    adjoint_out, gradient_out, carries,
):
    levels, ny, width = solved.shape
    nx = width // 2
    half = levels // 2
    sub = sublane((8, width))

    def rims(t):
        line = merge_rows(rows_n[t], rows_s[t])
        p = half + t // 8
        corner = roll(merge_rows(rows_n[p], rows_s[p]), 124 - GROUP * (t % 8), 1)
        both = jnp.concatenate([line, corner], axis=1)
        return both, roll(both, 4, 0)

    def across(k, rim):
        inner = part[k]
        near_part = roll(rim, 6, 0)
        south = solved[k, :8] - shift_down(rim, 0)
        north = shift_up(rim, 0) - solved[k, ny - 8 :]
        np_rim, nm_rim = np_[k, ny:], nm[k, ny:]
        np_top, nm_top = np_[k, ny - 8 : ny], nm[k, ny - 8 : ny]
        low = inner[:8] + jnp.where(sub == 0, shift_down(nm_rim, 0) * south, 0.0)
        high = inner[ny - 8 :] + jnp.where(sub == 7, np_top * north, 0.0)
        outer = near_part + jnp.where(
            sub == 0, shift_down(nm_top * north, 0), np_rim * shift_up(south, 0)
        )
        rise = (shift_up(middle[k, ny:], 0) - middle[k, ny - 8 : ny])[:, :nx]
        open_north = (sub[:, :nx] == 7) & (k.astype(F32) < counts[2, ny - 8 : ny, :nx])
        extra = jnp.where(open_north, north[:, :nx] * rise, 0.0)
        gradient_out[k, : ny - 8] = late[k, : ny - 8]
        gradient_out[k, ny - 8 :] = late[k, ny - 8 :] + extra
        middle_rows = [inner[8 : ny - 8]] if ny > 16 else []
        return jnp.concatenate([low, *middle_rows, high, outer], axis=0)

    def late_step(t, carry):
        new = []
        for k, rim, last in zip((t, levels - 1 - t), rims(t), carry):
            c = across(k, rim) * inv[k] + q[k] * last
            carries[k] = c
            new.append(c)
        return tuple(new)

    zero = jnp.zeros(carries.shape[1:], F32)
    ends = lax.fori_loop(0, half, late_step, (zero, zero), unroll=UNROLL // 2)

    def early(k, x):
        state = start[k]
        inner = x[:ny]
        east = shift_up(inner, 1)
        ge = east - inner
        result = inner[:, :nx] * damp[k, :, :nx] + (ep[k, :ny] * ge)[:, :nx]
        result = result + shift_down(em[k, :ny] * ge, 1)[:, :nx]
        column = x[:, :nx]
        gn = shift_up(column, 0) - column
        result = result + (np_[k, :, :nx] * gn + shift_down(nm[k, :, :nx] * gn, 0))[:ny]
        adjoint_out[k] = result
        level = k.astype(F32)
        run = (shift_up(state[:ny], 1) - state[:ny])[:, :nx]
        rise = (shift_up(state[:, :nx], 0) - state[:, :nx])[:ny]
        gradient_out[k] = -(
            gradient_out[k]
            + jnp.where(level < counts[1, :ny, :nx], ge[:, :nx] * run, 0.0)
            + jnp.where(level < counts[2, :ny, :nx], gn[:ny] * rise, 0.0)
        )

    solve_outward(levels, ends, lambda k: r[k], join[...], carries, early)


def ring(axis, distance):
    count = lax.axis_size(axis)
    return [(i, (i + distance) % count) for i in range(count)]


def both_ways(x):
    from_north = lax.ppermute(x, "ty", ring("ty", -1))
    if lax.axis_size("ty") == 2:
        return from_north, from_north
    return from_north, lax.ppermute(x, "ty", ring("ty", 1))


def swap(x, phase):
    nx = lax.axis_size("tx")
    return lax.ppermute(
        x, "tx", [(i, (i + 1) % nx if i % 2 == phase else (i - 1) % nx) for i in range(nx)]
    )


def per_device(
    tracer_start,
    observed,
    east_speed,
    north_speed,
    mixing,
    vertical_mixing,
    relax_rate,
    level_count,
    face_east,
    face_north,
):
    levels, ny, nx = tracer_start.shape
    per_plane = 128 // GROUP
    plane_count = levels // per_plane
    pairs = (len(NAMES) * plane_count + 2) // 2
    fields = (
        tracer_start, east_speed, north_speed, mixing, relax_rate, vertical_mixing, observed,
        level_count,
    )
    half = levels // 2
    corner_planes = 2 * plane_count + 2
    *fields, rows, corners = call(
        rim_kernel,
        [jax.ShapeDtypeStruct(x.shape, x.dtype) for x in fields]
        + [(levels + half + 1, 8, nx), (corner_planes, 8, nx)],
        [pltpu.SemaphoreType.DMA((8,))],
        *[pltpu.with_memory_space_constraint(x, pltpu.HBM) for x in fields],
        space=HBM,
    )
    corners_n, corners_s = both_ways(corners)
    (planes,) = call(column_kernel, [(2 * pairs, ny, nx)], [], *fields)
    packed = (pairs * ny + corner_planes // 2 * 8, nx)
    one, two, rows = call(
        halves_kernel,
        [packed, (packed[0] + 8, nx), rows.shape],
        [],
        planes,
        corners_n,
        corners_s,
        rows,
    )
    from_two = swap(two, 1)
    rows_n, rows_s = both_ways(rows)
    from_one = swap(one, 0)
    ext = (levels, ny + 8, 2 * nx)
    block = (levels, ny, 2 * nx)
    outs = call(
        forward_kernel,
        [ext] * 4 + [block] + [ext] * 4
        + [(2 * levels, ny, 2 * nx), block, (3,) + ext[1:], ext[1:], ext]
        + [(half + half // 8, 8, nx)],
        [(2 * pairs, ny, nx), (corner_planes, 8, nx), ext, ext, ext],
        *fields, from_one, from_two, rows_n, rows_s,
    )
    ep, em, np_, nm, _, inv, q, r, middle, damp, solved, counts, join, start, send = outs
    sent_n, sent_s = both_ways(send)
    part, late = call(
        inner_kernel,
        [block, (levels, ny, nx)],
        [],
        ep, em, np_, nm, damp, middle, solved, counts,
        cost=pl.CostEstimate(flops=0, bytes_accessed=8 << 20, transcendentals=0),
    )
    adjoint, gradient = call(
        backward_kernel,
        [(levels, ny, nx)] * 2,
        [ext],
        ep, em, np_, nm, inv, q, r, middle, damp, solved, counts, join, start, part, late,
        sent_n, sent_s,
    )
    return adjoint, gradient


def solution(mesh):
    block = P(None, "ty", "tx")
    plane = P("ty", "tx")
    return jax.shard_map(
        per_device,
        mesh=mesh,
        in_specs=(block,) * 7 + (plane,) * 3,
        out_specs=(block, block),
        check_vma=False,
    )
```

```python
import functools

import jax
import jax.numpy as jnp
from jax import lax
from jax.experimental import pallas as pl
from jax.experimental.pallas import tpu as pltpu
from jax.sharding import PartitionSpec as P

F32 = jnp.float32
VMEM = pl.BlockSpec(memory_space=pltpu.VMEM)
HBM = pl.BlockSpec(memory_space=pltpu.HBM)
UNROLL = 8
GROUP = 8
NAMES = ("s", "es", "ns", "mix", "relax", "vm", "obs")


def call(kernel, outs, scratch, *args, space=VMEM, out_space=VMEM, cost=None):
    def typed(x):
        return x if isinstance(x, jax.ShapeDtypeStruct) else jax.ShapeDtypeStruct(x, F32)

    return pl.pallas_call(
        kernel,
        out_shape=[typed(x) for x in outs],
        in_specs=[space] * len(args),
        out_specs=[out_space] * len(outs),
        scratch_shapes=[pltpu.VMEM(x, F32) if isinstance(x, tuple) else x for x in scratch],
        compiler_params=pltpu.CompilerParams(vmem_limit_bytes=16 << 20),
        cost_estimate=cost,
    )(*args)


def iota(shape, dim):
    return lax.broadcasted_iota(jnp.int32, shape, dim)


def roll(x, shift, axis):
    if isinstance(shift, int):
        shift = shift % x.shape[axis]
        if shift == 0:
            return x
    return pltpu.roll(x, shift, axis)


def odd_column():
    return lax.rem(lax.axis_index("tx"), 2) == 1


def level_of(ref, name, level):
    if name == "vm":
        level = jnp.minimum(level, ref.shape[0] - 1)
    return ref[level].astype(F32)


def edge_rows(block):
    return jnp.where(iota((8, block.shape[1]), 0) < 4, block[:8], block[-8:])


def sublane(shape):
    return iota(shape, 0)


def step_count(counts, axis):
    return jnp.minimum(counts, shift_up(counts, axis))


def pair_rows(first, second):
    sub = sublane(first.shape)
    return jnp.where((sub == 1) | (sub == 2), roll(second, 2, 0), first)


def level_pair(levels, t):
    return (t, t), (levels - 1 - t, levels - 2 - t)


def pack_rows(get, counts, level):
    tile = {name: edge_rows(get(name)) for name in NAMES[:6]}
    s = tile["s"]
    sub = sublane(s.shape)
    open_north = level < step_count(counts, 0)
    fn = jnp.where(
        open_north,
        (0.5 * tile["ns"] + tile["mix"]) * s + (0.5 * tile["ns"] - tile["mix"]) * shift_up(s, 0),
        0.0,
    )
    sink = jnp.where(level < counts, tile["relax"], 0.0)
    inner = jnp.where(sub == 0, -fn, jnp.where(sub == 7, shift_down(fn, 0), 0.0))
    base = s - sink * jnp.tanh(s) + inner
    first = pair_rows(s, base)
    first = jnp.where((sub == 3) | (sub == 4), roll(tile["es"], 4, 0), first)
    first = jnp.where((sub == 5) | (sub == 6), roll(tile["mix"], 6, 0), first)
    return first, pair_rows(tile["vm"], tile["ns"])


def unpack_rows(first, second):
    return {
        "s": first,
        "base": roll(first, 6, 0),
        "es": roll(first, 4, 0),
        "mix": roll(first, 2, 0),
        "vm": second,
        "ns": roll(second, 6, 0),
    }


def two_levels(x, y):
    sub = sublane(x.shape)
    return jnp.where((sub >= 3) & (sub <= 6), roll(y, 4, 0), x)


def shift_up(x, axis):
    return roll(x, -1, axis)


def shift_down(x, axis):
    return roll(x, 1, axis)


def rim_kernel(*args):
    fields = args[:8]
    s, es, ns, mix, relax, vm, obs, count = kept = args[8:16]
    rows, corners, arrived = args[16:]
    copies = [pltpu.make_async_copy(fields[i], kept[i], arrived.at[i]) for i in range(8)]
    for copy in copies:
        copy.start()
    for copy in copies:
        copy.wait()
    refs = dict(zip(NAMES, (s, es, ns, mix, relax, vm, obs)))
    levels = s.shape[0]
    per_plane = 128 // GROUP
    small = (8, s.shape[2])
    group = iota(small, 1) // GROUP
    half = per_plane // 2
    plane_count = levels // per_plane
    counts = edge_rows(count[...].astype(F32))

    def rims(p, carry):
        acc = jnp.zeros(small, F32)
        late = jnp.zeros(small, F32)
        for g in range(half):
            t = p * half + g
            seconds = []
            for j, (k, link) in enumerate(level_pair(levels, t)):
                first, second = pack_rows(
                    lambda name: level_of(refs[name], name, link if name == "vm" else k),
                    counts,
                    k.astype(F32),
                )
                seconds.append(second)
                rows[2 * t + j] = first
                place = 2 * g + j
                acc = jnp.where(group == place, roll(first, GROUP * place + 4, 1), acc)
            second = two_levels(*seconds)
            rows[levels + t] = second
            late = jnp.where(group == g, roll(second, GROUP * g + 4, 1), late)
        corners[p] = acc
        corners[plane_count + p] = late
        return carry

    lax.fori_loop(0, plane_count, rims, 0)
    rows[levels + levels // 2] = counts
    corners[2 * plane_count] = roll(counts, 4, 1)
    for p in range(2 * plane_count + 1, corners.shape[0]):
        corners[p] = jnp.zeros(small, F32)


def column_kernel(s, es, ns, mix, relax, vm, obs, count, planes):
    refs = dict(zip(NAMES, (s, es, ns, mix, relax, vm, obs)))
    levels = s.shape[0]
    per_plane = 128 // GROUP
    plane_count = levels // per_plane
    shape = s.shape[1:]
    group = iota(shape, 1) // GROUP

    def columns(p, carry):
        for a, name in enumerate(NAMES):
            acc = jnp.zeros(shape, F32)
            for g in range(per_plane):
                x = level_of(refs[name], name, p * per_plane + g)
                acc = jnp.where(group == g, roll(x, GROUP * g + 4, 1), acc)
            planes[a * plane_count + p] = acc
        return carry

    lax.fori_loop(0, plane_count, columns, 0)
    total = len(NAMES) * plane_count
    planes[total] = roll(count[...].astype(F32), 4, 1)
    for p in range(total + 1, planes.shape[0]):
        planes[p] = jnp.zeros(shape, F32)


def merge_rows(north, south):
    return jnp.where(sublane(north.shape) % 2 == 0, north, south)


def halves_kernel(planes, corners_n, corners_s, one, two):
    odd = odd_column()
    pairs = planes.shape[0] // 2
    ny = planes.shape[1]

    def put(place, x, y):
        low = iota(x.shape, 1) % GROUP < 4
        to_east = jnp.where(low, x, roll(y, 4, 1))
        to_west = jnp.where(low, roll(x, -4, 1), y)
        one[place] = jnp.where(odd, to_west, to_east)
        two[place] = jnp.where(odd, to_east, to_west)

    for h in range(pairs):
        put(pl.ds(h * ny, ny), planes[2 * h], planes[2 * h + 1])

    count = corners_n.shape[0]
    two[pl.ds(one.shape[0], 8)] = jnp.zeros((8, one.shape[1]), F32)

    def corner(p):
        return merge_rows(corners_n[p], corners_s[p])

    for h in range(count // 2):
        put(pl.ds(pairs * ny + h * 8, 8), corner(2 * h), corner(2 * h + 1))


def extend(main, side, rows=None, corners=None):
    top = jnp.concatenate([main, side], axis=1)
    if rows is None:
        return top
    return jnp.concatenate([top, jnp.concatenate([rows, corners], axis=1)], axis=0)


def solve_inward(levels, get, inv_q, carries):
    half = levels // 2
    inv, q = inv_q

    def step(t, carry):
        new = []
        for k, last in ((t, carry[0]), (levels - 1 - t, carry[1])):
            c = get(k) * inv(k) + q(k) * last
            carries[k] = c
            new.append(c)
        return tuple(new)

    zero = jnp.zeros(carries.shape[1:], F32)
    return lax.fori_loop(0, half, step, (zero, zero), unroll=UNROLL)


def solve_outward(levels, ends, ratio, join, carries, use):
    half = levels // 2
    high, low = ends
    upper = (high + ratio(half - 1) * low) * join
    lower = (low + ratio(half) * high) * join

    def step(t, carry):
        t = half - 1 - t
        new = []
        for k, last in ((t, carry[0]), (levels - 1 - t, carry[1])):
            new.append(carries[k] + ratio(k) * last)
        use(t, *new)
        return tuple(new)

    lax.fori_loop(0, half, step, (lower, upper), unroll=UNROLL)


def merge_halos(odd, from_one, from_two, planes, start):
    size = planes.shape[1]
    low = iota(planes.shape[1:], 1) % GROUP < 4
    for h in range(planes.shape[0] // 2):
        place = pl.ds(start + h * size, size)
        a, b = from_one[place], from_two[place]
        west = jnp.where(odd, a, b)
        east = jnp.where(odd, b, a)
        planes[2 * h] = jnp.where(low, west, roll(east, 4, 1))
        planes[2 * h + 1] = jnp.where(low, roll(west, -4, 1), east)


def part_of_pull(x, ep, em, damp):
    ge = shift_up(x, 1) - x
    return x * damp + ep * ge + shift_down(em * ge, 1), ge


def forward_kernel(
    s, es, ns, mix, relax, vm, obs, count, from_one, from_two, rows_n, rows_s,
    ep_out, em_out, np_out, nm_out, sink_out, inv_out, q_out, r_out, middle_out, damp_out,
    solved_out, counts_out, join_out, start_out, send,
    planes, corners, rhs, carries,
):
    refs = dict(zip(NAMES, (s, es, ns, mix, relax, vm, obs)))
    levels, ny, nx = s.shape
    half = levels // 2
    per_plane = 128 // GROUP
    plane_count = levels // per_plane
    odd = odd_column()
    merge_halos(odd, from_one, from_two, planes, 0)
    merge_halos(odd, from_one, from_two, corners, planes.shape[0] // 2 * planes.shape[1])

    def rim(index):
        return merge_rows(rows_n[index], rows_s[index])

    count_ext = extend(
        count[...].astype(F32),
        roll(planes[len(NAMES) * plane_count], 124, 1),
        rim(levels + half),
        roll(corners[2 * plane_count], 124, 1),
    )
    east_count = step_count(count_ext, 1)
    sub = sublane(count_ext.shape)
    north_count = jnp.where(
        (sub < ny) | (sub == ny + 7), step_count(count_ext, 0), 0.0
    )
    counts_out[0] = count_ext
    counts_out[1] = east_count
    counts_out[2] = north_count

    def side_of(name, k):
        p = NAMES.index(name) * plane_count + k // per_plane
        return roll(planes[p], 124 - GROUP * (k % per_plane), 1)

    def rim_ext(index, plane, group):
        corner = roll(corners[plane], 124 - GROUP * group, 1)
        return jnp.concatenate([rim(index), corner], axis=1)

    def prepare(t, j, k, link_level, second):
        per_half = per_plane // 2
        first = rim_ext(2 * t + j, t // per_half, 2 * (t % per_half) + j)
        x = unpack_rows(first, roll(second, 4, 0) if j else second)
        for name in NAMES[:4] + NAMES[5:6]:
            at = link_level if name == "vm" else k
            x[name] = jnp.concatenate(
                [extend(level_of(refs[name], name, at), side_of(name, at)), x[name]], axis=0
            )
        level = k.astype(F32)
        state = x["s"]
        open_east = level < east_count
        open_north = level < north_count
        ep = jnp.where(open_east, 0.5 * x["es"] + x["mix"], 0.0)
        em = jnp.where(open_east, 0.5 * x["es"] - x["mix"], 0.0)
        np_ = jnp.where(open_north, 0.5 * x["ns"] + x["mix"], 0.0)
        nm = jnp.where(open_north, 0.5 * x["ns"] - x["mix"], 0.0)
        inner = state[:ny]
        sink = extend(level_of(refs["relax"], "relax", k), side_of("relax", k))
        sink = jnp.where(level < count_ext[:ny], sink, 0.0)
        link = jnp.where(link_level.astype(F32) + 1.0 < count_ext, x["vm"], 0.0)
        squeeze = jnp.tanh(inner)
        base = jnp.concatenate([inner - sink * squeeze, x["base"]], axis=0)
        ep_out[k] = ep
        em_out[k] = em
        np_out[k] = np_
        nm_out[k] = nm
        sink_out[k] = sink
        start_out[k] = state
        damp_out[k] = 1.0 - sink * (1.0 - squeeze * squeeze)
        return base - spread(state, ep, em, np_, nm), link

    def spread(state, ep, em, np_, nm):
        fe = ep * state + em * shift_up(state, 1)
        fn = np_ * state + nm * shift_up(state, 0)
        return (fe - shift_down(fe, 1)) + (fn - shift_down(fn, 0))

    def factor(t, carry):
        per_half = per_plane // 2
        second = rim_ext(levels + t, plane_count + t // per_half, t % per_half)
        new = []
        for j, (k, link_level) in enumerate(level_pair(levels, t)):
            ratio, c, outer = carry[j]
            rhs_k, link = prepare(t, j, k, link_level, second)
            inv = 1.0 / (1.0 + outer + link - outer * ratio)
            q = outer * inv
            ratio = link * inv
            c = rhs_k * inv + q * c
            inv_out[k] = inv
            q_out[k] = q
            r_out[k] = ratio
            carries[k] = c
            new.append((ratio, c, link))
        return tuple(new)

    zero = jnp.zeros(rhs.shape[1:], F32)
    (r_top, c_top, _), (r_low, c_low, _) = lax.fori_loop(
        0, half, factor, ((zero,) * 3,) * 2, unroll=UNROLL // 2
    )
    join = 1.0 / (1.0 - r_top * r_low)
    join_out[...] = join

    def both(one):
        def use(t, top, low):
            one(t, top)
            one(levels - 1 - t, low)

        return use

    def to_second(k, x):
        middle_out[k] = x
        inner = x[:ny]
        squeeze = jnp.tanh(inner)
        sink = sink_out[k]
        damp_out[levels + k] = 1.0 - sink * (1.0 - squeeze * squeeze)
        flow = spread(x, ep_out[k], em_out[k], np_out[k], nm_out[k])
        rhs[k, :ny] = inner - flow[:ny] - sink * squeeze

    solve_outward(levels, (c_top, c_low), lambda k: r_out[k], join, carries, both(to_second))

    main = carries.at[:, :ny]
    inv_q = (lambda k: inv_out[k, :ny], lambda k: q_out[k, :ny])
    ratio = lambda k: r_out[k, :ny]
    ends = solve_inward(levels, lambda k: rhs[k, :ny], inv_q, main)

    def to_adjoint(k, x):
        seen = extend(level_of(refs["obs"], "obs", k), side_of("obs", k))
        rhs[k, :ny] = jnp.where(k.astype(F32) < count_ext[:ny], x - seen, 0.0)

    solve_outward(levels, ends, ratio, join[:ny], main, both(to_adjoint))
    ends = solve_inward(levels, lambda k: rhs[k, :ny], inv_q, main)

    def rim_part(k, solved):
        solved_out[k] = solved
        x = edge_rows(solved)
        edge = lambda ref: edge_rows(ref[k, :ny])
        part, _ = part_of_pull(x, edge(ep_out), edge(em_out), edge_rows(damp_out[levels + k]))
        gn = shift_up(x, 0) - x
        sub = sublane(x.shape)
        part = part + jnp.where(
            sub == 0,
            edge(np_out) * gn,
            jnp.where(sub == 7, shift_down(edge(nm_out) * gn, 0), 0.0),
        )
        return pair_rows(x, part)

    group = iota((8, nx), 1) // GROUP
    for p in range(half // 8):
        send[half + p] = jnp.zeros((8, nx), F32)

    def to_send(t, top, low):
        pair = two_levels(rim_part(t, top), rim_part(levels - 1 - t, low))
        send[t] = pair[:, :nx]
        p, g = half + t // 8, t % 8
        send[p] = jnp.where(group == g, roll(pair[:, nx:], GROUP * g + 4, 1), send[p])

    solve_outward(levels, ends, ratio, join[:ny], main, to_send)


def inner_kernel(
    ep, em, np_, nm, damp, middle, solved, counts, start, part_out, late_out, run_out, rise_out,
):
    levels, ny, width = solved.shape
    nx = width // 2
    sub = sublane((ny, width))
    inside = sub < ny - 1

    def inner(k, carry):
        x = solved[k]
        state = middle[k]
        part, ge = part_of_pull(x, ep[k, :ny], em[k, :ny], damp[levels + k])
        gn = jnp.where(inside, shift_up(x, 0) - x, 0.0)
        part_out[k] = part + np_[k, :ny] * gn + shift_down(nm[k, :ny] * gn, 0)
        level = k.astype(F32)
        open_east = level < counts[1, :ny, :nx]
        open_north = level < counts[2, :ny, :nx]

        def slopes(state):
            run = (shift_up(state[:ny], 1) - state[:ny])[:, :nx]
            rise = shift_up(state[:, :nx], 0)[:ny] - state[:ny, :nx]
            return jnp.where(open_east, run, 0.0), jnp.where(open_north, rise, 0.0)

        run, rise = slopes(state)
        late_out[k] = ge[:, :nx] * run + gn[:, :nx] * rise
        run_out[k], rise_out[k] = slopes(start[k])
        return carry

    lax.fori_loop(0, levels, inner, 0, unroll=UNROLL // 2)


def backward_kernel(
    ep, em, np_, nm, inv, q, r, middle, damp, solved, counts, join, part, late, run, rise,
    rows_n, rows_s,
    adjoint_out, gradient_out, carries, adjoint, gradient, sent,
):
    levels, ny, width = solved.shape
    nx = width // 2
    half = levels // 2
    sub = sublane((8, width))

    def rims(t):
        line = merge_rows(rows_n[t], rows_s[t])
        p = half + t // 8
        corner = roll(merge_rows(rows_n[p], rows_s[p]), 124 - GROUP * (t % 8), 1)
        both = jnp.concatenate([line, corner], axis=1)
        return both, roll(both, 4, 0)

    def across(k, rim):
        inner = part[k]
        near_part = roll(rim, 6, 0)
        south = solved[k, :8] - shift_down(rim, 0)
        north = shift_up(rim, 0) - solved[k, ny - 8 :]
        np_rim, nm_rim = np_[k, ny:], nm[k, ny:]
        np_top, nm_top = np_[k, ny - 8 : ny], nm[k, ny - 8 : ny]
        low = inner[:8] + jnp.where(sub == 0, shift_down(nm_rim, 0) * south, 0.0)
        high = inner[ny - 8 :] + jnp.where(sub == 7, np_top * north, 0.0)
        outer = near_part + jnp.where(
            sub == 0, shift_down(nm_top * north, 0), np_rim * shift_up(south, 0)
        )
        rise = (shift_up(middle[k, ny:], 0) - middle[k, ny - 8 : ny])[:, :nx]
        open_north = (sub[:, :nx] == 7) & (k.astype(F32) < counts[2, ny - 8 : ny, :nx])
        extra = jnp.where(open_north, north[:, :nx] * rise, 0.0)
        gradient[k, : ny - 8] = late[k, : ny - 8]
        gradient[k, ny - 8 :] = late[k, ny - 8 :] + extra
        middle_rows = [inner[8 : ny - 8]] if ny > 16 else []
        return jnp.concatenate([low, *middle_rows, high, outer], axis=0)

    def late_step(t, carry):
        new = []
        for k, rim, last in zip((t, levels - 1 - t), rims(t), carry):
            c = across(k, rim) * inv[k] + q[k] * last
            carries[k] = c
            new.append(c)
        return tuple(new)

    zero = jnp.zeros(carries.shape[1:], F32)
    ends = lax.fori_loop(0, half, late_step, (zero, zero), unroll=UNROLL // 2)

    def early(k, x):
        inner = x[:ny]
        ge = shift_up(inner, 1) - inner
        result = inner[:, :nx] * damp[k, :, :nx] + (ep[k, :ny] * ge)[:, :nx]
        result = result + shift_down(em[k, :ny] * ge, 1)[:, :nx]
        column = x[:, :nx]
        gn = shift_up(column, 0) - column
        result = result + (np_[k, :, :nx] * gn + shift_down(nm[k, :, :nx] * gn, 0))[:ny]
        adjoint[k] = result
        gradient[k] = -(gradient[k] + ge[:, :nx] * run[k] + gn[:ny] * rise[k])

    def copies(p):
        out = []
        for i, begin in enumerate((p * UNROLL, levels - (p + 1) * UNROLL)):
            place = pl.ds(begin, UNROLL)
            for j, (source, target) in enumerate(
                ((adjoint, adjoint_out), (gradient, gradient_out))
            ):
                out.append(
                    pltpu.make_async_copy(
                        source.at[place], target.at[place], sent.at[p, 2 * i + j]
                    )
                )
        return out

    high, low = ends
    steps = half // UNROLL
    last = (low + r[half] * high) * join[...], (high + r[half - 1] * low) * join[...]

    def block(i, last):
        p = steps - 1 - i
        for g in range(UNROLL - 1, -1, -1):
            t = p * UNROLL + g
            new = []
            for k, x in ((t, last[0]), (levels - 1 - t, last[1])):
                x = carries[k] + r[k] * x
                early(k, x)
                new.append(x)
            last = tuple(new)
        for copy in copies(p):
            copy.start()
        return last

    lax.fori_loop(0, steps, block, last)
    for p in range(steps):
        for copy in copies(p):
            copy.wait()


def ring(axis, distance):
    count = lax.axis_size(axis)
    return [(i, (i + distance) % count) for i in range(count)]


def both_ways(x):
    from_north = lax.ppermute(x, "ty", ring("ty", -1))
    if lax.axis_size("ty") == 2:
        return from_north, from_north
    return from_north, lax.ppermute(x, "ty", ring("ty", 1))


def swap(x, phase):
    nx = lax.axis_size("tx")
    return lax.ppermute(
        x, "tx", [(i, (i + 1) % nx if i % 2 == phase else (i - 1) % nx) for i in range(nx)]
    )


def per_device(
    tracer_start,
    observed,
    east_speed,
    north_speed,
    mixing,
    vertical_mixing,
    relax_rate,
    level_count,
    face_east,
    face_north,
):
    levels, ny, nx = tracer_start.shape
    per_plane = 128 // GROUP
    plane_count = levels // per_plane
    pairs = (len(NAMES) * plane_count + 2) // 2
    fields = (
        tracer_start, east_speed, north_speed, mixing, relax_rate, vertical_mixing, observed,
        level_count,
    )
    half = levels // 2
    corner_planes = 2 * plane_count + 2
    *fields, rows, corners = call(
        rim_kernel,
        [jax.ShapeDtypeStruct(x.shape, x.dtype) for x in fields]
        + [(levels + half + 1, 8, nx), (corner_planes, 8, nx)],
        [pltpu.SemaphoreType.DMA((8,))],
        *[pltpu.with_memory_space_constraint(x, pltpu.HBM) for x in fields],
        space=HBM,
    )
    corners_n, corners_s = both_ways(corners)
    rows_n, rows_s = both_ways(rows)
    (planes,) = call(column_kernel, [(2 * pairs, ny, nx)], [], *fields)
    packed = (pairs * ny + corner_planes // 2 * 8, nx)
    one, two = call(
        halves_kernel, [packed, (packed[0] + 8, nx)], [], planes, corners_n, corners_s,
        cost=pl.CostEstimate(flops=10**10, bytes_accessed=0, transcendentals=0),
    )
    from_two = swap(two, 1)
    from_one = swap(one, 0)
    ext = (levels, ny + 8, 2 * nx)
    block = (levels, ny, 2 * nx)
    outs = call(
        forward_kernel,
        [ext] * 4 + [block] + [ext] * 4
        + [(2 * levels, ny, 2 * nx), block, (3,) + ext[1:], ext[1:], ext]
        + [(half + half // 8, 8, nx)],
        [(2 * pairs, ny, nx), (corner_planes, 8, nx), ext, ext],
        *fields, from_one, from_two, rows_n, rows_s,
    )
    ep, em, np_, nm, _, inv, q, r, middle, damp, solved, counts, join, start, send = outs
    sent_n, sent_s = both_ways(send)
    part, late, run, rise = call(
        inner_kernel,
        [block] + [(levels, ny, nx)] * 3,
        [],
        ep, em, np_, nm, damp, middle, solved, counts, start,
        cost=pl.CostEstimate(flops=0, bytes_accessed=8 << 20, transcendentals=0),
    )
    adjoint, gradient = call(
        backward_kernel,
        [(levels, ny, nx)] * 2,
        [ext] + [(levels, ny, nx)] * 2 + [pltpu.SemaphoreType.DMA((half // UNROLL, 4))],
        ep, em, np_, nm, inv, q, r, middle, damp, solved, counts, join, part, late, run, rise,
        sent_n, sent_s,
        out_space=HBM,
    )
    return adjoint, gradient


def solution(mesh):
    block = P(None, "ty", "tx")
    plane = P("ty", "tx")
    return jax.shard_map(
        per_device,
        mesh=mesh,
        in_specs=(block,) * 7 + (plane,) * 3,
        out_specs=(block, block),
        check_vma=False,
    )
```

```python
import functools

import jax
import jax.numpy as jnp
from jax import lax
from jax.experimental import pallas as pl
from jax.experimental.pallas import tpu as pltpu
from jax.sharding import PartitionSpec as P

F32 = jnp.float32
VMEM = pl.BlockSpec(memory_space=pltpu.VMEM)
HBM = pl.BlockSpec(memory_space=pltpu.HBM)
UNROLL = 8
STEPS = 4
GROUP = 8
NAMES = ("s", "es", "ns", "mix", "relax", "vm", "obs")


def call(kernel, outs, scratch, *args, space=VMEM, out_space=VMEM, cost=None):
    def typed(x):
        return x if isinstance(x, jax.ShapeDtypeStruct) else jax.ShapeDtypeStruct(x, F32)

    return pl.pallas_call(
        kernel,
        out_shape=[typed(x) for x in outs],
        in_specs=[space] * len(args),
        out_specs=[out_space] * len(outs),
        scratch_shapes=[pltpu.VMEM(x, F32) if isinstance(x, tuple) else x for x in scratch],
        compiler_params=pltpu.CompilerParams(vmem_limit_bytes=16 << 20),
        cost_estimate=cost,
    )(*args)


def iota(shape, dim):
    return lax.broadcasted_iota(jnp.int32, shape, dim)


def roll(x, shift, axis):
    if isinstance(shift, int):
        shift = shift % x.shape[axis]
        if shift == 0:
            return x
    return pltpu.roll(x, shift, axis)


def odd_column():
    return lax.rem(lax.axis_index("tx"), 2) == 1


def level_of(ref, name, level):
    if name == "vm":
        level = jnp.minimum(level, ref.shape[0] - 1)
    return ref[level].astype(F32)


def edge_rows(block):
    return jnp.where(iota((8, block.shape[1]), 0) < 4, block[:8], block[-8:])


def sublane(shape):
    return iota(shape, 0)


def step_count(counts, axis):
    return jnp.minimum(counts, shift_up(counts, axis))


def pair_rows(first, second):
    sub = sublane(first.shape)
    return jnp.where((sub == 1) | (sub == 2), roll(second, 2, 0), first)


def level_pair(levels, t):
    return (t, t), (levels - 1 - t, levels - 2 - t)


def in_all_groups(x):
    group = iota(x.shape, 1) // GROUP
    out = jnp.zeros(x.shape, F32)
    for g in range(x.shape[1] // GROUP):
        out = jnp.where(group == g, roll(x, GROUP * g + 4, 1), out)
    return out


def pack_rows(get, counts, level):
    tile = {name: edge_rows(get(name)) for name in NAMES[:6]}
    s = tile["s"]
    sub = sublane(s.shape)
    open_north = level < step_count(counts, 0)
    fn = jnp.where(
        open_north,
        (0.5 * tile["ns"] + tile["mix"]) * s + (0.5 * tile["ns"] - tile["mix"]) * shift_up(s, 0),
        0.0,
    )
    sink = jnp.where(level < counts, tile["relax"], 0.0)
    inner = jnp.where(sub == 0, -fn, jnp.where(sub == 7, shift_down(fn, 0), 0.0))
    base = s - sink * jnp.tanh(s) + inner
    first = pair_rows(s, base)
    first = jnp.where((sub == 3) | (sub == 4), roll(tile["es"], 4, 0), first)
    first = jnp.where((sub == 5) | (sub == 6), roll(tile["mix"], 6, 0), first)
    return first, pair_rows(tile["vm"], tile["ns"])


def unpack_rows(first, second):
    return {
        "s": first,
        "base": roll(first, 6, 0),
        "es": roll(first, 4, 0),
        "mix": roll(first, 2, 0),
        "vm": second,
        "ns": roll(second, 6, 0),
    }


def two_levels(x, y):
    sub = sublane(x.shape)
    return jnp.where((sub >= 3) & (sub <= 6), roll(y, 4, 0), x)


def shift_up(x, axis):
    return roll(x, -1, axis)


def shift_down(x, axis):
    return roll(x, 1, axis)


def rim_kernel(*args):
    fields = args[:10]
    s, es, ns, mix, relax, vm, obs, count, *_ = kept = args[10:20]
    rows, corners, arrived = args[20:]
    copies = [pltpu.make_async_copy(fields[i], kept[i], arrived.at[i]) for i in range(10)]
    first = (7, 0, 1, 2, 3, 4, 5)
    rest = (6, 8, 9)
    for i in first + rest:
        copies[i].start()
    for i in first:
        copies[i].wait()
    refs = dict(zip(NAMES, (s, es, ns, mix, relax, vm, obs)))
    levels = s.shape[0]
    per_plane = 128 // GROUP
    small = (8, s.shape[2])
    group = iota(small, 1) // GROUP
    half = per_plane // 2
    plane_count = levels // per_plane
    counts = edge_rows(count[...].astype(F32))

    def rims(p, carry):
        acc = jnp.zeros(small, F32)
        late = jnp.zeros(small, F32)
        for g in range(half):
            t = p * half + g
            seconds = []
            for j, (k, link) in enumerate(level_pair(levels, t)):
                first, second = pack_rows(
                    lambda name: level_of(refs[name], name, link if name == "vm" else k),
                    counts,
                    k.astype(F32),
                )
                seconds.append(second)
                rows[2 * t + j] = first
                place = 2 * g + j
                acc = jnp.where(group == place, roll(first, GROUP * place + 4, 1), acc)
                late = jnp.where(group == place, roll(second, GROUP * place + 4, 1), late)
            rows[levels + t] = two_levels(*seconds)
        corners[p] = acc
        corners[plane_count + p] = late
        return carry

    lax.fori_loop(0, plane_count, rims, 0)
    rows[levels + levels // 2] = counts
    corners[2 * plane_count] = in_all_groups(counts)
    for p in range(2 * plane_count + 1, corners.shape[0]):
        corners[p] = jnp.zeros(small, F32)
    for i in rest:
        copies[i].wait()


def column_kernel(s, es, ns, mix, relax, vm, obs, count, planes):
    refs = dict(zip(NAMES, (s, es, ns, mix, relax, vm, obs)))
    levels = s.shape[0]
    per_plane = 128 // GROUP
    plane_count = levels // per_plane
    shape = s.shape[1:]
    group = iota(shape, 1) // GROUP

    def columns(p, carry):
        for a, name in enumerate(NAMES):
            acc = jnp.zeros(shape, F32)
            for g in range(per_plane):
                pair = level_pair(levels, p * (per_plane // 2) + g // 2)
                x = refs[name][pair[g % 2][name == "vm"]].astype(F32)
                acc = jnp.where(group == g, roll(x, GROUP * g + 4, 1), acc)
            planes[a * plane_count + p] = acc
        return carry

    lax.fori_loop(0, plane_count, columns, 0)
    total = len(NAMES) * plane_count
    planes[total] = in_all_groups(count[...].astype(F32))
    for p in range(total + 1, planes.shape[0]):
        planes[p] = jnp.zeros(shape, F32)


def merge_rows(north, south):
    return jnp.where(sublane(north.shape) % 2 == 0, north, south)


def halves_kernel(planes, corners_n, corners_s, one, two, kept):
    odd = odd_column()
    pairs = planes.shape[0] // 2
    ny = planes.shape[1]

    def put(place, x, y):
        low = iota(x.shape, 1) % GROUP < 4
        to_east = jnp.where(low, x, roll(y, 4, 1))
        to_west = jnp.where(low, roll(x, -4, 1), y)
        one[place] = jnp.where(odd, to_west, to_east)
        two[place] = jnp.where(odd, to_east, to_west)

    for h in range(pairs):
        put(pl.ds(h * ny, ny), planes[2 * h], planes[2 * h + 1])

    count = corners_n.shape[0]
    two[pl.ds(one.shape[0], 8)] = jnp.zeros((8, one.shape[1]), F32)

    def corner(p):
        return merge_rows(corners_n[p], corners_s[p])

    for h in range(count // 2):
        x, y = corner(2 * h), corner(2 * h + 1)
        kept[2 * h] = x
        kept[2 * h + 1] = y
        put(pl.ds(pairs * ny + h * 8, 8), x, y)


def extend(main, side, rows=None, corners=None):
    top = jnp.concatenate([main, side], axis=1)
    if rows is None:
        return top
    return jnp.concatenate([top, jnp.concatenate([rows, corners], axis=1)], axis=0)


def solve_inward(levels, get, inv_q, carries):
    half = levels // 2
    inv, q = inv_q

    def step(t, carry):
        new = []
        for k, last in ((t, carry[0]), (levels - 1 - t, carry[1])):
            c = get(k) * inv(k) + q(k) * last
            carries[k] = c
            new.append(c)
        return tuple(new)

    zero = jnp.zeros(carries.shape[1:], F32)
    return lax.fori_loop(0, half, step, (zero, zero), unroll=UNROLL)


def solve_outward(levels, ends, ratio, join, carries, use):
    half = levels // 2
    high, low = ends
    upper = (high + ratio(half - 1) * low) * join
    lower = (low + ratio(half) * high) * join

    def block(i, last):
        m = half // STEPS - 1 - i
        for u in range(STEPS - 1, -1, -1):
            t = m * STEPS + u
            new = []
            for k, x in ((t, last[0]), (levels - 1 - t, last[1])):
                new.append(carries[k] + ratio(k) * x)
            use(t, m, u, *new)
            last = tuple(new)
        return last

    lax.fori_loop(0, half // STEPS, block, (lower, upper), unroll=2)


def merge_halos(odd, from_one, from_two, planes, start):
    size = planes.shape[1]
    low = iota(planes.shape[1:], 1) % GROUP < 4
    for h in range(planes.shape[0] // 2):
        place = pl.ds(start + h * size, size)
        a, b = from_one[place], from_two[place]
        west = jnp.where(odd, a, b)
        east = jnp.where(odd, b, a)
        planes[2 * h] = jnp.where(low, west, roll(east, 4, 1))
        planes[2 * h + 1] = jnp.where(low, roll(west, -4, 1), east)


def part_of_pull(x, ep, em, damp):
    ge = shift_up(x, 1) - x
    return x * damp + ep * ge + shift_down(em * ge, 1), ge


def local_kernel(
    s, es, ns, mix, relax, vm, count, east, north, after,
    ep_out, em_out, np_out, nm_out, sink_out, damp_out, local_out, inv_out, q_out, r_out,
    moves_out,
):
    levels, ny, nx = s.shape
    half = levels // 2
    counts = count[...].astype(F32)
    east_count = east[...].astype(F32)
    north_count = north[...].astype(F32)
    lane = iota((ny, nx), 1)
    sub = sublane((ny, nx))

    def prepare(k):
        level = k.astype(F32)
        state = s[k]
        diffusion = mix[k].astype(F32)
        speed_east = 0.5 * es[k].astype(F32)
        speed_north = 0.5 * ns[k].astype(F32)
        open_east = level < east_count
        open_north = level < north_count
        ep = jnp.where(open_east, speed_east + diffusion, 0.0)
        em = jnp.where(open_east, speed_east - diffusion, 0.0)
        np_ = jnp.where(open_north, speed_north + diffusion, 0.0)
        nm = jnp.where(open_north, speed_north - diffusion, 0.0)
        sink = jnp.where(level < counts, relax[k].astype(F32), 0.0)
        squeeze = jnp.tanh(state)
        ep_out[k] = ep
        em_out[k] = em
        np_out[k] = np_
        nm_out[k] = nm
        sink_out[k] = sink
        damp_out[k] = 1.0 - sink * (1.0 - squeeze * squeeze)
        fe = ep * state + em * shift_up(state, 1)
        fe = jnp.where(lane == nx - 1, 0.0, fe)
        fn = np_ * state + nm * jnp.where(sub == ny - 1, 0.0, shift_up(state, 0))
        flow = fe - shift_down(fe, 1)
        flow = flow + (fn - jnp.where(sub == 0, 0.0, shift_down(fn, 0)))
        local_out[k] = state - sink * squeeze - flow

    def factor(t, carry):
        new = []
        for (k, link_level), (ratio, outer) in zip(level_pair(levels, t), carry):
            prepare(k)
            link = jnp.where(
                link_level.astype(F32) + 1.0 < counts, vm[link_level].astype(F32), 0.0
            )
            inv = 1.0 / (1.0 + outer + link - outer * ratio)
            ratio = link * inv
            inv_out[k] = inv
            q_out[k] = outer * inv
            r_out[k] = ratio
            new.append((ratio, link))
        return tuple(new)

    zero = jnp.zeros((ny, nx), F32)
    lax.fori_loop(0, half, factor, ((zero, zero), (zero, zero)), unroll=UNROLL)

    source = iota((2 * nx, 2 * nx), 0) % nx
    target = iota((2 * nx, 2 * nx), 1)
    for u in range(STEPS):
        group = 2 * u + target // nx
        hit = source == (target + 4 + GROUP * group) % nx
        moves_out[u] = jnp.where(hit, 1.0, 0.0).astype(jnp.bfloat16)


def whole(own, halo):
    ny = own.shape[0]
    return extend(own, halo[:ny], halo[ny + 8 :], halo[ny : ny + 8])


def forward_kernel(
    s, obs, count, from_one, from_two, own_planes, own_corners, rows_n, rows_s,
    ep, em, np_, nm, sink, local, inv, q, r, moves,
    ep_halo, em_halo, np_halo, nm_halo, sink_halo, inv_halo, q_halo, r_halo, s_halo,
    middle_out, damp_out, solved_out, counts_out, join_out, send,
    planes, corners, rhs, carries, packed, moved, moved_rows, sides,
):
    levels, ny, nx = s.shape
    half = levels // 2
    per_plane = 128 // GROUP
    plane_count = levels // per_plane
    odd = odd_column()
    merge_halos(odd, from_one, from_two, planes, 0)
    merge_halos(odd, from_one, from_two, corners, planes.shape[0] // 2 * planes.shape[1])

    def rim(index):
        return merge_rows(rows_n[index], rows_s[index])

    count_plane = len(NAMES) * plane_count
    count_ext = extend(
        count[...].astype(F32),
        roll(planes[count_plane], 124, 1),
        rim(levels + half),
        roll(corners[2 * plane_count], 124, 1),
    )
    east_ext = step_count(count_ext, 1)
    counts_out[0] = count_ext
    counts_out[1] = east_ext
    counts_out[2] = step_count(count_ext, 0)
    count_halo = jnp.concatenate(
        [count_ext[:ny, nx:], count_ext[ny:, nx:], count_ext[ny:, :nx]], axis=0
    )
    small_sub = sublane((8, nx))
    east_rows = east_ext[ny:, :nx]
    north_rows = jnp.where(small_sub == 7, counts_out[2, ny:, :nx], 0.0)
    lane = iota((ny, nx), 1)
    per_half = per_plane // 2

    strip = (ny + 8, nx)
    place = iota(strip, 1) % GROUP
    low = place < 4
    groups = iota(strip, 1) // GROUP
    from_top = groups % 2 == 0
    strip_sub = sublane(strip)

    def columns(p, carry):
        t = p * per_half + groups // 2
        level = jnp.where(from_top, t, levels - 1 - t).astype(F32)
        link_level = jnp.where(from_top, t, levels - 2 - t).astype(F32)

        def side_and_corner(a, c):
            return jnp.concatenate([a, c], axis=0)

        def strips(west):
            def pick(halo, own):
                near_side = low[: halo.shape[0]]
                return jnp.where(near_side, halo, own) if west else jnp.where(near_side, own, halo)

            x = unpack_rows(
                pick(corners[p], own_corners[p]),
                pick(corners[plane_count + p], own_corners[plane_count + p]),
            )
            side = {}
            for a, name in enumerate(NAMES[:6]):
                at = a * plane_count + p
                side[name] = pick(planes[at], own_planes[at])
            for name in NAMES[:4] + NAMES[5:6]:
                x[name] = side_and_corner(side[name], x[name])
            counts = side_and_corner(
                pick(planes[count_plane], own_planes[count_plane]),
                pick(corners[2 * plane_count], own_corners[2 * plane_count]),
            )
            state = x["s"]
            open_east = level < step_count(counts, 1)
            open_north = (level < step_count(counts, 0)) & (
                (strip_sub < ny) | (strip_sub == ny + 7)
            )
            ep_s = jnp.where(open_east, 0.5 * x["es"] + x["mix"], 0.0)
            em_s = jnp.where(open_east, 0.5 * x["es"] - x["mix"], 0.0)
            np_s = jnp.where(open_north, 0.5 * x["ns"] + x["mix"], 0.0)
            nm_s = jnp.where(open_north, 0.5 * x["ns"] - x["mix"], 0.0)
            sink_s = jnp.where(level[:ny] < counts[:ny], side["relax"], 0.0)
            link = jnp.where(link_level + 1.0 < counts, x["vm"], 0.0)
            fe = ep_s * state + em_s * shift_up(state, 1)
            fe_west = shift_down(fe, 1)
            fn = np_s * state + nm_s * shift_up(state, 0)
            base = side_and_corner(side["s"] - sink_s * jnp.tanh(side["s"]), x["base"])
            right = base - (fe - fe_west) - (fn - shift_down(fn, 0))
            return (right, link, np_s, nm_s, ep_s, em_s, sink_s, state), fe, fe_west

        west, _, through_west = strips(True)
        east, through_east, _ = strips(False)
        seam = jnp.where(place == 3, through_east, through_west)
        both = [jnp.where(low[: a.shape[0]], a, b) for a, b in zip(west, east)]
        right, link, np_c, nm_c = (x[ny:] for x in both[:4])
        corner = pair_rows(right, link)
        corner = jnp.where((small_sub == 3) | (small_sub == 4), roll(seam[ny:], 4, 0), corner)
        corner = jnp.where(small_sub == 5, roll(np_c, 6, 0), corner)
        corner = jnp.where(small_sub == 6, roll(nm_c, 7, 0), corner)
        both = [x[:ny] for x in both]
        seen = planes[NAMES.index("obs") * plane_count + p]
        both = both[:2] + [seam[:ny], seen] + both[2:] + [jnp.concatenate([corner] * 2, axis=0)]
        for i, x in enumerate(both):
            split(p, i * ny, x)
        return carry

    def split(p, at, x):
        for h, y in enumerate((x, roll(x, nx // 2, 1))):
            high = y.astype(jnp.bfloat16)
            packed[2 * p + h, at : at + ny, :nx] = high
            packed[2 * p + h, at : at + ny, nx:] = (y - high.astype(F32)).astype(jnp.bfloat16)

    lax.fori_loop(0, plane_count, columns, 0, unroll=plane_count)

    def unpack(u):
        move = moves[u]

        def place_both(m, carry):
            out = jnp.dot(packed[m], move, preferred_element_type=F32)
            t = m * STEPS + u
            for j, k in enumerate((t, levels - 1 - t)):
                x = out[:, j * nx : (j + 1) * nx]
                np_x, nm_x, ep_x, em_x, sink_x, s_x, corner = (
                    x[i * ny : (i + 1) * ny] for i in range(4, 11)
                )
                corner = corner[:8]
                moved[k] = x[: 4 * ny]
                moved_rows[k] = corner
                ep_halo[k, :ny] = ep_x
                em_halo[k, :ny] = em_x
                np_halo[k, :ny] = np_x
                nm_halo[k, :ny] = nm_x
                np_halo[k, ny : ny + 8] = roll(corner, 2, 0)
                nm_halo[k, ny : ny + 8] = roll(corner, 1, 0)
                sink_halo[k] = sink_x
                s_halo[k, :ny] = s_x
            return carry

        lax.fori_loop(0, 2 * plane_count, place_both, 0, unroll=2 * plane_count)

    for u in range(STEPS):
        unpack(u)

    def prepare(m, u, j, k, link_level, second):
        t = m * STEPS + u
        x = unpack_rows(rim(2 * t + j), roll(second, 4, 0) if j else second)
        level = k.astype(F32)
        row = x["s"]
        open_east = level < east_rows
        open_north = level < north_rows
        ep_r = jnp.where(open_east, 0.5 * x["es"] + x["mix"], 0.0)
        em_r = jnp.where(open_east, 0.5 * x["es"] - x["mix"], 0.0)
        np_r = jnp.where(open_north, 0.5 * x["ns"] + x["mix"], 0.0)
        nm_r = jnp.where(open_north, 0.5 * x["ns"] - x["mix"], 0.0)
        link_r = jnp.where(link_level.astype(F32) + 1.0 < count_halo[ny + 8 :], x["vm"], 0.0)
        corner = moved_rows[k]
        right, link, seam = (moved[k, i * ny : (i + 1) * ny] for i in range(3))
        seam_rows = roll(corner, 4, 0)
        np_halo[k, ny + 8 :] = np_r
        nm_halo[k, ny + 8 :] = nm_r
        s_halo[k, ny + 8 :] = row

        own = s[k]
        last, first = lane == nx - 1, lane == 0
        fe = ep_r * row + em_r * shift_up(row, 1)
        flow = jnp.where(last[:8], seam_rows, fe) - jnp.where(
            first[:8], seam_rows, shift_down(fe, 1)
        )
        fn = np_r * row + nm_r * shift_up(own[:8], 0)
        top = np_[k, ny - 8 :] * own[ny - 8 :]
        cross = nm[k, ny - 8 :] * shift_up(row, 0)
        from_block = jnp.where(small_sub == 0, shift_down(top + cross, 0), 0.0)
        right_r = x["base"] - flow - (fn - from_block)

        inner = local[k] + jnp.where(first, seam, jnp.where(last, -seam, 0.0))
        low_rows = inner[:8] + jnp.where(small_sub == 0, shift_down(fn, 0), 0.0)
        high_rows = inner[ny - 8 :] - jnp.where(small_sub == 7, cross, 0.0)
        between = [inner[8 : ny - 8]] if ny > 16 else []
        inner = jnp.concatenate([low_rows] + between + [high_rows], axis=0)
        halo = jnp.concatenate([right, corner, right_r], axis=0)
        return inner, halo, jnp.concatenate([link, roll(corner, 6, 0), link_r], axis=0)

    def factor(m, carry):
        for u in range(STEPS):
            carry = factor_step(m, u, carry)
        return carry

    def factor_step(m, u, carry):
        t = m * STEPS + u
        second = rim(levels + t)
        new = []
        for j, (k, link_level) in enumerate(level_pair(levels, t)):
            ratio, c_own, c_halo, outer = carry[j]
            own, halo, link = prepare(m, u, j, k, link_level, second)
            inv_h = 1.0 / (1.0 + outer + link - outer * ratio)
            q_h = outer * inv_h
            ratio = link * inv_h
            c_own = own * inv[k] + q[k] * c_own
            c_halo = halo * inv_h + q_h * c_halo
            inv_halo[k] = inv_h
            q_halo[k] = q_h
            r_halo[k] = ratio
            carries[k] = whole(c_own, c_halo)
            new.append((ratio, c_own, c_halo, link))
        return tuple(new)

    zero = jnp.zeros(count_halo.shape, F32)
    begin = (zero, jnp.zeros((ny, nx), F32), zero, zero)
    (r_top, top_own, top_halo, _), (r_low, low_own, low_halo, _) = lax.fori_loop(
        0, half // STEPS, factor, (begin, begin), unroll=2
    )
    c_top, c_low = whole(top_own, top_halo), whole(low_own, low_halo)
    join = 1.0 / (1.0 - whole(r[half - 1], r_top) * whole(r[half], r_low))
    join_out[...] = join

    def ext(own, halo):
        return lambda k: whole(own[k], halo[k])

    def inner(own, halo):
        return lambda k: extend(own[k], halo[k, :ny])

    def spread(state, ep, em, np_, nm):
        fe = ep * state + em * shift_up(state, 1)
        fn = np_ * state + nm * shift_up(state, 0)
        return (fe - shift_down(fe, 1)) + (fn - shift_down(fn, 0))

    def both(one):
        def use(t, m, u, top, low):
            one(t, top, m, u, 0)
            one(levels - 1 - t, low, m, u, 1)

        return use

    def to_second(k, x, m, u, j):
        middle_out[k] = x
        state = x[:ny]
        squeeze = jnp.tanh(state)
        loss = inner(sink, sink_halo)(k)
        damp_out[k] = 1.0 - loss * (1.0 - squeeze * squeeze)
        fields = (ext(ep, ep_halo), ext(em, em_halo), ext(np_, np_halo), ext(nm, nm_halo))
        flow = spread(x, *(field(k) for field in fields))
        rhs[k] = state - flow[:ny] - loss * squeeze

    solve_outward(levels, (c_top, c_low), ext(r, r_halo), join, carries, both(to_second))

    main = carries.at[:, :ny]
    inv_q = inner(inv, inv_halo), inner(q, q_halo)
    ratio = inner(r, r_halo)
    ends = solve_inward(levels, lambda k: rhs[k], inv_q, main)

    def to_adjoint(k, x, m, u, j):
        seen = extend(obs[k].astype(F32), moved[k, 3 * ny :])
        rhs[k] = jnp.where(k.astype(F32) < count_ext[:ny], x - seen, 0.0)

    solve_outward(levels, ends, ratio, join[:ny], main, both(to_adjoint))
    ends = solve_inward(levels, lambda k: rhs[k], inv_q, main)

    def rim_part(k, solved):
        solved_out[k] = solved
        x = edge_rows(solved)
        rows_of = lambda own, halo: edge_rows(inner(own, halo)(k))
        part, _ = part_of_pull(
            x, rows_of(ep, ep_halo), rows_of(em, em_halo), edge_rows(damp_out[k])
        )
        gn = shift_up(x, 0) - x
        sub = sublane(x.shape)
        part = part + jnp.where(
            sub == 0,
            rows_of(np_, np_halo) * gn,
            jnp.where(sub == 7, shift_down(rows_of(nm, nm_halo) * gn, 0), 0.0),
        )
        return pair_rows(x, part)

    group = iota((8, nx), 1) // GROUP

    def to_send(t, m, u, top, low):
        pair = two_levels(rim_part(t, top), rim_part(levels - 1 - t, low))
        send[t] = pair[:, :nx]
        before = jnp.zeros((8, nx), F32) if u == STEPS - 1 else sides[m]
        moved = roll(pair[:, nx:], 2 * GROUP * u + 4, 1)
        sides[m] = jnp.where(group == 2 * u, moved, before)

    solve_outward(levels, ends, ratio, join[:ny], main, to_send)
    for p in range(half // 8):
        send[half + p] = jnp.where(group % 2 == 0, sides[2 * p], roll(sides[2 * p + 1], GROUP, 1))


def inner_kernel(
    ep, em, np_, nm, ep_halo, em_halo, np_halo, nm_halo, damp, middle, solved, counts,
    s, s_halo, part_out, late_out, run_out, rise_out,
):
    levels, ny, width = solved.shape
    nx = width // 2
    sub = sublane((ny, width))
    inside = sub < ny - 1

    def inner(k, carry):
        x = solved[k]
        state = middle[k]
        field = lambda own, halo: extend(own[k], halo[k, :ny])
        part, ge = part_of_pull(x, field(ep, ep_halo), field(em, em_halo), damp[k])
        gn = jnp.where(inside, shift_up(x, 0) - x, 0.0)
        part_out[k] = (
            part + field(np_, np_halo) * gn + shift_down(field(nm, nm_halo) * gn, 0)
        )
        level = k.astype(F32)
        open_east = level < counts[1, :ny, :nx]
        open_north = level < counts[2, :ny, :nx]

        def slopes(state):
            run = (shift_up(state[:ny], 1) - state[:ny])[:, :nx]
            rise = shift_up(state[:, :nx], 0)[:ny] - state[:ny, :nx]
            return jnp.where(open_east, run, 0.0), jnp.where(open_north, rise, 0.0)

        run, rise = slopes(state)
        late_out[k] = ge[:, :nx] * run + gn[:, :nx] * rise
        run_out[k], rise_out[k] = slopes(whole(s[k], s_halo[k]))
        return carry

    lax.fori_loop(0, levels, inner, 0, unroll=UNROLL)


def backward_kernel(
    ep, em, np_, nm, inv, q, r, ep_halo, em_halo, np_halo, nm_halo, inv_halo, q_halo, r_halo,
    middle, damp, solved, counts, join, part, late, run, rise, rows_n, rows_s,
    adjoint_out, gradient_out, carries, adjoint, gradient, sides, sent,
):
    levels, ny, width = solved.shape
    nx = width // 2
    half = levels // 2
    sub = sublane((8, width))

    for p in range(half // 8):
        side = merge_rows(rows_n[half + p], rows_s[half + p])
        sides[2 * p] = side
        sides[2 * p + 1] = roll(side, -GROUP, 1)

    def rims(m, u):
        t = m * STEPS + u
        line = merge_rows(rows_n[t], rows_s[t])
        corner = roll(sides[m], 124 - 2 * GROUP * u, 1)
        both = jnp.concatenate([line, corner], axis=1)
        return both, roll(both, 4, 0)

    def across(k, rim):
        inner = part[k]
        near_part = roll(rim, 6, 0)
        south = solved[k, :8] - shift_down(rim, 0)
        north = shift_up(rim, 0) - solved[k, ny - 8 :]
        north_plus = whole(np_[k], np_halo[k])
        north_minus = whole(nm[k], nm_halo[k])
        np_rim, nm_rim = north_plus[ny:], north_minus[ny:]
        np_top, nm_top = north_plus[ny - 8 : ny], north_minus[ny - 8 : ny]
        low = inner[:8] + jnp.where(sub == 0, shift_down(nm_rim, 0) * south, 0.0)
        high = inner[ny - 8 :] + jnp.where(sub == 7, np_top * north, 0.0)
        outer = near_part + jnp.where(
            sub == 0, shift_down(nm_top * north, 0), np_rim * shift_up(south, 0)
        )
        rise = (shift_up(middle[k, ny:], 0) - middle[k, ny - 8 : ny])[:, :nx]
        open_north = (sub[:, :nx] == 7) & (k.astype(F32) < counts[2, ny - 8 : ny, :nx])
        extra = jnp.where(open_north, north[:, :nx] * rise, 0.0)
        gradient[k, : ny - 8] = late[k, : ny - 8]
        gradient[k, ny - 8 :] = late[k, ny - 8 :] + extra
        middle_rows = [inner[8 : ny - 8]] if ny > 16 else []
        return jnp.concatenate([low, *middle_rows, high, outer], axis=0)

    def late_steps(m, carry):
        for u in range(STEPS):
            t = m * STEPS + u
            new = []
            for k, rim, last in zip((t, levels - 1 - t), rims(m, u), carry):
                c = across(k, rim) * whole(inv[k], inv_halo[k])
                c = c + whole(q[k], q_halo[k]) * last
                carries[k] = c
                new.append(c)
            carry = tuple(new)
        return carry

    zero = jnp.zeros(carries.shape[1:], F32)
    ends = lax.fori_loop(0, half // STEPS, late_steps, (zero, zero), unroll=2)

    def early(k, x):
        inner = x[:ny]
        ge = shift_up(inner, 1) - inner
        result = inner[:, :nx] * damp[k] + ep[k] * ge[:, :nx]
        result = result + shift_down(extend(em[k], em_halo[k, :ny]) * ge, 1)[:, :nx]
        column = x[:, :nx]
        gn = shift_up(column, 0) - column
        minus = jnp.concatenate([nm[k], nm_halo[k, ny + 8 :]], axis=0)
        result = result + np_[k] * gn[:ny] + shift_down(minus * gn, 0)[:ny]
        adjoint[k] = result
        gradient[k] = -(gradient[k] + ge[:, :nx] * run[k] + gn[:ny] * rise[k])

    def copies(p):
        out = []
        for i, begin in enumerate((p * UNROLL, levels - (p + 1) * UNROLL)):
            place = pl.ds(begin, UNROLL)
            for j, (source, target) in enumerate(
                ((adjoint, adjoint_out), (gradient, gradient_out))
            ):
                out.append(
                    pltpu.make_async_copy(
                        source.at[place], target.at[place], sent.at[p, 2 * i + j]
                    )
                )
        return out

    high, low = ends
    steps = half // UNROLL
    ratio = lambda k: whole(r[k], r_halo[k])
    last = (low + ratio(half) * high) * join[...], (high + ratio(half - 1) * low) * join[...]

    def block(i, last):
        p = steps - 1 - i
        for g in range(UNROLL - 1, -1, -1):
            t = p * UNROLL + g
            new = []
            for k, x in ((t, last[0]), (levels - 1 - t, last[1])):
                x = carries[k] + ratio(k) * x
                early(k, x)
                new.append(x)
            last = tuple(new)
        for copy in copies(p):
            copy.start()
        return last

    lax.fori_loop(0, steps, block, last)
    for p in range(steps):
        for copy in copies(p):
            copy.wait()


def ring(axis, distance):
    count = lax.axis_size(axis)
    return [(i, (i + distance) % count) for i in range(count)]


def both_ways(x):
    from_north = lax.ppermute(x, "ty", ring("ty", -1))
    if lax.axis_size("ty") == 2:
        return from_north, from_north
    return from_north, lax.ppermute(x, "ty", ring("ty", 1))


def swap(x, phase):
    nx = lax.axis_size("tx")
    return lax.ppermute(
        x, "tx", [(i, (i + 1) % nx if i % 2 == phase else (i - 1) % nx) for i in range(nx)]
    )


def per_device(
    tracer_start,
    observed,
    east_speed,
    north_speed,
    mixing,
    vertical_mixing,
    relax_rate,
    level_count,
    face_east,
    face_north,
):
    levels, ny, nx = tracer_start.shape
    per_plane = 128 // GROUP
    plane_count = levels // per_plane
    pairs = (len(NAMES) * plane_count + 2) // 2
    fields = (
        tracer_start, east_speed, north_speed, mixing, relax_rate, vertical_mixing, observed,
        level_count, face_east, face_north,
    )
    half = levels // 2
    corner_planes = 2 * plane_count + 2
    *fields, rows, corners = call(
        rim_kernel,
        [jax.ShapeDtypeStruct(x.shape, x.dtype) for x in fields]
        + [(levels + half + 1, 8, nx), (corner_planes, 8, nx)],
        [pltpu.SemaphoreType.DMA((10,))],
        *[pltpu.with_memory_space_constraint(x, pltpu.HBM) for x in fields],
        space=HBM,
    )
    corners_n, corners_s = both_ways(corners)
    rows_n, rows_s = both_ways(rows)
    (planes,) = call(column_kernel, [(2 * pairs, ny, nx)], [], *fields[:8])
    packed = (pairs * ny + corner_planes // 2 * 8, nx)
    one, two, own_corners = call(
        halves_kernel, [packed, (packed[0] + 8, nx), corners.shape], [],
        planes, corners_n, corners_s,
        cost=pl.CostEstimate(flops=10**10, bytes_accessed=0, transcendentals=0),
    )
    from_two = swap(two, 1)
    from_one = swap(one, 0)
    ext = (levels, ny + 8, 2 * nx)
    block = (levels, ny, 2 * nx)
    own = (levels, ny, nx)
    halo = (levels, ny + 16, nx)
    s, es, ns, mix, relax, vm, obs, count, east, north = fields
    *coefficients, damp, local, inv, q, r, moves = call(
        local_kernel,
        [own] * 10 + [jax.ShapeDtypeStruct((STEPS, 2 * nx, 2 * nx), jnp.bfloat16)],
        [],
        s, es, ns, mix, relax, vm, count, east, north, one,
        cost=pl.CostEstimate(flops=10**9, bytes_accessed=0, transcendentals=0),
    )
    ep, em, np_, nm, sink = coefficients
    outs = call(
        forward_kernel,
        [halo] * 4 + [own] + [halo] * 4 + [ext, block, block, (3,) + ext[1:], ext[1:]]
        + [(half + half // 8, 8, nx)],
        [
            planes.shape,
            corners.shape,
            block,
            ext,
            pltpu.VMEM((2 * plane_count, 11 * ny, 2 * nx), jnp.bfloat16),
            (levels, 4 * ny, nx),
            (levels, 8, nx),
            (2 * plane_count, 8, nx),
        ],
        s, obs, count, from_one, from_two, planes, own_corners, rows_n, rows_s,
        ep, em, np_, nm, sink, local, inv, q, r, moves,
    )
    ep_h, em_h, np_h, nm_h, _, inv_h, q_h, r_h, s_h, *outs = outs
    middle, late_damp, solved, counts, join, send = outs
    sent_n, sent_s = both_ways(send)
    faces = ep, em, np_, nm
    halo_faces = ep_h, em_h, np_h, nm_h
    part, late, run, rise = call(
        inner_kernel,
        [block] + [own] * 3,
        [],
        *faces, *halo_faces, late_damp, middle, solved, counts, s, s_h,
        cost=pl.CostEstimate(flops=0, bytes_accessed=8 << 20, transcendentals=0),
    )
    adjoint, gradient = call(
        backward_kernel,
        [own] * 2,
        [ext, own, own, (2 * plane_count, 8, nx), pltpu.SemaphoreType.DMA((half // UNROLL, 4))],
        *faces, inv, q, r, *halo_faces, inv_h, q_h, r_h,
        middle, damp, solved, counts, join, part, late, run, rise, sent_n, sent_s,
        out_space=HBM,
    )
    return adjoint, gradient


def solution(mesh):
    block = P(None, "ty", "tx")
    plane = P("ty", "tx")
    return jax.shard_map(
        per_device,
        mesh=mesh,
        in_specs=(block,) * 7 + (plane,) * 3,
        out_specs=(block, block),
        check_vma=False,
    )
```

```python
import functools

import jax
import jax.numpy as jnp
from jax import lax
from jax.experimental import pallas as pl
from jax.experimental.pallas import tpu as pltpu
from jax.sharding import PartitionSpec as P

F32 = jnp.float32
VMEM = pl.BlockSpec(memory_space=pltpu.VMEM)
HBM = pl.BlockSpec(memory_space=pltpu.HBM)
UNROLL = 8
STEPS = 4
GROUP = 8
NAMES = ("s", "es", "ns", "mix", "relax", "vm", "obs")


def call(kernel, outs, scratch, *args, space=VMEM, out_space=VMEM, cost=None):
    def typed(x):
        return x if isinstance(x, jax.ShapeDtypeStruct) else jax.ShapeDtypeStruct(x, F32)

    return pl.pallas_call(
        kernel,
        out_shape=[typed(x) for x in outs],
        in_specs=[space] * len(args),
        out_specs=[out_space] * len(outs),
        scratch_shapes=[pltpu.VMEM(x, F32) if isinstance(x, tuple) else x for x in scratch],
        compiler_params=pltpu.CompilerParams(vmem_limit_bytes=16 << 20),
        cost_estimate=cost,
    )(*args)


def iota(shape, dim):
    return lax.broadcasted_iota(jnp.int32, shape, dim)


def roll(x, shift, axis):
    if isinstance(shift, int):
        shift = shift % x.shape[axis]
        if shift == 0:
            return x
    return pltpu.roll(x, shift, axis)


def odd_column():
    return lax.rem(lax.axis_index("tx"), 2) == 1


def level_of(ref, name, level):
    if name == "vm":
        level = jnp.minimum(level, ref.shape[0] - 1)
    return ref[level].astype(F32)


def edge_rows(block):
    return jnp.where(iota((8, block.shape[1]), 0) < 4, block[:8], block[-8:])


def sublane(shape):
    return iota(shape, 0)


def step_count(counts, axis):
    return jnp.minimum(counts, shift_up(counts, axis))


def pair_rows(first, second):
    sub = sublane(first.shape)
    return jnp.where((sub == 1) | (sub == 2), roll(second, 2, 0), first)


def level_pair(levels, t):
    return (t, t), (levels - 1 - t, levels - 2 - t)


def in_all_groups(x):
    group = iota(x.shape, 1) // GROUP
    out = jnp.zeros(x.shape, F32)
    for g in range(x.shape[1] // GROUP):
        out = jnp.where(group == g, roll(x, GROUP * g + 4, 1), out)
    return out


def pack_rows(get, counts, level):
    tile = {name: edge_rows(get(name)) for name in NAMES[:6]}
    s = tile["s"]
    sub = sublane(s.shape)
    open_north = level < step_count(counts, 0)
    fn = jnp.where(
        open_north,
        (0.5 * tile["ns"] + tile["mix"]) * s + (0.5 * tile["ns"] - tile["mix"]) * shift_up(s, 0),
        0.0,
    )
    sink = jnp.where(level < counts, tile["relax"], 0.0)
    inner = jnp.where(sub == 0, -fn, jnp.where(sub == 7, shift_down(fn, 0), 0.0))
    base = s - sink * jnp.tanh(s) + inner
    first = pair_rows(s, base)
    first = jnp.where((sub == 3) | (sub == 4), roll(tile["es"], 4, 0), first)
    first = jnp.where((sub == 5) | (sub == 6), roll(tile["mix"], 6, 0), first)
    return first, pair_rows(tile["vm"], tile["ns"])


def unpack_rows(first, second):
    return {
        "s": first,
        "base": roll(first, 6, 0),
        "es": roll(first, 4, 0),
        "mix": roll(first, 2, 0),
        "vm": second,
        "ns": roll(second, 6, 0),
    }


def two_levels(x, y):
    sub = sublane(x.shape)
    return jnp.where((sub >= 3) & (sub <= 6), roll(y, 4, 0), x)


def shift_up(x, axis):
    return roll(x, -1, axis)


def shift_down(x, axis):
    return roll(x, 1, axis)


def rim_kernel(*args):
    fields = args[:10]
    s, es, ns, mix, relax, vm, obs, count, *_ = kept = args[10:20]
    rows, corners, arrived = args[20:]
    copies = [pltpu.make_async_copy(fields[i], kept[i], arrived.at[i]) for i in range(10)]
    first = (7, 0, 1, 2, 3, 4, 5)
    rest = (6, 8, 9)
    for i in first + rest:
        copies[i].start()
    for i in first:
        copies[i].wait()
    refs = dict(zip(NAMES, (s, es, ns, mix, relax, vm, obs)))
    levels = s.shape[0]
    per_plane = 128 // GROUP
    small = (8, s.shape[2])
    group = iota(small, 1) // GROUP
    half = per_plane // 2
    plane_count = levels // per_plane
    counts = edge_rows(count[...].astype(F32))

    def rims(p, carry):
        acc = jnp.zeros(small, F32)
        late = jnp.zeros(small, F32)
        for g in range(half):
            t = p * half + g
            seconds = []
            for j, (k, link) in enumerate(level_pair(levels, t)):
                first, second = pack_rows(
                    lambda name: level_of(refs[name], name, link if name == "vm" else k),
                    counts,
                    k.astype(F32),
                )
                seconds.append(second)
                rows[2 * t + j] = first
                place = 2 * g + j
                acc = jnp.where(group == place, roll(first, GROUP * place + 4, 1), acc)
                late = jnp.where(group == place, roll(second, GROUP * place + 4, 1), late)
            rows[levels + t] = two_levels(*seconds)
        corners[p] = acc
        corners[plane_count + p] = late
        return carry

    lax.fori_loop(0, plane_count, rims, 0)
    rows[levels + levels // 2] = counts
    corners[2 * plane_count] = in_all_groups(counts)
    for p in range(2 * plane_count + 1, corners.shape[0]):
        corners[p] = jnp.zeros(small, F32)
    for i in rest:
        copies[i].wait()


def column_kernel(s, es, ns, mix, relax, vm, obs, count, planes):
    refs = dict(zip(NAMES, (s, es, ns, mix, relax, vm, obs)))
    levels = s.shape[0]
    per_plane = 128 // GROUP
    plane_count = levels // per_plane
    shape = s.shape[1:]
    group = iota(shape, 1) // GROUP

    def columns(p, carry):
        for a, name in enumerate(NAMES):
            acc = jnp.zeros(shape, F32)
            for g in range(per_plane):
                pair = level_pair(levels, p * (per_plane // 2) + g // 2)
                x = refs[name][pair[g % 2][name == "vm"]].astype(F32)
                acc = jnp.where(group == g, roll(x, GROUP * g + 4, 1), acc)
            planes[a * plane_count + p] = acc
        return carry

    lax.fori_loop(0, plane_count, columns, 0)
    total = len(NAMES) * plane_count
    planes[total] = in_all_groups(count[...].astype(F32))
    for p in range(total + 1, planes.shape[0]):
        planes[p] = jnp.zeros(shape, F32)


def merge_rows(north, south):
    return jnp.where(sublane(north.shape) % 2 == 0, north, south)


def halves_kernel(planes, corners_n, corners_s, one, two, kept):
    odd = odd_column()
    pairs = planes.shape[0] // 2
    ny = planes.shape[1]

    def put(place, x, y):
        low = iota(x.shape, 1) % GROUP < 4
        to_east = jnp.where(low, x, roll(y, 4, 1))
        to_west = jnp.where(low, roll(x, -4, 1), y)
        one[place] = jnp.where(odd, to_west, to_east)
        two[place] = jnp.where(odd, to_east, to_west)

    for h in range(pairs):
        put(pl.ds(h * ny, ny), planes[2 * h], planes[2 * h + 1])

    count = corners_n.shape[0]
    two[pl.ds(one.shape[0], 8)] = jnp.zeros((8, one.shape[1]), F32)

    def corner(p):
        return merge_rows(corners_n[p], corners_s[p])

    for h in range(count // 2):
        x, y = corner(2 * h), corner(2 * h + 1)
        kept[2 * h] = x
        kept[2 * h + 1] = y
        put(pl.ds(pairs * ny + h * 8, 8), x, y)


def halves(x):
    nx = x.shape[1] // 2
    return x[:, :nx], x[:, nx:]


def east(x):
    main, side = halves(x)
    lane = iota(main.shape, 1)
    return jnp.concatenate(
        [
            jnp.where(lane == lane.shape[1] - 1, side, roll(main, -1, 1)),
            jnp.where(lane == 0, main, roll(side, 1, 1)),
        ],
        axis=1,
    )


def west(x):
    main, side = halves(x)
    lane = iota(main.shape, 1)
    return jnp.concatenate(
        [
            jnp.where(lane == 0, side, roll(main, 1, 1)),
            jnp.where(lane == lane.shape[1] - 1, main, roll(side, -1, 1)),
        ],
        axis=1,
    )


def pull_x(main, side, ep, em, em_side):
    lane = iota(main.shape, 1)
    ge = jnp.where(lane == lane.shape[1] - 1, side, roll(main, -1, 1)) - main
    return ep * ge + jnp.where(lane == 0, em_side * (main - side), roll(em * ge, 1, 1)), ge


def extend(main, side, rows=None, corners=None):
    top = jnp.concatenate([main, side], axis=1)
    if rows is None:
        return top
    return jnp.concatenate([top, jnp.concatenate([rows, corners], axis=1)], axis=0)


def solve_inward(levels, get, inv_q, carries):
    half = levels // 2
    inv, q = inv_q

    def step(t, carry):
        new = []
        for k, last in ((t, carry[0]), (levels - 1 - t, carry[1])):
            c = get(k) * inv(k) + q(k) * last
            carries[k] = c
            new.append(c)
        return tuple(new)

    zero = jnp.zeros(carries.shape[1:], F32)
    return lax.fori_loop(0, half, step, (zero, zero), unroll=UNROLL)


def solve_outward(levels, ends, ratio, join, carries, use):
    half = levels // 2
    high, low = ends
    upper = (high + ratio(half - 1) * low) * join
    lower = (low + ratio(half) * high) * join

    def block(i, last):
        m = half // STEPS - 1 - i
        for u in range(STEPS - 1, -1, -1):
            t = m * STEPS + u
            new = []
            for k, x in ((t, last[0]), (levels - 1 - t, last[1])):
                new.append(carries[k] + ratio(k) * x)
            use(t, m, u, *new)
            last = tuple(new)
        return last

    lax.fori_loop(0, half // STEPS, block, (lower, upper), unroll=2)


def merge_halos(odd, from_one, from_two, planes, start):
    size = planes.shape[1]
    low = iota(planes.shape[1:], 1) % GROUP < 4
    for h in range(planes.shape[0] // 2):
        place = pl.ds(start + h * size, size)
        a, b = from_one[place], from_two[place]
        west = jnp.where(odd, a, b)
        east = jnp.where(odd, b, a)
        planes[2 * h] = jnp.where(low, west, roll(east, 4, 1))
        planes[2 * h + 1] = jnp.where(low, roll(west, -4, 1), east)


def part_of_pull(x, ep, em, damp):
    ge = east(x) - x
    return x * damp + ep * ge + west(em * ge), ge


def local_kernel(
    s, es, ns, mix, relax, vm, count, east, north, after,
    ep_out, em_out, np_out, nm_out, sink_out, damp_out, local_out, inv_out, q_out, r_out,
    moves_out,
):
    levels, ny, nx = s.shape
    half = levels // 2
    counts = count[...].astype(F32)
    east_count = east[...].astype(F32)
    north_count = north[...].astype(F32)
    lane = iota((ny, nx), 1)
    sub = sublane((ny, nx))

    def prepare(k):
        level = k.astype(F32)
        state = s[k]
        diffusion = mix[k].astype(F32)
        speed_east = 0.5 * es[k].astype(F32)
        speed_north = 0.5 * ns[k].astype(F32)
        open_east = level < east_count
        open_north = level < north_count
        ep = jnp.where(open_east, speed_east + diffusion, 0.0)
        em = jnp.where(open_east, speed_east - diffusion, 0.0)
        np_ = jnp.where(open_north, speed_north + diffusion, 0.0)
        nm = jnp.where(open_north, speed_north - diffusion, 0.0)
        sink = jnp.where(level < counts, relax[k].astype(F32), 0.0)
        squeeze = jnp.tanh(state)
        ep_out[k] = ep
        em_out[k] = em
        np_out[k] = np_
        nm_out[k] = nm
        sink_out[k] = sink
        damp_out[k] = 1.0 - sink * (1.0 - squeeze * squeeze)
        fe = ep * state + em * shift_up(state, 1)
        fe = jnp.where(lane == nx - 1, 0.0, fe)
        fn = np_ * state + nm * jnp.where(sub == ny - 1, 0.0, shift_up(state, 0))
        flow = fe - shift_down(fe, 1)
        flow = flow + (fn - jnp.where(sub == 0, 0.0, shift_down(fn, 0)))
        local_out[k] = state - sink * squeeze - flow

    def factor(t, carry):
        new = []
        for (k, link_level), (ratio, outer) in zip(level_pair(levels, t), carry):
            prepare(k)
            link = jnp.where(
                link_level.astype(F32) + 1.0 < counts, vm[link_level].astype(F32), 0.0
            )
            inv = 1.0 / (1.0 + outer + link - outer * ratio)
            ratio = link * inv
            inv_out[k] = inv
            q_out[k] = outer * inv
            r_out[k] = ratio
            new.append((ratio, link))
        return tuple(new)

    zero = jnp.zeros((ny, nx), F32)
    lax.fori_loop(0, half, factor, ((zero, zero), (zero, zero)), unroll=UNROLL)

    source = iota((2 * nx, 2 * nx), 0) % nx
    target = iota((2 * nx, 2 * nx), 1)
    for u in range(STEPS):
        group = 2 * u + target // nx
        lane = target % nx
        column = jnp.where(lane < 4, 3 - lane, jnp.where(lane >= nx - 4, nx + 3 - lane, -nx))
        hit = source == GROUP * group + column
        moves_out[u] = jnp.where(hit, 1.0, 0.0).astype(jnp.bfloat16)


def whole(own, halo):
    ny = own.shape[0]
    return extend(own, halo[:ny], halo[ny + 8 :], halo[ny : ny + 8])


def forward_kernel(
    s, obs, count, from_one, from_two, own_planes, own_corners, rows_n, rows_s,
    ep, em, np_, nm, sink, local, inv, q, r, moves,
    ep_halo, em_halo, np_halo, nm_halo, sink_halo, inv_halo, q_halo, r_halo, s_halo,
    middle_out, damp_out, solved_out, counts_out, join_out, send,
    planes, corners, rhs, carries, packed, moved, moved_rows, sides,
):
    levels, ny, nx = s.shape
    half = levels // 2
    per_plane = 128 // GROUP
    plane_count = levels // per_plane
    odd = odd_column()
    merge_halos(odd, from_one, from_two, planes, 0)
    merge_halos(odd, from_one, from_two, corners, planes.shape[0] // 2 * planes.shape[1])

    def rim(index):
        return merge_rows(rows_n[index], rows_s[index])

    count_plane = len(NAMES) * plane_count
    side_counts = jnp.dot(
        jnp.concatenate([planes[count_plane]] + [corners[2 * plane_count]] * 2, axis=0).astype(
            jnp.bfloat16
        ),
        moves[0, :nx, :nx],
        preferred_element_type=F32,
    )
    count_ext = extend(
        count[...].astype(F32),
        side_counts[:ny],
        rim(levels + half),
        side_counts[ny : ny + 8],
    )
    east_ext = jnp.minimum(count_ext, east(count_ext))
    counts_out[0] = count_ext
    counts_out[1] = east_ext
    counts_out[2] = step_count(count_ext, 0)
    count_halo = jnp.concatenate(
        [count_ext[:ny, nx:], count_ext[ny:, nx:], count_ext[ny:, :nx]], axis=0
    )
    small_sub = sublane((8, nx))
    east_rows = east_ext[ny:, :nx]
    north_rows = jnp.where(small_sub == 7, counts_out[2, ny:, :nx], 0.0)
    lane = iota((ny, nx), 1)
    per_half = per_plane // 2

    strip = (ny + 8, nx)
    place = iota(strip, 1) % GROUP
    low = place < 4
    groups = iota(strip, 1) // GROUP
    from_top = groups % 2 == 0
    strip_sub = sublane(strip)

    def columns(p, carry):
        t = p * per_half + groups // 2
        level = jnp.where(from_top, t, levels - 1 - t).astype(F32)
        link_level = jnp.where(from_top, t, levels - 2 - t).astype(F32)

        def side_and_corner(a, c):
            return jnp.concatenate([a, c], axis=0)

        def strips(west):
            def pick(halo, own):
                near_side = low[: halo.shape[0]]
                return jnp.where(near_side, halo, own) if west else jnp.where(near_side, own, halo)

            x = unpack_rows(
                pick(corners[p], own_corners[p]),
                pick(corners[plane_count + p], own_corners[plane_count + p]),
            )
            side = {}
            for a, name in enumerate(NAMES[:6]):
                at = a * plane_count + p
                side[name] = pick(planes[at], own_planes[at])
            for name in NAMES[:4] + NAMES[5:6]:
                x[name] = side_and_corner(side[name], x[name])
            counts = side_and_corner(
                pick(planes[count_plane], own_planes[count_plane]),
                pick(corners[2 * plane_count], own_corners[2 * plane_count]),
            )
            state = x["s"]
            open_east = level < step_count(counts, 1)
            open_north = (level < step_count(counts, 0)) & (
                (strip_sub < ny) | (strip_sub == ny + 7)
            )
            ep_s = jnp.where(open_east, 0.5 * x["es"] + x["mix"], 0.0)
            em_s = jnp.where(open_east, 0.5 * x["es"] - x["mix"], 0.0)
            np_s = jnp.where(open_north, 0.5 * x["ns"] + x["mix"], 0.0)
            nm_s = jnp.where(open_north, 0.5 * x["ns"] - x["mix"], 0.0)
            sink_s = jnp.where(level[:ny] < counts[:ny], side["relax"], 0.0)
            link = jnp.where(link_level + 1.0 < counts, x["vm"], 0.0)
            fe = ep_s * state + em_s * shift_up(state, 1)
            fe_west = shift_down(fe, 1)
            fn = np_s * state + nm_s * shift_up(state, 0)
            base = side_and_corner(side["s"] - sink_s * jnp.tanh(side["s"]), x["base"])
            right = base - (fe - fe_west) - (fn - shift_down(fn, 0))
            return (right, link, np_s, nm_s, ep_s, em_s, sink_s, state), fe, fe_west

        western, through_west, _ = strips(True)
        eastern, _, through_east = strips(False)
        seam = jnp.where(place == 3, through_west, through_east)
        both = [jnp.where(low[: a.shape[0]], a, b) for a, b in zip(western, eastern)]
        right, link, np_c, nm_c = (x[ny:] for x in both[:4])
        corner = pair_rows(right, link)
        corner = jnp.where((small_sub == 3) | (small_sub == 4), roll(seam[ny:], 4, 0), corner)
        corner = jnp.where(small_sub == 5, roll(np_c, 6, 0), corner)
        corner = jnp.where(small_sub == 6, roll(nm_c, 7, 0), corner)
        both = [x[:ny] for x in both]
        seen = planes[NAMES.index("obs") * plane_count + p]
        both = both[:2] + [seam[:ny], seen] + both[2:] + [jnp.concatenate([corner] * 2, axis=0)]
        for i, x in enumerate(both):
            split(p, i * ny, x)
        return carry

    def split(p, at, x):
        for h, y in enumerate((x, roll(x, nx // 2, 1))):
            high = y.astype(jnp.bfloat16)
            packed[2 * p + h, at : at + ny, :nx] = high
            packed[2 * p + h, at : at + ny, nx:] = (y - high.astype(F32)).astype(jnp.bfloat16)

    lax.fori_loop(0, plane_count, columns, 0, unroll=plane_count)

    def unpack(u):
        move = moves[u]

        def place_both(m, carry):
            out = jnp.dot(packed[m], move, preferred_element_type=F32)
            t = m * STEPS + u
            for j, k in enumerate((t, levels - 1 - t)):
                x = out[:, j * nx : (j + 1) * nx]
                np_x, nm_x, ep_x, em_x, sink_x, s_x, corner = (
                    x[i * ny : (i + 1) * ny] for i in range(4, 11)
                )
                corner = corner[:8]
                moved[k] = x[: 4 * ny]
                moved_rows[k] = corner
                ep_halo[k, :ny] = ep_x
                em_halo[k, :ny] = em_x
                np_halo[k, :ny] = np_x
                nm_halo[k, :ny] = nm_x
                np_halo[k, ny : ny + 8] = roll(corner, 2, 0)
                nm_halo[k, ny : ny + 8] = roll(corner, 1, 0)
                sink_halo[k] = sink_x
                s_halo[k, :ny] = s_x
            return carry

        lax.fori_loop(0, 2 * plane_count, place_both, 0, unroll=2 * plane_count)

    for u in range(STEPS):
        unpack(u)

    def prepare(m, u, j, k, link_level, second):
        t = m * STEPS + u
        x = unpack_rows(rim(2 * t + j), roll(second, 4, 0) if j else second)
        level = k.astype(F32)
        row = x["s"]
        open_east = level < east_rows
        open_north = level < north_rows
        ep_r = jnp.where(open_east, 0.5 * x["es"] + x["mix"], 0.0)
        em_r = jnp.where(open_east, 0.5 * x["es"] - x["mix"], 0.0)
        np_r = jnp.where(open_north, 0.5 * x["ns"] + x["mix"], 0.0)
        nm_r = jnp.where(open_north, 0.5 * x["ns"] - x["mix"], 0.0)
        link_r = jnp.where(link_level.astype(F32) + 1.0 < count_halo[ny + 8 :], x["vm"], 0.0)
        corner = moved_rows[k]
        right, link, seam = (moved[k, i * ny : (i + 1) * ny] for i in range(3))
        seam_rows = roll(corner, 4, 0)
        np_halo[k, ny + 8 :] = np_r
        nm_halo[k, ny + 8 :] = nm_r
        s_halo[k, ny + 8 :] = row

        own = s[k]
        last, first = lane == nx - 1, lane == 0
        fe = ep_r * row + em_r * shift_up(row, 1)
        flow = jnp.where(last[:8], seam_rows, fe) - jnp.where(
            first[:8], seam_rows, shift_down(fe, 1)
        )
        fn = np_r * row + nm_r * shift_up(own[:8], 0)
        top = np_[k, ny - 8 :] * own[ny - 8 :]
        cross = nm[k, ny - 8 :] * shift_up(row, 0)
        from_block = jnp.where(small_sub == 0, shift_down(top + cross, 0), 0.0)
        right_r = x["base"] - flow - (fn - from_block)

        inner = local[k] + jnp.where(first, seam, jnp.where(last, -seam, 0.0))
        low_rows = inner[:8] + jnp.where(small_sub == 0, shift_down(fn, 0), 0.0)
        high_rows = inner[ny - 8 :] - jnp.where(small_sub == 7, cross, 0.0)
        between = [inner[8 : ny - 8]] if ny > 16 else []
        inner = jnp.concatenate([low_rows] + between + [high_rows], axis=0)
        halo = jnp.concatenate([right, corner, right_r], axis=0)
        return inner, halo, jnp.concatenate([link, roll(corner, 6, 0), link_r], axis=0)

    def factor(m, carry):
        for u in range(STEPS):
            carry = factor_step(m, u, carry)
        return carry

    def factor_step(m, u, carry):
        t = m * STEPS + u
        second = rim(levels + t)
        new = []
        for j, (k, link_level) in enumerate(level_pair(levels, t)):
            ratio, c_own, c_halo, outer = carry[j]
            own, halo, link = prepare(m, u, j, k, link_level, second)
            inv_h = 1.0 / (1.0 + outer + link - outer * ratio)
            q_h = outer * inv_h
            ratio = link * inv_h
            c_own = own * inv[k] + q[k] * c_own
            c_halo = halo * inv_h + q_h * c_halo
            inv_halo[k] = inv_h
            q_halo[k] = q_h
            r_halo[k] = ratio
            carries[k] = whole(c_own, c_halo)
            new.append((ratio, c_own, c_halo, link))
        return tuple(new)

    zero = jnp.zeros(count_halo.shape, F32)
    begin = (zero, jnp.zeros((ny, nx), F32), zero, zero)
    (r_top, top_own, top_halo, _), (r_low, low_own, low_halo, _) = lax.fori_loop(
        0, half // STEPS, factor, (begin, begin), unroll=2
    )
    c_top, c_low = whole(top_own, top_halo), whole(low_own, low_halo)
    join = 1.0 / (1.0 - whole(r[half - 1], r_top) * whole(r[half], r_low))
    join_out[...] = join

    def ext(own, halo):
        return lambda k: whole(own[k], halo[k])

    def inner(own, halo):
        return lambda k: extend(own[k], halo[k, :ny])

    def spread(state, ep, em, np_, nm):
        fe = ep * state + em * east(state)
        fn = np_ * state + nm * shift_up(state, 0)
        return (fe - west(fe)) + (fn - shift_down(fn, 0))

    def both(one):
        def use(t, m, u, top, low):
            one(t, top, m, u, 0)
            one(levels - 1 - t, low, m, u, 1)

        return use

    def to_second(k, x, m, u, j):
        middle_out[k] = x
        state = x[:ny]
        squeeze = jnp.tanh(state)
        loss = inner(sink, sink_halo)(k)
        damp_out[k] = 1.0 - loss * (1.0 - squeeze * squeeze)
        fields = (ext(ep, ep_halo), ext(em, em_halo), ext(np_, np_halo), ext(nm, nm_halo))
        flow = spread(x, *(field(k) for field in fields))
        rhs[k] = state - flow[:ny] - loss * squeeze

    solve_outward(levels, (c_top, c_low), ext(r, r_halo), join, carries, both(to_second))

    main = carries.at[:, :ny]
    inv_q = inner(inv, inv_halo), inner(q, q_halo)
    ratio = inner(r, r_halo)
    ends = solve_inward(levels, lambda k: rhs[k], inv_q, main)

    def to_adjoint(k, x, m, u, j):
        seen = extend(obs[k].astype(F32), moved[k, 3 * ny :])
        rhs[k] = jnp.where(k.astype(F32) < count_ext[:ny], x - seen, 0.0)

    solve_outward(levels, ends, ratio, join[:ny], main, both(to_adjoint))
    ends = solve_inward(levels, lambda k: rhs[k], inv_q, main)

    def rim_part(k, solved):
        solved_out[k] = solved
        x = edge_rows(solved)
        main, side = halves(x)
        rows_of = lambda ref: edge_rows(ref[k])
        part, _ = pull_x(main, side, rows_of(ep), rows_of(em), edge_rows(em_halo[k, :ny]))
        part = part + main * edge_rows(damp_out[k, :, :nx])
        gn = shift_up(main, 0) - main
        sub = sublane(main.shape)
        part = part + jnp.where(
            sub == 0,
            rows_of(np_) * gn,
            jnp.where(sub == 7, shift_down(rows_of(nm) * gn, 0), 0.0),
        )
        return jnp.concatenate([pair_rows(main, part), side], axis=1)

    group = iota((8, nx), 1) // GROUP

    def to_send(t, m, u, top, low):
        pair = two_levels(rim_part(t, top), rim_part(levels - 1 - t, low))
        send[t] = pair[:, :nx]
        before = jnp.zeros((8, nx), F32) if u == STEPS - 1 else sides[m]
        moved = roll(pair[:, nx:], 2 * GROUP * u + 4, 1)
        sides[m] = jnp.where(group == 2 * u, moved, before)

    solve_outward(levels, ends, ratio, join[:ny], main, to_send)
    for p in range(half // 8):
        send[half + p] = jnp.where(group % 2 == 0, sides[2 * p], roll(sides[2 * p + 1], GROUP, 1))


def inner_kernel(
    ep, em, np_, nm, ep_halo, em_halo, np_halo, nm_halo, damp, middle, solved, counts,
    s, s_halo, part_out, late_out, run_out, rise_out,
):
    levels, ny, width = solved.shape
    nx = width // 2
    sub = sublane((ny, width))
    inside = sub < ny - 1

    def inner(k, carry):
        x = solved[k]
        state = middle[k]
        field = lambda own, halo: extend(own[k], halo[k, :ny])
        part, ge = part_of_pull(x, field(ep, ep_halo), field(em, em_halo), damp[k])
        gn = jnp.where(inside, shift_up(x, 0) - x, 0.0)
        part_out[k] = (
            part + field(np_, np_halo) * gn + shift_down(field(nm, nm_halo) * gn, 0)
        )
        level = k.astype(F32)
        open_east = level < counts[1, :ny, :nx]
        open_north = level < counts[2, :ny, :nx]

        def slopes(state):
            run = (east(state[:ny]) - state[:ny])[:, :nx]
            rise = shift_up(state[:, :nx], 0)[:ny] - state[:ny, :nx]
            return jnp.where(open_east, run, 0.0), jnp.where(open_north, rise, 0.0)

        run, rise = slopes(state)
        late_out[k] = ge[:, :nx] * run + gn[:, :nx] * rise
        run_out[k], rise_out[k] = slopes(whole(s[k], s_halo[k]))
        return carry

    lax.fori_loop(0, levels, inner, 0, unroll=UNROLL)


def backward_kernel(
    ep, em, np_, nm, inv, q, r, ep_halo, em_halo, np_halo, nm_halo, inv_halo, q_halo, r_halo,
    middle, damp, solved, counts, join, part, late, run, rise, rows_n, rows_s,
    adjoint_out, gradient_out, carries, adjoint, gradient, sides, sent,
):
    levels, ny, width = solved.shape
    nx = width // 2
    half = levels // 2
    sub = sublane((8, width))

    for p in range(half // 8):
        side = merge_rows(rows_n[half + p], rows_s[half + p])
        sides[2 * p] = side
        sides[2 * p + 1] = roll(side, -GROUP, 1)

    def rims(m, u):
        t = m * STEPS + u
        line = merge_rows(rows_n[t], rows_s[t])
        corner = roll(sides[m], 124 - 2 * GROUP * u, 1)
        both = jnp.concatenate([line, corner], axis=1)
        return both, roll(both, 4, 0)

    def across(k, rim):
        inner = part[k]
        near_part = roll(rim, 6, 0)
        south = solved[k, :8] - shift_down(rim, 0)
        north = shift_up(rim, 0) - solved[k, ny - 8 :]
        north_plus = whole(np_[k], np_halo[k])
        north_minus = whole(nm[k], nm_halo[k])
        np_rim, nm_rim = north_plus[ny:], north_minus[ny:]
        np_top, nm_top = north_plus[ny - 8 : ny], north_minus[ny - 8 : ny]
        low = inner[:8] + jnp.where(sub == 0, shift_down(nm_rim, 0) * south, 0.0)
        high = inner[ny - 8 :] + jnp.where(sub == 7, np_top * north, 0.0)
        outer = near_part + jnp.where(
            sub == 0, shift_down(nm_top * north, 0), np_rim * shift_up(south, 0)
        )
        rise = (shift_up(middle[k, ny:], 0) - middle[k, ny - 8 : ny])[:, :nx]
        open_north = (sub[:, :nx] == 7) & (k.astype(F32) < counts[2, ny - 8 : ny, :nx])
        extra = jnp.where(open_north, north[:, :nx] * rise, 0.0)
        gradient[k, : ny - 8] = late[k, : ny - 8]
        gradient[k, ny - 8 :] = late[k, ny - 8 :] + extra
        middle_rows = [inner[8 : ny - 8]] if ny > 16 else []
        return jnp.concatenate([low, *middle_rows, high, outer], axis=0)

    def late_steps(m, carry):
        for u in range(STEPS):
            t = m * STEPS + u
            new = []
            for k, rim, last in zip((t, levels - 1 - t), rims(m, u), carry):
                c = across(k, rim) * whole(inv[k], inv_halo[k])
                c = c + whole(q[k], q_halo[k]) * last
                carries[k] = c
                new.append(c)
            carry = tuple(new)
        return carry

    zero = jnp.zeros(carries.shape[1:], F32)
    ends = lax.fori_loop(0, half // STEPS, late_steps, (zero, zero), unroll=2)

    def early(k, x):
        main, side = halves(x[:ny])
        flow, ge = pull_x(main, side, ep[k], em[k], em_halo[k, :ny])
        result = main * damp[k] + flow
        column = x[:, :nx]
        gn = shift_up(column, 0) - column
        minus = jnp.concatenate([nm[k], nm_halo[k, ny + 8 :]], axis=0)
        result = result + np_[k] * gn[:ny] + shift_down(minus * gn, 0)[:ny]
        adjoint[k] = result
        gradient[k] = -(gradient[k] + ge * run[k] + gn[:ny] * rise[k])

    def copies(p):
        out = []
        for i, begin in enumerate((p * UNROLL, levels - (p + 1) * UNROLL)):
            place = pl.ds(begin, UNROLL)
            for j, (source, target) in enumerate(
                ((adjoint, adjoint_out), (gradient, gradient_out))
            ):
                out.append(
                    pltpu.make_async_copy(
                        source.at[place], target.at[place], sent.at[p, 2 * i + j]
                    )
                )
        return out

    high, low = ends
    steps = half // UNROLL
    ratio = lambda k: whole(r[k], r_halo[k])
    last = (low + ratio(half) * high) * join[...], (high + ratio(half - 1) * low) * join[...]

    def block(i, last):
        p = steps - 1 - i
        for g in range(UNROLL - 1, -1, -1):
            t = p * UNROLL + g
            new = []
            for k, x in ((t, last[0]), (levels - 1 - t, last[1])):
                x = carries[k] + ratio(k) * x
                early(k, x)
                new.append(x)
            last = tuple(new)
        for copy in copies(p):
            copy.start()
        return last

    lax.fori_loop(0, steps, block, last)
    for p in range(steps):
        for copy in copies(p):
            copy.wait()


def ring(axis, distance):
    count = lax.axis_size(axis)
    return [(i, (i + distance) % count) for i in range(count)]


def both_ways(x):
    from_north = lax.ppermute(x, "ty", ring("ty", -1))
    if lax.axis_size("ty") == 2:
        return from_north, from_north
    return from_north, lax.ppermute(x, "ty", ring("ty", 1))


def swap(x, phase):
    nx = lax.axis_size("tx")
    return lax.ppermute(
        x, "tx", [(i, (i + 1) % nx if i % 2 == phase else (i - 1) % nx) for i in range(nx)]
    )


def per_device(
    tracer_start,
    observed,
    east_speed,
    north_speed,
    mixing,
    vertical_mixing,
    relax_rate,
    level_count,
    face_east,
    face_north,
):
    levels, ny, nx = tracer_start.shape
    per_plane = 128 // GROUP
    plane_count = levels // per_plane
    pairs = (len(NAMES) * plane_count + 2) // 2
    fields = (
        tracer_start, east_speed, north_speed, mixing, relax_rate, vertical_mixing, observed,
        level_count, face_east, face_north,
    )
    half = levels // 2
    corner_planes = 2 * plane_count + 2
    *fields, rows, corners = call(
        rim_kernel,
        [jax.ShapeDtypeStruct(x.shape, x.dtype) for x in fields]
        + [(levels + half + 1, 8, nx), (corner_planes, 8, nx)],
        [pltpu.SemaphoreType.DMA((10,))],
        *[pltpu.with_memory_space_constraint(x, pltpu.HBM) for x in fields],
        space=HBM,
    )
    corners_n, corners_s = both_ways(corners)
    rows_n, rows_s = both_ways(rows)
    (planes,) = call(column_kernel, [(2 * pairs, ny, nx)], [], *fields[:8])
    packed = (pairs * ny + corner_planes // 2 * 8, nx)
    one, two, own_corners = call(
        halves_kernel, [packed, (packed[0] + 8, nx), corners.shape], [],
        planes, corners_n, corners_s,
        cost=pl.CostEstimate(flops=10**10, bytes_accessed=0, transcendentals=0),
    )
    from_two = swap(two, 1)
    from_one = swap(one, 0)
    ext = (levels, ny + 8, 2 * nx)
    block = (levels, ny, 2 * nx)
    own = (levels, ny, nx)
    halo = (levels, ny + 16, nx)
    s, es, ns, mix, relax, vm, obs, count, east, north = fields
    *coefficients, damp, local, inv, q, r, moves = call(
        local_kernel,
        [own] * 10 + [jax.ShapeDtypeStruct((STEPS, 2 * nx, 2 * nx), jnp.bfloat16)],
        [],
        s, es, ns, mix, relax, vm, count, east, north, one,
        cost=pl.CostEstimate(flops=10**9, bytes_accessed=0, transcendentals=0),
    )
    ep, em, np_, nm, sink = coefficients
    outs = call(
        forward_kernel,
        [halo] * 4 + [own] + [halo] * 4 + [ext, block, block, (3,) + ext[1:], ext[1:]]
        + [(half + half // 8, 8, nx)],
        [
            planes.shape,
            corners.shape,
            block,
            ext,
            pltpu.VMEM((2 * plane_count, 11 * ny, 2 * nx), jnp.bfloat16),
            (levels, 4 * ny, nx),
            (levels, 8, nx),
            (2 * plane_count, 8, nx),
        ],
        s, obs, count, from_one, from_two, planes, own_corners, rows_n, rows_s,
        ep, em, np_, nm, sink, local, inv, q, r, moves,
    )
    ep_h, em_h, np_h, nm_h, _, inv_h, q_h, r_h, s_h, *outs = outs
    middle, late_damp, solved, counts, join, send = outs
    sent_n, sent_s = both_ways(send)
    faces = ep, em, np_, nm
    halo_faces = ep_h, em_h, np_h, nm_h
    part, late, run, rise = call(
        inner_kernel,
        [block] + [own] * 3,
        [],
        *faces, *halo_faces, late_damp, middle, solved, counts, s, s_h,
        cost=pl.CostEstimate(flops=0, bytes_accessed=8 << 20, transcendentals=0),
    )
    adjoint, gradient = call(
        backward_kernel,
        [own] * 2,
        [ext, own, own, (2 * plane_count, 8, nx), pltpu.SemaphoreType.DMA((half // UNROLL, 4))],
        *faces, inv, q, r, *halo_faces, inv_h, q_h, r_h,
        middle, damp, solved, counts, join, part, late, run, rise, sent_n, sent_s,
        out_space=HBM,
    )
    return adjoint, gradient


def solution(mesh):
    block = P(None, "ty", "tx")
    plane = P("ty", "tx")
    return jax.shard_map(
        per_device,
        mesh=mesh,
        in_specs=(block,) * 7 + (plane,) * 3,
        out_specs=(block, block),
        check_vma=False,
    )
```

```python
import functools

import jax
import jax.numpy as jnp
from jax import lax
from jax.experimental import pallas as pl
from jax.experimental.pallas import tpu as pltpu
from jax.sharding import PartitionSpec as P

F32 = jnp.float32
VMEM = pl.BlockSpec(memory_space=pltpu.VMEM)
HBM = pl.BlockSpec(memory_space=pltpu.HBM)
UNROLL = 8
STEPS = 4
GROUP = 8
NAMES = ("s", "es", "ns", "mix", "relax", "vm", "obs")


def call(kernel, outs, scratch, *args, space=VMEM, out_space=VMEM, cost=None):
    def typed(x):
        return x if isinstance(x, jax.ShapeDtypeStruct) else jax.ShapeDtypeStruct(x, F32)

    return pl.pallas_call(
        kernel,
        out_shape=[typed(x) for x in outs],
        in_specs=[space] * len(args),
        out_specs=[out_space] * len(outs),
        scratch_shapes=[pltpu.VMEM(x, F32) if isinstance(x, tuple) else x for x in scratch],
        compiler_params=pltpu.CompilerParams(vmem_limit_bytes=16 << 20),
        cost_estimate=cost,
    )(*args)


def iota(shape, dim):
    return lax.broadcasted_iota(jnp.int32, shape, dim)


def roll(x, shift, axis):
    if isinstance(shift, int):
        shift = shift % x.shape[axis]
        if shift == 0:
            return x
    return pltpu.roll(x, shift, axis)


def odd_column():
    return lax.rem(lax.axis_index("tx"), 2) == 1


def level_of(ref, name, level):
    if name == "vm":
        level = jnp.minimum(level, ref.shape[0] - 1)
    return ref[level].astype(F32)


def edge_rows(block):
    return jnp.where(iota((8, block.shape[1]), 0) < 4, block[:8], block[-8:])


def sublane(shape):
    return iota(shape, 0)


def step_count(counts, axis):
    return jnp.minimum(counts, shift_up(counts, axis))


def pair_rows(first, second):
    sub = sublane(first.shape)
    return jnp.where((sub == 1) | (sub == 2), roll(second, 2, 0), first)


def level_pair(levels, t):
    return (t, t), (levels - 1 - t, levels - 2 - t)


def in_all_groups(x):
    group = iota(x.shape, 1) // GROUP
    out = jnp.zeros(x.shape, F32)
    for g in range(x.shape[1] // GROUP):
        out = jnp.where(group == g, roll(x, GROUP * g + 4, 1), out)
    return out


def pack_rows(get, counts, level):
    tile = {name: edge_rows(get(name)) for name in NAMES[:6]}
    s = tile["s"]
    sub = sublane(s.shape)
    open_north = level < step_count(counts, 0)
    fn = jnp.where(
        open_north,
        (0.5 * tile["ns"] + tile["mix"]) * s + (0.5 * tile["ns"] - tile["mix"]) * shift_up(s, 0),
        0.0,
    )
    sink = jnp.where(level < counts, tile["relax"], 0.0)
    inner = jnp.where(sub == 0, -fn, jnp.where(sub == 7, shift_down(fn, 0), 0.0))
    base = s - sink * jnp.tanh(s) + inner
    first = pair_rows(s, base)
    first = jnp.where((sub == 3) | (sub == 4), roll(tile["es"], 4, 0), first)
    first = jnp.where((sub == 5) | (sub == 6), roll(tile["mix"], 6, 0), first)
    return first, pair_rows(tile["vm"], tile["ns"])


def unpack_rows(first, second):
    return {
        "s": first,
        "base": roll(first, 6, 0),
        "es": roll(first, 4, 0),
        "mix": roll(first, 2, 0),
        "vm": second,
        "ns": roll(second, 6, 0),
    }


def two_levels(x, y):
    sub = sublane(x.shape)
    return jnp.where((sub >= 3) & (sub <= 6), roll(y, 4, 0), x)


def shift_up(x, axis):
    return roll(x, -1, axis)


def shift_down(x, axis):
    return roll(x, 1, axis)


def rim_kernel(*args):
    fields = args[:10]
    s, es, ns, mix, relax, vm, obs, count, *_ = kept = args[10:20]
    rows, corners, arrived = args[20:]
    copies = [pltpu.make_async_copy(fields[i], kept[i], arrived.at[i]) for i in range(10)]
    first = (7, 0, 1, 2, 3, 4, 5)
    rest = (6, 8, 9)
    for i in first + rest:
        copies[i].start()
    for i in first:
        copies[i].wait()
    refs = dict(zip(NAMES, (s, es, ns, mix, relax, vm, obs)))
    levels = s.shape[0]
    per_plane = 128 // GROUP
    small = (8, s.shape[2])
    group = iota(small, 1) // GROUP
    half = per_plane // 2
    plane_count = levels // per_plane
    counts = edge_rows(count[...].astype(F32))
    sub = sublane(small)

    def rims(p, carry):
        acc = jnp.zeros(small, F32)
        late = jnp.zeros(small, F32)
        for g in range(half):
            t = p * half + g
            seconds = []
            for j, (k, link) in enumerate(level_pair(levels, t)):
                first, second = pack_rows(
                    lambda name: level_of(refs[name], name, link if name == "vm" else k),
                    counts,
                    k.astype(F32),
                )
                seconds.append(second)
                rows[2 * t + j] = first
                place = 2 * g + j
                acc = jnp.where(group == place, roll(first, GROUP * place + 4, 1), acc)
                second = jnp.where((sub == 3) | (sub == 4), roll(counts, 4, 0), second)
                late = jnp.where(group == place, roll(second, GROUP * place + 4, 1), late)
            rows[levels + t] = two_levels(*seconds)
        corners[p] = acc
        corners[plane_count + p] = late
        return carry

    lax.fori_loop(0, plane_count, rims, 0)
    rows[levels + levels // 2] = counts
    for i in rest:
        copies[i].wait()


def column_kernel(s, es, ns, mix, relax, vm, obs, count, planes):
    refs = dict(zip(NAMES, (s, es, ns, mix, relax, vm, obs)))
    levels = s.shape[0]
    per_plane = 128 // GROUP
    plane_count = levels // per_plane
    shape = s.shape[1:]
    group = iota(shape, 1) // GROUP

    place = iota(shape, 1) % GROUP

    def columns(p, carry):
        packed = []
        for name in NAMES:
            acc = jnp.zeros(shape, F32)
            for g in range(per_plane):
                pair = level_pair(levels, p * (per_plane // 2) + g // 2)
                x = refs[name][pair[g % 2][name == "vm"]].astype(F32)
                acc = jnp.where(group == g, roll(x, GROUP * g + 4, 1), acc)
            packed.append(acc)
        seen = packed.pop()
        for name, distance in (("ns", 2), ("relax", 3)):
            i = NAMES.index(name)
            x = jnp.where(place == 0, roll(seen, -distance, 1), packed[i])
            packed[i] = jnp.where(place == GROUP - 1, roll(seen, distance, 1), x)
        for a, x in enumerate(packed):
            planes[a * plane_count + p] = x
        return carry

    lax.fori_loop(0, plane_count, columns, 0)
    total = len(NAMES[:6]) * plane_count
    planes[total] = in_all_groups(count[...].astype(F32))
    for p in range(total + 1, planes.shape[0]):
        planes[p] = jnp.zeros(shape, F32)


def merge_rows(north, south):
    return jnp.where(sublane(north.shape) % 2 == 0, north, south)


def halves_kernel(planes, corners_n, corners_s, one, two, kept):
    odd = odd_column()
    pairs = planes.shape[0] // 2
    ny = planes.shape[1]

    def put(place, x, y):
        low = iota(x.shape, 1) % GROUP < 4
        to_east = jnp.where(low, x, roll(y, 4, 1))
        to_west = jnp.where(low, roll(x, -4, 1), y)
        one[place] = jnp.where(odd, to_west, to_east)
        two[place] = jnp.where(odd, to_east, to_west)

    for h in range(pairs):
        put(pl.ds(h * ny, ny), planes[2 * h], planes[2 * h + 1])

    count = corners_n.shape[0]
    def corner(p):
        return merge_rows(corners_n[p], corners_s[p])

    for h in range(count // 2):
        x, y = corner(2 * h), corner(2 * h + 1)
        kept[2 * h] = x
        kept[2 * h + 1] = y
        put(pl.ds(pairs * ny + h * 8, 8), x, y)


def halves(x):
    nx = x.shape[1] // 2
    return x[:, :nx], x[:, nx:]


def east(x):
    main, side = halves(x)
    lane = iota(main.shape, 1)
    return jnp.concatenate(
        [
            jnp.where(lane == lane.shape[1] - 1, side, roll(main, -1, 1)),
            jnp.where(lane == 0, main, roll(side, 1, 1)),
        ],
        axis=1,
    )


def west(x):
    main, side = halves(x)
    lane = iota(main.shape, 1)
    return jnp.concatenate(
        [
            jnp.where(lane == 0, side, roll(main, 1, 1)),
            jnp.where(lane == lane.shape[1] - 1, main, roll(side, -1, 1)),
        ],
        axis=1,
    )


def pull_x(main, side, ep, em, em_side):
    lane = iota(main.shape, 1)
    ge = jnp.where(lane == lane.shape[1] - 1, side, roll(main, -1, 1)) - main
    return ep * ge + jnp.where(lane == 0, em_side * (main - side), roll(em * ge, 1, 1)), ge


def extend(main, side, rows=None, corners=None):
    top = jnp.concatenate([main, side], axis=1)
    if rows is None:
        return top
    return jnp.concatenate([top, jnp.concatenate([rows, corners], axis=1)], axis=0)


def solve_inward(levels, get, inv_q, carries):
    half = levels // 2
    inv, q = inv_q

    def step(t, carry):
        new = []
        for k, last in ((t, carry[0]), (levels - 1 - t, carry[1])):
            c = get(k) * inv(k) + q(k) * last
            carries[k] = c
            new.append(c)
        return tuple(new)

    zero = jnp.zeros(carries.shape[1:], F32)
    return lax.fori_loop(0, half, step, (zero, zero), unroll=UNROLL)


def solve_outward(levels, ends, ratio, join, carries, use):
    half = levels // 2
    high, low = ends
    upper = (high + ratio(half - 1) * low) * join
    lower = (low + ratio(half) * high) * join

    def block(i, last):
        m = half // STEPS - 1 - i
        for u in range(STEPS - 1, -1, -1):
            t = m * STEPS + u
            new = []
            for k, x in ((t, last[0]), (levels - 1 - t, last[1])):
                new.append(carries[k] + ratio(k) * x)
            use(t, m, u, *new)
            last = tuple(new)
        return last

    lax.fori_loop(0, half // STEPS, block, (lower, upper), unroll=2)


def merge_halos(odd, from_one, from_two, planes, start):
    size = planes.shape[1]
    low = iota(planes.shape[1:], 1) % GROUP < 4
    for h in range(planes.shape[0] // 2):
        place = pl.ds(start + h * size, size)
        a, b = from_one[place], from_two[place]
        west = jnp.where(odd, a, b)
        east = jnp.where(odd, b, a)
        planes[2 * h] = jnp.where(low, west, roll(east, 4, 1))
        planes[2 * h + 1] = jnp.where(low, roll(west, -4, 1), east)


def part_of_pull(x, ep, em, damp):
    ge = east(x) - x
    return x * damp + ep * ge + west(em * ge), ge


def local_kernel(
    s, es, ns, mix, relax, vm, count, east, north, after,
    ep_out, em_out, np_out, nm_out, sink_out, damp_out, local_out, inv_out, q_out, r_out,
    moves_out,
):
    levels, ny, nx = s.shape
    half = levels // 2
    counts = count[...].astype(F32)
    east_count = east[...].astype(F32)
    north_count = north[...].astype(F32)
    lane = iota((ny, nx), 1)
    sub = sublane((ny, nx))

    def prepare(k):
        level = k.astype(F32)
        state = s[k]
        diffusion = mix[k].astype(F32)
        speed_east = 0.5 * es[k].astype(F32)
        speed_north = 0.5 * ns[k].astype(F32)
        open_east = level < east_count
        open_north = level < north_count
        ep = jnp.where(open_east, speed_east + diffusion, 0.0)
        em = jnp.where(open_east, speed_east - diffusion, 0.0)
        np_ = jnp.where(open_north, speed_north + diffusion, 0.0)
        nm = jnp.where(open_north, speed_north - diffusion, 0.0)
        sink = jnp.where(level < counts, relax[k].astype(F32), 0.0)
        squeeze = jnp.tanh(state)
        ep_out[k] = ep
        em_out[k] = em
        np_out[k] = np_
        nm_out[k] = nm
        sink_out[k] = sink
        damp_out[k] = 1.0 - sink * (1.0 - squeeze * squeeze)
        fe = ep * state + em * shift_up(state, 1)
        fe = jnp.where(lane == nx - 1, 0.0, fe)
        fn = np_ * state + nm * jnp.where(sub == ny - 1, 0.0, shift_up(state, 0))
        flow = fe - shift_down(fe, 1)
        flow = flow + (fn - jnp.where(sub == 0, 0.0, shift_down(fn, 0)))
        local_out[k] = state - sink * squeeze - flow

    def factor(t, carry):
        new = []
        for (k, link_level), (ratio, outer) in zip(level_pair(levels, t), carry):
            prepare(k)
            link = jnp.where(
                link_level.astype(F32) + 1.0 < counts, vm[link_level].astype(F32), 0.0
            )
            inv = 1.0 / (1.0 + outer + link - outer * ratio)
            ratio = link * inv
            inv_out[k] = inv
            q_out[k] = outer * inv
            r_out[k] = ratio
            new.append((ratio, link))
        return tuple(new)

    zero = jnp.zeros((ny, nx), F32)
    lax.fori_loop(0, half, factor, ((zero, zero), (zero, zero)), unroll=UNROLL)

    source = iota((2 * nx, 2 * nx), 0) % nx
    target = iota((2 * nx, 2 * nx), 1)
    for u in range(STEPS):
        group = 2 * u + target // nx
        lane = target % nx
        column = jnp.where(lane < 4, 3 - lane, jnp.where(lane >= nx - 4, nx + 3 - lane, -nx))
        hit = source == GROUP * group + column
        moves_out[u] = jnp.where(hit, 1.0, 0.0).astype(jnp.bfloat16)


def whole(own, halo):
    ny = own.shape[0]
    return extend(own, halo[:ny], halo[ny + 8 :], halo[ny : ny + 8])


def forward_kernel(
    s, obs, count, from_one, from_two, own_planes, own_corners, rows_n, rows_s,
    ep, em, np_, nm, sink, local, inv, q, r, moves,
    ep_halo, em_halo, np_halo, nm_halo, sink_halo, inv_halo, q_halo, r_halo, s_halo,
    middle_out, damp_out, solved_out, counts_out, join_out, send,
    planes, corners, rhs, carries, packed, moved, moved_rows, sides,
):
    levels, ny, nx = s.shape
    half = levels // 2
    per_plane = 128 // GROUP
    plane_count = levels // per_plane
    odd = odd_column()
    merge_halos(odd, from_one, from_two, planes, 0)
    merge_halos(odd, from_one, from_two, corners, planes.shape[0] // 2 * planes.shape[1])

    def rim(index):
        return merge_rows(rows_n[index], rows_s[index])

    count_plane = len(NAMES[:6]) * plane_count
    side_counts = jnp.dot(
        jnp.concatenate([planes[count_plane]] + [roll(corners[plane_count], 4, 0)] * 2, axis=0).astype(
            jnp.bfloat16
        ),
        moves[0, :nx, :nx],
        preferred_element_type=F32,
    )
    count_ext = extend(
        count[...].astype(F32),
        side_counts[:ny],
        rim(levels + half),
        side_counts[ny : ny + 8],
    )
    east_ext = jnp.minimum(count_ext, east(count_ext))
    counts_out[0] = count_ext
    counts_out[1] = east_ext
    counts_out[2] = step_count(count_ext, 0)
    count_halo = jnp.concatenate(
        [count_ext[:ny, nx:], count_ext[ny:, nx:], count_ext[ny:, :nx]], axis=0
    )
    small_sub = sublane((8, nx))
    east_rows = east_ext[ny:, :nx]
    north_rows = jnp.where(small_sub == 7, counts_out[2, ny:, :nx], 0.0)
    lane = iota((ny, nx), 1)
    per_half = per_plane // 2

    strip = (ny + 8, nx)
    place = iota(strip, 1) % GROUP
    low = place < 4
    groups = iota(strip, 1) // GROUP
    from_top = groups % 2 == 0
    strip_sub = sublane(strip)

    def columns(p, carry):
        t = p * per_half + groups // 2
        level = jnp.where(from_top, t, levels - 1 - t).astype(F32)
        link_level = jnp.where(from_top, t, levels - 2 - t).astype(F32)

        def side_and_corner(a, c):
            return jnp.concatenate([a, c], axis=0)

        def strips(west):
            def pick(halo, own):
                near_side = low[: halo.shape[0]]
                return jnp.where(near_side, halo, own) if west else jnp.where(near_side, own, halo)

            x = unpack_rows(
                pick(corners[p], own_corners[p]),
                pick(corners[plane_count + p], own_corners[plane_count + p]),
            )
            side = {}
            for a, name in enumerate(NAMES[:6]):
                at = a * plane_count + p
                side[name] = pick(planes[at], own_planes[at])
            for name in NAMES[:4] + NAMES[5:6]:
                x[name] = side_and_corner(side[name], x[name])
            counts = side_and_corner(
                pick(planes[count_plane], own_planes[count_plane]),
                roll(pick(corners[plane_count + p], own_corners[plane_count + p]), 4, 0),
            )
            state = x["s"]
            open_east = level < step_count(counts, 1)
            open_north = (level < step_count(counts, 0)) & (
                (strip_sub < ny) | (strip_sub == ny + 7)
            )
            ep_s = jnp.where(open_east, 0.5 * x["es"] + x["mix"], 0.0)
            em_s = jnp.where(open_east, 0.5 * x["es"] - x["mix"], 0.0)
            np_s = jnp.where(open_north, 0.5 * x["ns"] + x["mix"], 0.0)
            nm_s = jnp.where(open_north, 0.5 * x["ns"] - x["mix"], 0.0)
            sink_s = jnp.where(level[:ny] < counts[:ny], side["relax"], 0.0)
            link = jnp.where(link_level + 1.0 < counts, x["vm"], 0.0)
            fe = ep_s * state + em_s * shift_up(state, 1)
            fe_west = shift_down(fe, 1)
            fn = np_s * state + nm_s * shift_up(state, 0)
            base = side_and_corner(side["s"] - sink_s * jnp.tanh(side["s"]), x["base"])
            right = base - (fe - fe_west) - (fn - shift_down(fn, 0))
            return (right, link, np_s, nm_s, ep_s, em_s, sink_s, state), fe, fe_west

        western, through_west, _ = strips(True)
        eastern, _, through_east = strips(False)
        seam = jnp.where(place == 3, through_west, through_east)
        both = [jnp.where(low[: a.shape[0]], a, b) for a, b in zip(western, eastern)]
        right, link, np_c, nm_c = (x[ny:] for x in both[:4])
        corner = pair_rows(right, link)
        corner = jnp.where((small_sub == 3) | (small_sub == 4), roll(seam[ny:], 4, 0), corner)
        corner = jnp.where(small_sub == 5, roll(np_c, 6, 0), corner)
        corner = jnp.where(small_sub == 6, roll(nm_c, 7, 0), corner)
        both = [x[:ny] for x in both]
        near_seam = planes[NAMES.index("relax") * plane_count + p]
        further = planes[NAMES.index("ns") * plane_count + p]
        side_place = place[:ny]
        seen = jnp.where(side_place < 3, roll(further, 2, 1), roll(near_seam, 3, 1))
        beyond = jnp.where(side_place > 4, roll(further, -2, 1), roll(near_seam, -3, 1))
        seen = jnp.where(side_place < 4, seen, beyond)
        both = both[:2] + [seam[:ny], seen] + both[2:] + [jnp.concatenate([corner] * 2, axis=0)]
        for i, x in enumerate(both):
            split(p, i * ny, x)
        return carry

    def split(p, at, x):
        for h, y in enumerate((x, roll(x, nx // 2, 1))):
            high = y.astype(jnp.bfloat16)
            packed[2 * p + h, at : at + ny, :nx] = high
            packed[2 * p + h, at : at + ny, nx:] = (y - high.astype(F32)).astype(jnp.bfloat16)

    lax.fori_loop(0, plane_count, columns, 0, unroll=plane_count)

    def unpack(u):
        move = moves[u]

        def place_both(m, carry):
            out = jnp.dot(packed[m], move, preferred_element_type=F32)
            t = m * STEPS + u
            for j, k in enumerate((t, levels - 1 - t)):
                x = out[:, j * nx : (j + 1) * nx]
                np_x, nm_x, ep_x, em_x, sink_x, s_x, corner = (
                    x[i * ny : (i + 1) * ny] for i in range(4, 11)
                )
                corner = corner[:8]
                moved[k] = x[: 4 * ny]
                moved_rows[k] = corner
                ep_halo[k, :ny] = ep_x
                em_halo[k, :ny] = em_x
                np_halo[k, :ny] = np_x
                nm_halo[k, :ny] = nm_x
                np_halo[k, ny : ny + 8] = roll(corner, 2, 0)
                nm_halo[k, ny : ny + 8] = roll(corner, 1, 0)
                sink_halo[k] = sink_x
                s_halo[k, :ny] = s_x
            return carry

        lax.fori_loop(0, 2 * plane_count, place_both, 0, unroll=2 * plane_count)

    for u in range(STEPS):
        unpack(u)

    def prepare(m, u, j, k, link_level, second):
        t = m * STEPS + u
        x = unpack_rows(rim(2 * t + j), roll(second, 4, 0) if j else second)
        level = k.astype(F32)
        row = x["s"]
        open_east = level < east_rows
        open_north = level < north_rows
        ep_r = jnp.where(open_east, 0.5 * x["es"] + x["mix"], 0.0)
        em_r = jnp.where(open_east, 0.5 * x["es"] - x["mix"], 0.0)
        np_r = jnp.where(open_north, 0.5 * x["ns"] + x["mix"], 0.0)
        nm_r = jnp.where(open_north, 0.5 * x["ns"] - x["mix"], 0.0)
        link_r = jnp.where(link_level.astype(F32) + 1.0 < count_halo[ny + 8 :], x["vm"], 0.0)
        corner = moved_rows[k]
        right, link, seam = (moved[k, i * ny : (i + 1) * ny] for i in range(3))
        seam_rows = roll(corner, 4, 0)
        np_halo[k, ny + 8 :] = np_r
        nm_halo[k, ny + 8 :] = nm_r
        s_halo[k, ny + 8 :] = row

        own = s[k]
        last, first = lane == nx - 1, lane == 0
        fe = ep_r * row + em_r * shift_up(row, 1)
        flow = jnp.where(last[:8], seam_rows, fe) - jnp.where(
            first[:8], seam_rows, shift_down(fe, 1)
        )
        fn = np_r * row + nm_r * shift_up(own[:8], 0)
        top = np_[k, ny - 8 :] * own[ny - 8 :]
        cross = nm[k, ny - 8 :] * shift_up(row, 0)
        from_block = jnp.where(small_sub == 0, shift_down(top + cross, 0), 0.0)
        right_r = x["base"] - flow - (fn - from_block)

        inner = local[k] + jnp.where(first, seam, jnp.where(last, -seam, 0.0))
        low_rows = inner[:8] + jnp.where(small_sub == 0, shift_down(fn, 0), 0.0)
        high_rows = inner[ny - 8 :] - jnp.where(small_sub == 7, cross, 0.0)
        between = [inner[8 : ny - 8]] if ny > 16 else []
        inner = jnp.concatenate([low_rows] + between + [high_rows], axis=0)
        halo = jnp.concatenate([right, corner, right_r], axis=0)
        return inner, halo, jnp.concatenate([link, roll(corner, 6, 0), link_r], axis=0)

    def factor(m, carry):
        for u in range(STEPS):
            carry = factor_step(m, u, carry)
        return carry

    def factor_step(m, u, carry):
        t = m * STEPS + u
        second = rim(levels + t)
        new = []
        for j, (k, link_level) in enumerate(level_pair(levels, t)):
            ratio, c_own, c_halo, outer = carry[j]
            own, halo, link = prepare(m, u, j, k, link_level, second)
            inv_h = 1.0 / (1.0 + outer + link - outer * ratio)
            q_h = outer * inv_h
            ratio = link * inv_h
            c_own = own * inv[k] + q[k] * c_own
            c_halo = halo * inv_h + q_h * c_halo
            inv_halo[k] = inv_h
            q_halo[k] = q_h
            r_halo[k] = ratio
            carries[k] = whole(c_own, c_halo)
            new.append((ratio, c_own, c_halo, link))
        return tuple(new)

    zero = jnp.zeros(count_halo.shape, F32)
    begin = (zero, jnp.zeros((ny, nx), F32), zero, zero)
    (r_top, top_own, top_halo, _), (r_low, low_own, low_halo, _) = lax.fori_loop(
        0, half // STEPS, factor, (begin, begin), unroll=2
    )
    c_top, c_low = whole(top_own, top_halo), whole(low_own, low_halo)
    join = 1.0 / (1.0 - whole(r[half - 1], r_top) * whole(r[half], r_low))
    join_out[...] = join

    def ext(own, halo):
        return lambda k: whole(own[k], halo[k])

    def inner(own, halo):
        return lambda k: extend(own[k], halo[k, :ny])

    def spread(state, ep, em, np_, nm):
        fe = ep * state + em * east(state)
        fn = np_ * state + nm * shift_up(state, 0)
        return (fe - west(fe)) + (fn - shift_down(fn, 0))

    def both(one):
        def use(t, m, u, top, low):
            one(t, top, m, u, 0)
            one(levels - 1 - t, low, m, u, 1)

        return use

    def to_second(k, x, m, u, j):
        middle_out[k] = x
        state = x[:ny]
        squeeze = jnp.tanh(state)
        loss = inner(sink, sink_halo)(k)
        damp_out[k] = 1.0 - loss * (1.0 - squeeze * squeeze)
        fields = (ext(ep, ep_halo), ext(em, em_halo), ext(np_, np_halo), ext(nm, nm_halo))
        flow = spread(x, *(field(k) for field in fields))
        rhs[k] = state - flow[:ny] - loss * squeeze

    solve_outward(levels, (c_top, c_low), ext(r, r_halo), join, carries, both(to_second))

    main = carries.at[:, :ny]
    inv_q = inner(inv, inv_halo), inner(q, q_halo)
    ratio = inner(r, r_halo)
    ends = solve_inward(levels, lambda k: rhs[k], inv_q, main)

    def to_adjoint(k, x, m, u, j):
        seen = extend(obs[k].astype(F32), moved[k, 3 * ny :])
        rhs[k] = jnp.where(k.astype(F32) < count_ext[:ny], x - seen, 0.0)

    solve_outward(levels, ends, ratio, join[:ny], main, both(to_adjoint))
    ends = solve_inward(levels, lambda k: rhs[k], inv_q, main)

    def rim_part(k, solved):
        solved_out[k] = solved
        x = edge_rows(solved)
        main, side = halves(x)
        rows_of = lambda ref: edge_rows(ref[k])
        part, _ = pull_x(main, side, rows_of(ep), rows_of(em), edge_rows(em_halo[k, :ny]))
        part = part + main * edge_rows(damp_out[k, :, :nx])
        gn = shift_up(main, 0) - main
        sub = sublane(main.shape)
        part = part + jnp.where(
            sub == 0,
            rows_of(np_) * gn,
            jnp.where(sub == 7, shift_down(rows_of(nm) * gn, 0), 0.0),
        )
        return jnp.concatenate([pair_rows(main, part), side], axis=1)

    lane8 = iota((8, nx), 1)

    def to_send(t, m, u, top, low):
        pair = two_levels(rim_part(t, top), rim_part(levels - 1 - t, low))
        send[t] = pair[:, :nx]
        before = jnp.zeros((8, nx), F32) if u == STEPS - 1 else sides[m]
        moved = roll(pair[:, nx:], 2 * u + 1, 1)
        sides[m] = jnp.where(lane8 // 2 == u, moved, before)

    solve_outward(levels, ends, ratio, join[:ny], main, to_send)
    both_sides = sides[0]
    for m in range(1, half // STEPS):
        place = m * 2 * STEPS
        both_sides = jnp.where(lane8 < place, both_sides, roll(sides[m], place, 1))
    send[half] = both_sides


def inner_kernel(
    ep, em, np_, nm, ep_halo, em_halo, np_halo, nm_halo, damp, middle, solved, counts,
    s, s_halo, part_out, late_out, run_out, rise_out,
):
    levels, ny, width = solved.shape
    nx = width // 2
    sub = sublane((ny, width))
    inside = sub < ny - 1

    def inner(k, carry):
        x = solved[k]
        state = middle[k]
        field = lambda own, halo: extend(own[k], halo[k, :ny])
        part, ge = part_of_pull(x, field(ep, ep_halo), field(em, em_halo), damp[k])
        gn = jnp.where(inside, shift_up(x, 0) - x, 0.0)
        part_out[k] = (
            part + field(np_, np_halo) * gn + shift_down(field(nm, nm_halo) * gn, 0)
        )
        level = k.astype(F32)
        open_east = level < counts[1, :ny, :nx]
        open_north = level < counts[2, :ny, :nx]

        def slopes(state):
            run = (east(state[:ny]) - state[:ny])[:, :nx]
            rise = shift_up(state[:, :nx], 0)[:ny] - state[:ny, :nx]
            return jnp.where(open_east, run, 0.0), jnp.where(open_north, rise, 0.0)

        run, rise = slopes(state)
        late_out[k] = ge[:, :nx] * run + gn[:, :nx] * rise
        run_out[k], rise_out[k] = slopes(whole(s[k], s_halo[k]))
        return carry

    lax.fori_loop(0, levels, inner, 0, unroll=UNROLL)


def backward_kernel(
    ep, em, np_, nm, inv, q, r, ep_halo, em_halo, np_halo, nm_halo, inv_halo, q_halo, r_halo,
    middle, damp, solved, counts, join, part, late, run, rise, rows_n, rows_s,
    adjoint_out, gradient_out, carries, adjoint, gradient, sides, sent,
):
    levels, ny, width = solved.shape
    nx = width // 2
    half = levels // 2
    sub = sublane((8, width))

    side = merge_rows(rows_n[half], rows_s[half])
    for m in range(half // STEPS):
        sides[m] = roll(side, -2 * STEPS * m, 1)

    def rims(m, u):
        t = m * STEPS + u
        line = merge_rows(rows_n[t], rows_s[t])
        corner = roll(sides[m], -1 - 2 * u, 1)
        both = jnp.concatenate([line, corner], axis=1)
        return both, roll(both, 4, 0)

    def across(k, rim):
        inner = part[k]
        near_part = roll(rim, 6, 0)
        south = solved[k, :8] - shift_down(rim, 0)
        north = shift_up(rim, 0) - solved[k, ny - 8 :]
        north_plus = whole(np_[k], np_halo[k])
        north_minus = whole(nm[k], nm_halo[k])
        np_rim, nm_rim = north_plus[ny:], north_minus[ny:]
        np_top, nm_top = north_plus[ny - 8 : ny], north_minus[ny - 8 : ny]
        low = inner[:8] + jnp.where(sub == 0, shift_down(nm_rim, 0) * south, 0.0)
        high = inner[ny - 8 :] + jnp.where(sub == 7, np_top * north, 0.0)
        outer = near_part + jnp.where(
            sub == 0, shift_down(nm_top * north, 0), np_rim * shift_up(south, 0)
        )
        rise = (shift_up(middle[k, ny:], 0) - middle[k, ny - 8 : ny])[:, :nx]
        open_north = (sub[:, :nx] == 7) & (k.astype(F32) < counts[2, ny - 8 : ny, :nx])
        extra = jnp.where(open_north, north[:, :nx] * rise, 0.0)
        gradient[k, : ny - 8] = late[k, : ny - 8]
        gradient[k, ny - 8 :] = late[k, ny - 8 :] + extra
        middle_rows = [inner[8 : ny - 8]] if ny > 16 else []
        return jnp.concatenate([low, *middle_rows, high, outer], axis=0)

    def late_steps(m, carry):
        for u in range(STEPS):
            t = m * STEPS + u
            new = []
            for k, rim, last in zip((t, levels - 1 - t), rims(m, u), carry):
                c = across(k, rim) * whole(inv[k], inv_halo[k])
                c = c + whole(q[k], q_halo[k]) * last
                carries[k] = c
                new.append(c)
            carry = tuple(new)
        return carry

    zero = jnp.zeros(carries.shape[1:], F32)
    ends = lax.fori_loop(0, half // STEPS, late_steps, (zero, zero), unroll=2)

    def early(k, x):
        main, side = halves(x[:ny])
        flow, ge = pull_x(main, side, ep[k], em[k], em_halo[k, :ny])
        result = main * damp[k] + flow
        column = x[:, :nx]
        gn = shift_up(column, 0) - column
        minus = jnp.concatenate([nm[k], nm_halo[k, ny + 8 :]], axis=0)
        result = result + np_[k] * gn[:ny] + shift_down(minus * gn, 0)[:ny]
        adjoint[k] = result
        gradient[k] = -(gradient[k] + ge * run[k] + gn[:ny] * rise[k])

    def copies(p):
        out = []
        for i, begin in enumerate((p * UNROLL, levels - (p + 1) * UNROLL)):
            place = pl.ds(begin, UNROLL)
            for j, (source, target) in enumerate(
                ((adjoint, adjoint_out), (gradient, gradient_out))
            ):
                out.append(
                    pltpu.make_async_copy(
                        source.at[place], target.at[place], sent.at[p, 2 * i + j]
                    )
                )
        return out

    high, low = ends
    steps = half // UNROLL
    ratio = lambda k: whole(r[k], r_halo[k])
    last = (low + ratio(half) * high) * join[...], (high + ratio(half - 1) * low) * join[...]

    def block(i, last):
        p = steps - 1 - i
        for g in range(UNROLL - 1, -1, -1):
            t = p * UNROLL + g
            new = []
            for k, x in ((t, last[0]), (levels - 1 - t, last[1])):
                x = carries[k] + ratio(k) * x
                early(k, x)
                new.append(x)
            last = tuple(new)
        for copy in copies(p):
            copy.start()
        return last

    lax.fori_loop(0, steps, block, last)
    for p in range(steps):
        for copy in copies(p):
            copy.wait()


def ring(axis, distance):
    count = lax.axis_size(axis)
    return [(i, (i + distance) % count) for i in range(count)]


def both_ways(x):
    from_north = lax.ppermute(x, "ty", ring("ty", -1))
    if lax.axis_size("ty") == 2:
        return from_north, from_north
    return from_north, lax.ppermute(x, "ty", ring("ty", 1))


def swap(x, phase):
    nx = lax.axis_size("tx")
    return lax.ppermute(
        x, "tx", [(i, (i + 1) % nx if i % 2 == phase else (i - 1) % nx) for i in range(nx)]
    )


def per_device(
    tracer_start,
    observed,
    east_speed,
    north_speed,
    mixing,
    vertical_mixing,
    relax_rate,
    level_count,
    face_east,
    face_north,
):
    levels, ny, nx = tracer_start.shape
    per_plane = 128 // GROUP
    plane_count = levels // per_plane
    pairs = (len(NAMES[:6]) * plane_count + 2) // 2
    fields = (
        tracer_start, east_speed, north_speed, mixing, relax_rate, vertical_mixing, observed,
        level_count, face_east, face_north,
    )
    half = levels // 2
    corner_planes = 2 * plane_count
    *fields, rows, corners = call(
        rim_kernel,
        [jax.ShapeDtypeStruct(x.shape, x.dtype) for x in fields]
        + [(levels + half + 1, 8, nx), (corner_planes, 8, nx)],
        [pltpu.SemaphoreType.DMA((10,))],
        *[pltpu.with_memory_space_constraint(x, pltpu.HBM) for x in fields],
        space=HBM,
    )
    corners_n, corners_s = both_ways(corners)
    rows_n, rows_s = both_ways(rows)
    (planes,) = call(column_kernel, [(2 * pairs, ny, nx)], [], *fields[:8])
    packed = (pairs * ny + corner_planes // 2 * 8, nx)
    one, two, own_corners = call(
        halves_kernel, [packed, packed, corners.shape], [],
        planes, corners_n, corners_s,
        cost=pl.CostEstimate(flops=10**10, bytes_accessed=0, transcendentals=0),
    )
    from_two = swap(two, 1)
    from_one = swap(one, 0)
    ext = (levels, ny + 8, 2 * nx)
    block = (levels, ny, 2 * nx)
    own = (levels, ny, nx)
    halo = (levels, ny + 16, nx)
    s, es, ns, mix, relax, vm, obs, count, east, north = fields
    *coefficients, damp, local, inv, q, r, moves = call(
        local_kernel,
        [own] * 10 + [jax.ShapeDtypeStruct((STEPS, 2 * nx, 2 * nx), jnp.bfloat16)],
        [],
        s, es, ns, mix, relax, vm, count, east, north, one,
        cost=pl.CostEstimate(flops=10**9, bytes_accessed=0, transcendentals=0),
    )
    ep, em, np_, nm, sink = coefficients
    outs = call(
        forward_kernel,
        [halo] * 4 + [own] + [halo] * 4 + [ext, block, block, (3,) + ext[1:], ext[1:]]
        + [(half + 1, 8, nx)],
        [
            planes.shape,
            corners.shape,
            block,
            ext,
            pltpu.VMEM((2 * plane_count, 11 * ny, 2 * nx), jnp.bfloat16),
            (levels, 4 * ny, nx),
            (levels, 8, nx),
            (2 * plane_count, 8, nx),
        ],
        s, obs, count, from_one, from_two, planes, own_corners, rows_n, rows_s,
        ep, em, np_, nm, sink, local, inv, q, r, moves,
    )
    ep_h, em_h, np_h, nm_h, _, inv_h, q_h, r_h, s_h, *outs = outs
    middle, late_damp, solved, counts, join, send = outs
    sent_n, sent_s = both_ways(send)
    faces = ep, em, np_, nm
    halo_faces = ep_h, em_h, np_h, nm_h
    part, late, run, rise = call(
        inner_kernel,
        [block] + [own] * 3,
        [],
        *faces, *halo_faces, late_damp, middle, solved, counts, s, s_h,
        cost=pl.CostEstimate(flops=0, bytes_accessed=8 << 20, transcendentals=0),
    )
    adjoint, gradient = call(
        backward_kernel,
        [own] * 2,
        [ext, own, own, (2 * plane_count, 8, nx), pltpu.SemaphoreType.DMA((half // UNROLL, 4))],
        *faces, inv, q, r, *halo_faces, inv_h, q_h, r_h,
        middle, damp, solved, counts, join, part, late, run, rise, sent_n, sent_s,
        out_space=HBM,
    )
    return adjoint, gradient


def solution(mesh):
    block = P(None, "ty", "tx")
    plane = P("ty", "tx")
    return jax.shard_map(
        per_device,
        mesh=mesh,
        in_specs=(block,) * 7 + (plane,) * 3,
        out_specs=(block, block),
        check_vma=False,
    )
```

```python
import functools

import jax
import jax.numpy as jnp
from jax import lax
from jax.experimental import pallas as pl
from jax.experimental.pallas import tpu as pltpu
from jax.sharding import PartitionSpec as P

F32 = jnp.float32
VMEM = pl.BlockSpec(memory_space=pltpu.VMEM)
HBM = pl.BlockSpec(memory_space=pltpu.HBM)
UNROLL = 8
STEPS = 4
GROUP = 8
NAMES = ("s", "es", "ns", "mix", "relax", "vm", "obs")


def call(kernel, outs, scratch, *args, space=VMEM, out_space=VMEM, cost=None):
    def typed(x):
        return x if isinstance(x, jax.ShapeDtypeStruct) else jax.ShapeDtypeStruct(x, F32)

    return pl.pallas_call(
        kernel,
        out_shape=[typed(x) for x in outs],
        in_specs=[space] * len(args),
        out_specs=[out_space] * len(outs),
        scratch_shapes=[pltpu.VMEM(x, F32) if isinstance(x, tuple) else x for x in scratch],
        compiler_params=pltpu.CompilerParams(vmem_limit_bytes=16 << 20),
        cost_estimate=cost,
    )(*args)


def iota(shape, dim):
    return lax.broadcasted_iota(jnp.int32, shape, dim)


def roll(x, shift, axis):
    if isinstance(shift, int):
        shift = shift % x.shape[axis]
        if shift == 0:
            return x
    return pltpu.roll(x, shift, axis)


def odd_column():
    return lax.rem(lax.axis_index("tx"), 2) == 1


def level_of(ref, name, level):
    if name == "vm":
        level = jnp.minimum(level, ref.shape[0] - 1)
    return ref[level].astype(F32)


def edge_rows(block):
    return jnp.where(iota((8, block.shape[1]), 0) < 4, block[:8], block[-8:])


def sublane(shape):
    return iota(shape, 0)


def step_count(counts, axis):
    return jnp.minimum(counts, shift_up(counts, axis))


def pair_rows(first, second):
    sub = sublane(first.shape)
    return jnp.where((sub == 1) | (sub == 2), roll(second, 2, 0), first)


def level_pair(levels, t):
    return (t, t), (levels - 1 - t, levels - 2 - t)


def in_all_groups(x):
    group = iota(x.shape, 1) // GROUP
    out = jnp.zeros(x.shape, F32)
    for g in range(x.shape[1] // GROUP):
        out = jnp.where(group == g, roll(x, GROUP * g + 4, 1), out)
    return out


def pack_rows(get, counts, level):
    tile = {name: edge_rows(get(name)) for name in NAMES[:6]}
    s = tile["s"]
    sub = sublane(s.shape)
    open_north = level < step_count(counts, 0)
    fn = jnp.where(
        open_north,
        (0.5 * tile["ns"] + tile["mix"]) * s + (0.5 * tile["ns"] - tile["mix"]) * shift_up(s, 0),
        0.0,
    )
    sink = jnp.where(level < counts, tile["relax"], 0.0)
    inner = jnp.where(sub == 0, -fn, jnp.where(sub == 7, shift_down(fn, 0), 0.0))
    base = s - sink * jnp.tanh(s) + inner
    first = pair_rows(s, base)
    first = jnp.where((sub == 3) | (sub == 4), roll(tile["es"], 4, 0), first)
    first = jnp.where((sub == 5) | (sub == 6), roll(tile["mix"], 6, 0), first)
    lane = iota(s.shape, 1)
    fe = (0.5 * tile["es"] + tile["mix"]) * s
    fe = fe + (0.5 * tile["es"] - tile["mix"]) * shift_up(s, 1)
    fe = jnp.where((level < step_count(counts, 1)) & (lane < s.shape[1] - 1), fe, 0.0)
    line = pair_rows(s, base - (fe - shift_down(fe, 1)))
    line = jnp.where((sub == 3) | (sub == 4), roll(tile["vm"], 4, 0), line)
    line = jnp.where(sub == 5, roll(tile["ns"], 6, 0), line)
    line = jnp.where(sub == 6, roll(tile["mix"], 7, 0), line)
    return line, first, pair_rows(tile["vm"], tile["ns"])


def merge_lines(north, south):
    sub = sublane(north.shape)
    return jnp.where((sub == 0) | (sub == 2) | (sub == 4), north, south)


def unpack_line(line):
    return {
        "s": line,
        "base": roll(line, 6, 0),
        "vm": roll(line, 4, 0),
        "ns": roll(line, 2, 0),
        "mix": roll(line, 1, 0),
    }


def unpack_rows(first, second):
    return {
        "s": first,
        "base": roll(first, 6, 0),
        "es": roll(first, 4, 0),
        "mix": roll(first, 2, 0),
        "vm": second,
        "ns": roll(second, 6, 0),
    }


def two_levels(x, y):
    sub = sublane(x.shape)
    return jnp.where((sub >= 3) & (sub <= 6), roll(y, 4, 0), x)


def shift_up(x, axis):
    return roll(x, -1, axis)


def shift_down(x, axis):
    return roll(x, 1, axis)


def rim_kernel(*args):
    fields = args[:10]
    s, es, ns, mix, relax, vm, obs, count, *_ = kept = args[10:20]
    corners, arrived = args[20:]
    copies = [pltpu.make_async_copy(fields[i], kept[i], arrived.at[i]) for i in range(10)]
    first = (7, 0, 1, 2, 3, 4, 5)
    rest = (6, 8, 9)
    for i in first + rest:
        copies[i].start()
    for i in first:
        copies[i].wait()
    refs = dict(zip(NAMES, (s, es, ns, mix, relax, vm, obs)))
    levels = s.shape[0]
    per_plane = 128 // GROUP
    small = (8, s.shape[2])
    group = iota(small, 1) // GROUP
    half = per_plane // 2
    plane_count = levels // per_plane
    counts = edge_rows(count[...].astype(F32))
    sub = sublane(small)

    def rims(p, carry):
        acc = jnp.zeros(small, F32)
        late = jnp.zeros(small, F32)
        for g in range(half):
            t = p * half + g
            for j, (k, link) in enumerate(level_pair(levels, t)):
                _, first, second = pack_rows(
                    lambda name: level_of(refs[name], name, link if name == "vm" else k),
                    counts,
                    k.astype(F32),
                )
                place = 2 * g + j
                acc = jnp.where(group == place, roll(first, GROUP * place + 4, 1), acc)
                second = jnp.where((sub == 3) | (sub == 4), roll(counts, 4, 0), second)
                late = jnp.where(group == place, roll(second, GROUP * place + 4, 1), late)
        corners[p] = acc
        corners[plane_count + p] = late
        return carry

    lax.fori_loop(0, plane_count, rims, 0)
    for i in rest:
        copies[i].wait()


def column_kernel(s, es, ns, mix, relax, vm, obs, count, planes, rows):
    refs = dict(zip(NAMES, (s, es, ns, mix, relax, vm, obs)))
    levels = s.shape[0]
    per_plane = 128 // GROUP
    plane_count = levels // per_plane
    shape = s.shape[1:]
    group = iota(shape, 1) // GROUP

    place = iota(shape, 1) % GROUP
    counts = edge_rows(count[...].astype(F32))
    rows[levels] = counts

    def lines(t, carry):
        for j, (k, link) in enumerate(level_pair(levels, t)):
            rows[2 * t + j], _, _ = pack_rows(
                lambda name: level_of(refs[name], name, link if name == "vm" else k),
                counts,
                k.astype(F32),
            )
        return carry

    lax.fori_loop(0, levels // 2, lines, 0, unroll=UNROLL)

    def columns(p, carry):
        packed = []
        for name in NAMES:
            acc = jnp.zeros(shape, F32)
            for g in range(per_plane):
                pair = level_pair(levels, p * (per_plane // 2) + g // 2)
                x = refs[name][pair[g % 2][name == "vm"]].astype(F32)
                acc = jnp.where(group == g, roll(x, GROUP * g + 4, 1), acc)
            packed.append(acc)
        seen = packed.pop()
        for name, distance in (("ns", 2), ("relax", 3)):
            i = NAMES.index(name)
            x = jnp.where(place == 0, roll(seen, -distance, 1), packed[i])
            packed[i] = jnp.where(place == GROUP - 1, roll(seen, distance, 1), x)
        for a, x in enumerate(packed):
            planes[a * plane_count + p] = x
        return carry

    lax.fori_loop(0, plane_count, columns, 0)
    total = len(NAMES[:6]) * plane_count
    planes[total] = in_all_groups(count[...].astype(F32))
    for p in range(total + 1, planes.shape[0]):
        planes[p] = jnp.zeros(shape, F32)


def merge_rows(north, south):
    return jnp.where(sublane(north.shape) % 2 == 0, north, south)


def halves_kernel(planes, corners_n, corners_s, one, two, kept):
    odd = odd_column()
    pairs = planes.shape[0] // 2
    ny = planes.shape[1]

    def put(place, x, y):
        low = iota(x.shape, 1) % GROUP < 4
        to_east = jnp.where(low, x, roll(y, 4, 1))
        to_west = jnp.where(low, roll(x, -4, 1), y)
        one[place] = jnp.where(odd, to_west, to_east)
        two[place] = jnp.where(odd, to_east, to_west)

    for h in range(pairs):
        put(pl.ds(h * ny, ny), planes[2 * h], planes[2 * h + 1])

    count = corners_n.shape[0]
    def corner(p):
        return merge_rows(corners_n[p], corners_s[p])

    for h in range(count // 2):
        x, y = corner(2 * h), corner(2 * h + 1)
        kept[2 * h] = x
        kept[2 * h + 1] = y
        put(pl.ds(pairs * ny + h * 8, 8), x, y)


def halves(x):
    nx = x.shape[1] // 2
    return x[:, :nx], x[:, nx:]


def east(x):
    main, side = halves(x)
    lane = iota(main.shape, 1)
    return jnp.concatenate(
        [
            jnp.where(lane == lane.shape[1] - 1, side, roll(main, -1, 1)),
            jnp.where(lane == 0, main, roll(side, 1, 1)),
        ],
        axis=1,
    )


def west(x):
    main, side = halves(x)
    lane = iota(main.shape, 1)
    return jnp.concatenate(
        [
            jnp.where(lane == 0, side, roll(main, 1, 1)),
            jnp.where(lane == lane.shape[1] - 1, main, roll(side, -1, 1)),
        ],
        axis=1,
    )


def pull_x(main, side, ep, em, em_side):
    lane = iota(main.shape, 1)
    ge = jnp.where(lane == lane.shape[1] - 1, side, roll(main, -1, 1)) - main
    return ep * ge + jnp.where(lane == 0, em_side * (main - side), roll(em * ge, 1, 1)), ge


def extend(main, side, rows=None, corners=None):
    top = jnp.concatenate([main, side], axis=1)
    if rows is None:
        return top
    return jnp.concatenate([top, jnp.concatenate([rows, corners], axis=1)], axis=0)


def solve_inward(levels, get, inv_q, carries):
    half = levels // 2
    inv, q = inv_q

    def step(t, carry):
        new = []
        for k, last in ((t, carry[0]), (levels - 1 - t, carry[1])):
            c = get(k) * inv(k) + q(k) * last
            carries[k] = c
            new.append(c)
        return tuple(new)

    zero = jnp.zeros(carries.shape[1:], F32)
    return lax.fori_loop(0, half, step, (zero, zero), unroll=UNROLL)


def solve_outward(levels, ends, ratio, join, carries, use):
    half = levels // 2
    high, low = ends
    upper = (high + ratio(half - 1) * low) * join
    lower = (low + ratio(half) * high) * join

    def block(i, last):
        m = half // STEPS - 1 - i
        for u in range(STEPS - 1, -1, -1):
            t = m * STEPS + u
            new = []
            for k, x in ((t, last[0]), (levels - 1 - t, last[1])):
                new.append(carries[k] + ratio(k) * x)
            use(t, m, u, *new)
            last = tuple(new)
        return last

    lax.fori_loop(0, half // STEPS, block, (lower, upper), unroll=2)


def merge_halos(odd, from_one, from_two, planes, start):
    size = planes.shape[1]
    low = iota(planes.shape[1:], 1) % GROUP < 4
    for h in range(planes.shape[0] // 2):
        place = pl.ds(start + h * size, size)
        a, b = from_one[place], from_two[place]
        west = jnp.where(odd, a, b)
        east = jnp.where(odd, b, a)
        planes[2 * h] = jnp.where(low, west, roll(east, 4, 1))
        planes[2 * h + 1] = jnp.where(low, roll(west, -4, 1), east)


def part_of_pull(x, ep, em, damp):
    ge = east(x) - x
    return x * damp + ep * ge + west(em * ge), ge


def local_kernel(
    s, es, ns, mix, relax, vm, count, east, north, after,
    ep_out, em_out, np_out, nm_out, sink_out, damp_out, local_out, inv_out, q_out, r_out,
    moves_out,
):
    levels, ny, nx = s.shape
    half = levels // 2
    counts = count[...].astype(F32)
    east_count = east[...].astype(F32)
    north_count = north[...].astype(F32)
    lane = iota((ny, nx), 1)
    sub = sublane((ny, nx))

    def prepare(k):
        level = k.astype(F32)
        state = s[k]
        diffusion = mix[k].astype(F32)
        speed_east = 0.5 * es[k].astype(F32)
        speed_north = 0.5 * ns[k].astype(F32)
        open_east = level < east_count
        open_north = level < north_count
        ep = jnp.where(open_east, speed_east + diffusion, 0.0)
        em = jnp.where(open_east, speed_east - diffusion, 0.0)
        np_ = jnp.where(open_north, speed_north + diffusion, 0.0)
        nm = jnp.where(open_north, speed_north - diffusion, 0.0)
        sink = jnp.where(level < counts, relax[k].astype(F32), 0.0)
        squeeze = jnp.tanh(state)
        ep_out[k] = ep
        em_out[k] = em
        np_out[k] = np_
        nm_out[k] = nm
        sink_out[k] = sink
        damp_out[k] = 1.0 - sink * (1.0 - squeeze * squeeze)
        fe = ep * state + em * shift_up(state, 1)
        fe = jnp.where(lane == nx - 1, 0.0, fe)
        fn = np_ * state + nm * jnp.where(sub == ny - 1, 0.0, shift_up(state, 0))
        flow = fe - shift_down(fe, 1)
        flow = flow + (fn - jnp.where(sub == 0, 0.0, shift_down(fn, 0)))
        local_out[k] = state - sink * squeeze - flow

    def factor(t, carry):
        new = []
        for (k, link_level), (ratio, outer) in zip(level_pair(levels, t), carry):
            prepare(k)
            link = jnp.where(
                link_level.astype(F32) + 1.0 < counts, vm[link_level].astype(F32), 0.0
            )
            inv = 1.0 / (1.0 + outer + link - outer * ratio)
            ratio = link * inv
            inv_out[k] = inv
            q_out[k] = outer * inv
            r_out[k] = ratio
            new.append((ratio, link))
        return tuple(new)

    zero = jnp.zeros((ny, nx), F32)
    lax.fori_loop(0, half, factor, ((zero, zero), (zero, zero)), unroll=UNROLL)

    source = iota((2 * nx, 2 * nx), 0) % nx
    target = iota((2 * nx, 2 * nx), 1)
    for u in range(STEPS):
        group = 2 * u + target // nx
        lane = target % nx
        column = jnp.where(lane < 4, 3 - lane, jnp.where(lane >= nx - 4, nx + 3 - lane, -nx))
        hit = source == GROUP * group + column
        moves_out[u] = jnp.where(hit, 1.0, 0.0).astype(jnp.bfloat16)


def whole(own, halo):
    ny = own.shape[0]
    return extend(own, halo[:ny], halo[ny + 8 :], halo[ny : ny + 8])


def forward_kernel(
    s, obs, count, from_one, from_two, own_planes, own_corners, rows_n, rows_s,
    ep, em, np_, nm, sink, local, inv, q, r, moves,
    ep_halo, em_halo, np_halo, nm_halo, sink_halo, inv_halo, q_halo, r_halo, s_halo,
    middle_out, damp_out, solved_out, counts_out, join_out, send,
    planes, corners, rhs, carries, packed, moved, moved_rows, sides,
):
    levels, ny, nx = s.shape
    half = levels // 2
    per_plane = 128 // GROUP
    plane_count = levels // per_plane
    odd = odd_column()
    merge_halos(odd, from_one, from_two, planes, 0)
    merge_halos(odd, from_one, from_two, corners, planes.shape[0] // 2 * planes.shape[1])

    def rim(index):
        return merge_lines(rows_n[index], rows_s[index])

    count_plane = len(NAMES[:6]) * plane_count
    side_counts = jnp.dot(
        jnp.concatenate([planes[count_plane]] + [roll(corners[plane_count], 4, 0)] * 2, axis=0).astype(
            jnp.bfloat16
        ),
        moves[0, :nx, :nx],
        preferred_element_type=F32,
    )
    count_ext = extend(
        count[...].astype(F32),
        side_counts[:ny],
        rim(levels),
        side_counts[ny : ny + 8],
    )
    east_ext = jnp.minimum(count_ext, east(count_ext))
    counts_out[0] = count_ext
    counts_out[1] = east_ext
    counts_out[2] = step_count(count_ext, 0)
    count_halo = jnp.concatenate(
        [count_ext[:ny, nx:], count_ext[ny:, nx:], count_ext[ny:, :nx]], axis=0
    )
    small_sub = sublane((8, nx))
    north_rows = jnp.where(small_sub == 7, counts_out[2, ny:, :nx], 0.0)
    lane = iota((ny, nx), 1)
    per_half = per_plane // 2

    strip = (ny + 8, nx)
    place = iota(strip, 1) % GROUP
    low = place < 4
    groups = iota(strip, 1) // GROUP
    from_top = groups % 2 == 0
    strip_sub = sublane(strip)

    def columns(p, carry):
        t = p * per_half + groups // 2
        level = jnp.where(from_top, t, levels - 1 - t).astype(F32)
        link_level = jnp.where(from_top, t, levels - 2 - t).astype(F32)

        def side_and_corner(a, c):
            return jnp.concatenate([a, c], axis=0)

        def strips(west):
            def pick(halo, own):
                near_side = low[: halo.shape[0]]
                return jnp.where(near_side, halo, own) if west else jnp.where(near_side, own, halo)

            x = unpack_rows(
                pick(corners[p], own_corners[p]),
                pick(corners[plane_count + p], own_corners[plane_count + p]),
            )
            side = {}
            for a, name in enumerate(NAMES[:6]):
                at = a * plane_count + p
                side[name] = pick(planes[at], own_planes[at])
            for name in NAMES[:4] + NAMES[5:6]:
                x[name] = side_and_corner(side[name], x[name])
            counts = side_and_corner(
                pick(planes[count_plane], own_planes[count_plane]),
                roll(pick(corners[plane_count + p], own_corners[plane_count + p]), 4, 0),
            )
            state = x["s"]
            open_east = level < step_count(counts, 1)
            open_north = (level < step_count(counts, 0)) & (
                (strip_sub < ny) | (strip_sub == ny + 7)
            )
            ep_s = jnp.where(open_east, 0.5 * x["es"] + x["mix"], 0.0)
            em_s = jnp.where(open_east, 0.5 * x["es"] - x["mix"], 0.0)
            np_s = jnp.where(open_north, 0.5 * x["ns"] + x["mix"], 0.0)
            nm_s = jnp.where(open_north, 0.5 * x["ns"] - x["mix"], 0.0)
            sink_s = jnp.where(level[:ny] < counts[:ny], side["relax"], 0.0)
            link = jnp.where(link_level + 1.0 < counts, x["vm"], 0.0)
            fe = ep_s * state + em_s * shift_up(state, 1)
            fe_west = shift_down(fe, 1)
            fn = np_s * state + nm_s * shift_up(state, 0)
            base = side_and_corner(side["s"] - sink_s * jnp.tanh(side["s"]), x["base"])
            right = base - (fe - fe_west) - (fn - shift_down(fn, 0))
            return (right, link, np_s, nm_s, ep_s, em_s, sink_s, state), fe, fe_west

        western, through_west, _ = strips(True)
        eastern, _, through_east = strips(False)
        seam = jnp.where(place == 3, through_west, through_east)
        both = [jnp.where(low[: a.shape[0]], a, b) for a, b in zip(western, eastern)]
        right, link, np_c, nm_c = (x[ny:] for x in both[:4])
        corner = pair_rows(right, link)
        corner = jnp.where((small_sub == 3) | (small_sub == 4), roll(seam[ny:], 4, 0), corner)
        corner = jnp.where(small_sub == 5, roll(np_c, 6, 0), corner)
        corner = jnp.where(small_sub == 6, roll(nm_c, 7, 0), corner)
        both = [x[:ny] for x in both]
        near_seam = planes[NAMES.index("relax") * plane_count + p]
        further = planes[NAMES.index("ns") * plane_count + p]
        side_place = place[:ny]
        seen = jnp.where(side_place < 3, roll(further, 2, 1), roll(near_seam, 3, 1))
        beyond = jnp.where(side_place > 4, roll(further, -2, 1), roll(near_seam, -3, 1))
        seen = jnp.where(side_place < 4, seen, beyond)
        both = both[:2] + [seam[:ny], seen] + both[2:] + [jnp.concatenate([corner] * 2, axis=0)]
        for i, x in enumerate(both):
            split(p, i * ny, x)
        return carry

    def split(p, at, x):
        for h, y in enumerate((x, roll(x, nx // 2, 1))):
            high = y.astype(jnp.bfloat16)
            packed[2 * p + h, at : at + ny, :nx] = high
            packed[2 * p + h, at : at + ny, nx:] = (y - high.astype(F32)).astype(jnp.bfloat16)

    lax.fori_loop(0, plane_count, columns, 0, unroll=plane_count)

    def unpack(u):
        move = moves[u]

        def place_both(m, carry):
            out = jnp.dot(packed[m], move, preferred_element_type=F32)
            t = m * STEPS + u
            for j, k in enumerate((t, levels - 1 - t)):
                x = out[:, j * nx : (j + 1) * nx]
                np_x, nm_x, ep_x, em_x, sink_x, s_x, corner = (
                    x[i * ny : (i + 1) * ny] for i in range(4, 11)
                )
                corner = corner[:8]
                moved[k] = x[: 4 * ny]
                moved_rows[k] = corner
                ep_halo[k, :ny] = ep_x
                em_halo[k, :ny] = em_x
                np_halo[k, :ny] = np_x
                nm_halo[k, :ny] = nm_x
                np_halo[k, ny : ny + 8] = roll(corner, 2, 0)
                nm_halo[k, ny : ny + 8] = roll(corner, 1, 0)
                sink_halo[k] = sink_x
                s_halo[k, :ny] = s_x
            return carry

        lax.fori_loop(0, 2 * plane_count, place_both, 0, unroll=2 * plane_count)

    for u in range(STEPS):
        unpack(u)

    def prepare(m, u, j, k, link_level):
        t = m * STEPS + u
        x = unpack_line(rim(2 * t + j))
        level = k.astype(F32)
        row = x["s"]
        open_north = level < north_rows
        np_r = jnp.where(open_north, 0.5 * x["ns"] + x["mix"], 0.0)
        nm_r = jnp.where(open_north, 0.5 * x["ns"] - x["mix"], 0.0)
        link_r = jnp.where(link_level.astype(F32) + 1.0 < count_halo[ny + 8 :], x["vm"], 0.0)
        corner = moved_rows[k]
        right, link, seam = (moved[k, i * ny : (i + 1) * ny] for i in range(3))
        seam_rows = roll(corner, 4, 0)
        np_halo[k, ny + 8 :] = np_r
        nm_halo[k, ny + 8 :] = nm_r
        s_halo[k, ny + 8 :] = row

        own = s[k]
        last, first = lane == nx - 1, lane == 0
        through = jnp.where(first[:8], seam_rows, jnp.where(last[:8], -seam_rows, 0.0))
        fn = np_r * row + nm_r * shift_up(own[:8], 0)
        top = np_[k, ny - 8 :] * own[ny - 8 :]
        cross = nm[k, ny - 8 :] * shift_up(row, 0)
        from_block = jnp.where(small_sub == 0, shift_down(top + cross, 0), 0.0)
        right_r = x["base"] + through - (fn - from_block)

        inner = local[k] + jnp.where(first, seam, jnp.where(last, -seam, 0.0))
        low_rows = inner[:8] + jnp.where(small_sub == 0, shift_down(fn, 0), 0.0)
        high_rows = inner[ny - 8 :] - jnp.where(small_sub == 7, cross, 0.0)
        between = [inner[8 : ny - 8]] if ny > 16 else []
        inner = jnp.concatenate([low_rows] + between + [high_rows], axis=0)
        halo = jnp.concatenate([right, corner, right_r], axis=0)
        return inner, halo, jnp.concatenate([link, roll(corner, 6, 0), link_r], axis=0)

    def factor(m, carry):
        for u in range(STEPS):
            carry = factor_step(m, u, carry)
        return carry

    def factor_step(m, u, carry):
        t = m * STEPS + u
        new = []
        for j, (k, link_level) in enumerate(level_pair(levels, t)):
            ratio, c_own, c_halo, outer = carry[j]
            own, halo, link = prepare(m, u, j, k, link_level)
            inv_h = 1.0 / (1.0 + outer + link - outer * ratio)
            q_h = outer * inv_h
            ratio = link * inv_h
            c_own = own * inv[k] + q[k] * c_own
            c_halo = halo * inv_h + q_h * c_halo
            inv_halo[k] = inv_h
            q_halo[k] = q_h
            r_halo[k] = ratio
            carries[k] = whole(c_own, c_halo)
            new.append((ratio, c_own, c_halo, link))
        return tuple(new)

    zero = jnp.zeros(count_halo.shape, F32)
    begin = (zero, jnp.zeros((ny, nx), F32), zero, zero)
    (r_top, top_own, top_halo, _), (r_low, low_own, low_halo, _) = lax.fori_loop(
        0, half // STEPS, factor, (begin, begin), unroll=2
    )
    c_top, c_low = whole(top_own, top_halo), whole(low_own, low_halo)
    join = 1.0 / (1.0 - whole(r[half - 1], r_top) * whole(r[half], r_low))
    join_out[...] = join

    def ext(own, halo):
        return lambda k: whole(own[k], halo[k])

    def inner(own, halo):
        return lambda k: extend(own[k], halo[k, :ny])

    def spread(state, ep, em, np_, nm):
        fe = ep * state + em * east(state)
        fn = np_ * state + nm * shift_up(state, 0)
        return (fe - west(fe)) + (fn - shift_down(fn, 0))

    def both(one):
        def use(t, m, u, top, low):
            one(t, top, m, u, 0)
            one(levels - 1 - t, low, m, u, 1)

        return use

    def to_second(k, x, m, u, j):
        middle_out[k] = x
        state = x[:ny]
        squeeze = jnp.tanh(state)
        loss = inner(sink, sink_halo)(k)
        damp_out[k] = 1.0 - loss * (1.0 - squeeze * squeeze)
        fields = (ext(ep, ep_halo), ext(em, em_halo), ext(np_, np_halo), ext(nm, nm_halo))
        flow = spread(x, *(field(k) for field in fields))
        rhs[k] = state - flow[:ny] - loss * squeeze

    solve_outward(levels, (c_top, c_low), ext(r, r_halo), join, carries, both(to_second))

    main = carries.at[:, :ny]
    inv_q = inner(inv, inv_halo), inner(q, q_halo)
    ratio = inner(r, r_halo)
    ends = solve_inward(levels, lambda k: rhs[k], inv_q, main)

    def to_adjoint(k, x, m, u, j):
        seen = extend(obs[k].astype(F32), moved[k, 3 * ny :])
        rhs[k] = jnp.where(k.astype(F32) < count_ext[:ny], x - seen, 0.0)

    solve_outward(levels, ends, ratio, join[:ny], main, both(to_adjoint))
    ends = solve_inward(levels, lambda k: rhs[k], inv_q, main)

    def rim_part(k, solved):
        solved_out[k] = solved
        x = edge_rows(solved)
        main, side = halves(x)
        rows_of = lambda ref: edge_rows(ref[k])
        part, _ = pull_x(main, side, rows_of(ep), rows_of(em), edge_rows(em_halo[k, :ny]))
        part = part + main * edge_rows(damp_out[k, :, :nx])
        gn = shift_up(main, 0) - main
        sub = sublane(main.shape)
        part = part + jnp.where(
            sub == 0,
            rows_of(np_) * gn,
            jnp.where(sub == 7, shift_down(rows_of(nm) * gn, 0), 0.0),
        )
        return jnp.concatenate([pair_rows(main, part), side], axis=1)

    lane8 = iota((8, nx), 1)

    def to_send(t, m, u, top, low):
        pair = two_levels(rim_part(t, top), rim_part(levels - 1 - t, low))
        send[t] = pair[:, :nx]
        before = jnp.zeros((8, nx), F32) if u == STEPS - 1 else sides[m]
        moved = roll(pair[:, nx:], 2 * u + 1, 1)
        sides[m] = jnp.where(lane8 // 2 == u, moved, before)

    solve_outward(levels, ends, ratio, join[:ny], main, to_send)
    both_sides = sides[0]
    for m in range(1, half // STEPS):
        place = m * 2 * STEPS
        both_sides = jnp.where(lane8 < place, both_sides, roll(sides[m], place, 1))
    send[half] = both_sides


def inner_kernel(
    ep, em, np_, nm, ep_halo, em_halo, np_halo, nm_halo, damp, middle, solved, counts,
    s, s_halo, part_out, late_out, run_out, rise_out,
):
    levels, ny, width = solved.shape
    nx = width // 2
    sub = sublane((ny, width))
    inside = sub < ny - 1

    def inner(k, carry):
        x = solved[k]
        state = middle[k]
        field = lambda own, halo: extend(own[k], halo[k, :ny])
        part, ge = part_of_pull(x, field(ep, ep_halo), field(em, em_halo), damp[k])
        gn = jnp.where(inside, shift_up(x, 0) - x, 0.0)
        part_out[k] = (
            part + field(np_, np_halo) * gn + shift_down(field(nm, nm_halo) * gn, 0)
        )
        level = k.astype(F32)
        open_east = level < counts[1, :ny, :nx]
        open_north = level < counts[2, :ny, :nx]

        def slopes(state):
            run = (east(state[:ny]) - state[:ny])[:, :nx]
            rise = shift_up(state[:, :nx], 0)[:ny] - state[:ny, :nx]
            return jnp.where(open_east, run, 0.0), jnp.where(open_north, rise, 0.0)

        run, rise = slopes(state)
        late_out[k] = ge[:, :nx] * run + gn[:, :nx] * rise
        run_out[k], rise_out[k] = slopes(whole(s[k], s_halo[k]))
        return carry

    lax.fori_loop(0, levels, inner, 0, unroll=UNROLL)


def backward_kernel(
    ep, em, np_, nm, inv, q, r, ep_halo, em_halo, np_halo, nm_halo, inv_halo, q_halo, r_halo,
    middle, damp, solved, counts, join, part, late, run, rise, rows_n, rows_s,
    adjoint_out, gradient_out, carries, adjoint, gradient, sides, sent,
):
    levels, ny, width = solved.shape
    nx = width // 2
    half = levels // 2
    sub = sublane((8, width))

    side = merge_rows(rows_n[half], rows_s[half])
    for m in range(half // STEPS):
        sides[m] = roll(side, -2 * STEPS * m, 1)

    def rims(m, u):
        t = m * STEPS + u
        line = merge_rows(rows_n[t], rows_s[t])
        corner = roll(sides[m], -1 - 2 * u, 1)
        both = jnp.concatenate([line, corner], axis=1)
        return both, roll(both, 4, 0)

    def across(k, rim):
        inner = part[k]
        near_part = roll(rim, 6, 0)
        south = solved[k, :8] - shift_down(rim, 0)
        north = shift_up(rim, 0) - solved[k, ny - 8 :]
        north_plus = whole(np_[k], np_halo[k])
        north_minus = whole(nm[k], nm_halo[k])
        np_rim, nm_rim = north_plus[ny:], north_minus[ny:]
        np_top, nm_top = north_plus[ny - 8 : ny], north_minus[ny - 8 : ny]
        low = inner[:8] + jnp.where(sub == 0, shift_down(nm_rim, 0) * south, 0.0)
        high = inner[ny - 8 :] + jnp.where(sub == 7, np_top * north, 0.0)
        outer = near_part + jnp.where(
            sub == 0, shift_down(nm_top * north, 0), np_rim * shift_up(south, 0)
        )
        rise = (shift_up(middle[k, ny:], 0) - middle[k, ny - 8 : ny])[:, :nx]
        open_north = (sub[:, :nx] == 7) & (k.astype(F32) < counts[2, ny - 8 : ny, :nx])
        extra = jnp.where(open_north, north[:, :nx] * rise, 0.0)
        gradient[k, : ny - 8] = late[k, : ny - 8]
        gradient[k, ny - 8 :] = late[k, ny - 8 :] + extra
        middle_rows = [inner[8 : ny - 8]] if ny > 16 else []
        return jnp.concatenate([low, *middle_rows, high, outer], axis=0)

    def late_steps(m, carry):
        for u in range(STEPS):
            t = m * STEPS + u
            new = []
            for k, rim, last in zip((t, levels - 1 - t), rims(m, u), carry):
                c = across(k, rim) * whole(inv[k], inv_halo[k])
                c = c + whole(q[k], q_halo[k]) * last
                carries[k] = c
                new.append(c)
            carry = tuple(new)
        return carry

    zero = jnp.zeros(carries.shape[1:], F32)
    ends = lax.fori_loop(0, half // STEPS, late_steps, (zero, zero), unroll=2)

    def early(k, x):
        main, side = halves(x[:ny])
        flow, ge = pull_x(main, side, ep[k], em[k], em_halo[k, :ny])
        result = main * damp[k] + flow
        column = x[:, :nx]
        gn = shift_up(column, 0) - column
        minus = jnp.concatenate([nm[k], nm_halo[k, ny + 8 :]], axis=0)
        result = result + np_[k] * gn[:ny] + shift_down(minus * gn, 0)[:ny]
        adjoint[k] = result
        gradient[k] = -(gradient[k] + ge * run[k] + gn[:ny] * rise[k])

    def copies(p):
        out = []
        for i, begin in enumerate((p * UNROLL, levels - (p + 1) * UNROLL)):
            place = pl.ds(begin, UNROLL)
            for j, (source, target) in enumerate(
                ((adjoint, adjoint_out), (gradient, gradient_out))
            ):
                out.append(
                    pltpu.make_async_copy(
                        source.at[place], target.at[place], sent.at[p, 2 * i + j]
                    )
                )
        return out

    high, low = ends
    steps = half // UNROLL
    ratio = lambda k: whole(r[k], r_halo[k])
    last = (low + ratio(half) * high) * join[...], (high + ratio(half - 1) * low) * join[...]

    def block(i, last):
        p = steps - 1 - i
        for g in range(UNROLL - 1, -1, -1):
            t = p * UNROLL + g
            new = []
            for k, x in ((t, last[0]), (levels - 1 - t, last[1])):
                x = carries[k] + ratio(k) * x
                early(k, x)
                new.append(x)
            last = tuple(new)
        for copy in copies(p):
            copy.start()
        return last

    lax.fori_loop(0, steps, block, last)
    for p in range(steps):
        for copy in copies(p):
            copy.wait()


def ring(axis, distance):
    count = lax.axis_size(axis)
    return [(i, (i + distance) % count) for i in range(count)]


def both_ways(x):
    from_north = lax.ppermute(x, "ty", ring("ty", -1))
    if lax.axis_size("ty") == 2:
        return from_north, from_north
    return from_north, lax.ppermute(x, "ty", ring("ty", 1))


def swap(x, phase):
    nx = lax.axis_size("tx")
    return lax.ppermute(
        x, "tx", [(i, (i + 1) % nx if i % 2 == phase else (i - 1) % nx) for i in range(nx)]
    )


def per_device(
    tracer_start,
    observed,
    east_speed,
    north_speed,
    mixing,
    vertical_mixing,
    relax_rate,
    level_count,
    face_east,
    face_north,
):
    levels, ny, nx = tracer_start.shape
    per_plane = 128 // GROUP
    plane_count = levels // per_plane
    pairs = (len(NAMES[:6]) * plane_count + 2) // 2
    fields = (
        tracer_start, east_speed, north_speed, mixing, relax_rate, vertical_mixing, observed,
        level_count, face_east, face_north,
    )
    half = levels // 2
    corner_planes = 2 * plane_count
    *fields, corners = call(
        rim_kernel,
        [jax.ShapeDtypeStruct(x.shape, x.dtype) for x in fields]
        + [(corner_planes, 8, nx)],
        [pltpu.SemaphoreType.DMA((10,))],
        *[pltpu.with_memory_space_constraint(x, pltpu.HBM) for x in fields],
        space=HBM,
    )
    corners_n, corners_s = both_ways(corners)
    planes, rows = call(
        column_kernel, [(2 * pairs, ny, nx), (levels + 1, 8, nx)], [], *fields[:8]
    )
    rows_n, rows_s = both_ways(rows)
    packed = (pairs * ny + corner_planes // 2 * 8, nx)
    one, two, own_corners = call(
        halves_kernel, [packed, packed, corners.shape], [],
        planes, corners_n, corners_s,
        cost=pl.CostEstimate(flops=10**10, bytes_accessed=0, transcendentals=0),
    )
    from_two = swap(two, 1)
    from_one = swap(one, 0)
    ext = (levels, ny + 8, 2 * nx)
    block = (levels, ny, 2 * nx)
    own = (levels, ny, nx)
    halo = (levels, ny + 16, nx)
    s, es, ns, mix, relax, vm, obs, count, east, north = fields
    *coefficients, damp, local, inv, q, r, moves = call(
        local_kernel,
        [own] * 10 + [jax.ShapeDtypeStruct((STEPS, 2 * nx, 2 * nx), jnp.bfloat16)],
        [],
        s, es, ns, mix, relax, vm, count, east, north, one,
        cost=pl.CostEstimate(flops=10**9, bytes_accessed=0, transcendentals=0),
    )
    ep, em, np_, nm, sink = coefficients
    outs = call(
        forward_kernel,
        [halo] * 4 + [own] + [halo] * 4 + [ext, block, block, (3,) + ext[1:], ext[1:]]
        + [(half + 1, 8, nx)],
        [
            planes.shape,
            corners.shape,
            block,
            ext,
            pltpu.VMEM((2 * plane_count, 11 * ny, 2 * nx), jnp.bfloat16),
            (levels, 4 * ny, nx),
            (levels, 8, nx),
            (2 * plane_count, 8, nx),
        ],
        s, obs, count, from_one, from_two, planes, own_corners, rows_n, rows_s,
        ep, em, np_, nm, sink, local, inv, q, r, moves,
    )
    ep_h, em_h, np_h, nm_h, _, inv_h, q_h, r_h, s_h, *outs = outs
    middle, late_damp, solved, counts, join, send = outs
    sent_n, sent_s = both_ways(send)
    faces = ep, em, np_, nm
    halo_faces = ep_h, em_h, np_h, nm_h
    part, late, run, rise = call(
        inner_kernel,
        [block] + [own] * 3,
        [],
        *faces, *halo_faces, late_damp, middle, solved, counts, s, s_h,
        cost=pl.CostEstimate(flops=0, bytes_accessed=8 << 20, transcendentals=0),
    )
    adjoint, gradient = call(
        backward_kernel,
        [own] * 2,
        [ext, own, own, (2 * plane_count, 8, nx), pltpu.SemaphoreType.DMA((half // UNROLL, 4))],
        *faces, inv, q, r, *halo_faces, inv_h, q_h, r_h,
        middle, damp, solved, counts, join, part, late, run, rise, sent_n, sent_s,
        out_space=HBM,
    )
    return adjoint, gradient


def solution(mesh):
    block = P(None, "ty", "tx")
    plane = P("ty", "tx")
    return jax.shard_map(
        per_device,
        mesh=mesh,
        in_specs=(block,) * 7 + (plane,) * 3,
        out_specs=(block, block),
        check_vma=False,
    )
```

```python
import functools

import jax
import jax.numpy as jnp
from jax import lax
from jax.experimental import pallas as pl
from jax.experimental.pallas import tpu as pltpu
from jax.sharding import PartitionSpec as P

F32 = jnp.float32
VMEM = pl.BlockSpec(memory_space=pltpu.VMEM)
HBM = pl.BlockSpec(memory_space=pltpu.HBM)
UNROLL = 8
STEPS = 4
GROUP = 8
NAMES = ("s", "es", "ns", "mix", "relax", "vm", "obs")


def call(kernel, outs, scratch, *args, space=VMEM, out_space=VMEM, cost=None):
    def typed(x):
        return x if isinstance(x, jax.ShapeDtypeStruct) else jax.ShapeDtypeStruct(x, F32)

    return pl.pallas_call(
        kernel,
        out_shape=[typed(x) for x in outs],
        in_specs=[space] * len(args),
        out_specs=[out_space] * len(outs),
        scratch_shapes=[pltpu.VMEM(x, F32) if isinstance(x, tuple) else x for x in scratch],
        compiler_params=pltpu.CompilerParams(vmem_limit_bytes=16 << 20),
        cost_estimate=cost,
    )(*args)


def iota(shape, dim):
    return lax.broadcasted_iota(jnp.int32, shape, dim)


def roll(x, shift, axis):
    if isinstance(shift, int):
        shift = shift % x.shape[axis]
        if shift == 0:
            return x
    return pltpu.roll(x, shift, axis)


def odd_column():
    return lax.rem(lax.axis_index("tx"), 2) == 1


def level_of(ref, name, level):
    if name == "vm":
        level = jnp.minimum(level, ref.shape[0] - 1)
    return ref[level].astype(F32)


def edge_rows(block):
    return jnp.where(iota((8, block.shape[1]), 0) < 4, block[:8], block[-8:])


def sublane(shape):
    return iota(shape, 0)


def step_count(counts, axis):
    return jnp.minimum(counts, shift_up(counts, axis))


def pair_rows(first, second):
    sub = sublane(first.shape)
    return jnp.where((sub == 1) | (sub == 2), roll(second, 2, 0), first)


def level_pair(levels, t):
    return (t, t), (levels - 1 - t, levels - 2 - t)


def in_all_groups(x):
    group = iota(x.shape, 1) // GROUP
    out = jnp.zeros(x.shape, F32)
    for g in range(x.shape[1] // GROUP):
        out = jnp.where(group == g, roll(x, GROUP * g + 4, 1), out)
    return out


def pack_rows(get, counts, level):
    tile = {name: edge_rows(get(name)) for name in NAMES[:6]}
    s = tile["s"]
    sub = sublane(s.shape)
    open_north = level < step_count(counts, 0)
    fn = jnp.where(
        open_north,
        (0.5 * tile["ns"] + tile["mix"]) * s + (0.5 * tile["ns"] - tile["mix"]) * shift_up(s, 0),
        0.0,
    )
    sink = jnp.where(level < counts, tile["relax"], 0.0)
    inner = jnp.where(sub == 0, -fn, jnp.where(sub == 7, shift_down(fn, 0), 0.0))
    base = s - sink * jnp.tanh(s) + inner
    first = pair_rows(s, base)
    first = jnp.where((sub == 3) | (sub == 4), roll(tile["es"], 4, 0), first)
    first = jnp.where((sub == 5) | (sub == 6), roll(tile["mix"], 6, 0), first)
    lane = iota(s.shape, 1)
    fe = (0.5 * tile["es"] + tile["mix"]) * s
    fe = fe + (0.5 * tile["es"] - tile["mix"]) * shift_up(s, 1)
    fe = jnp.where((level < step_count(counts, 1)) & (lane < s.shape[1] - 1), fe, 0.0)
    line = pair_rows(s, base - (fe - shift_down(fe, 1)))
    line = jnp.where((sub == 3) | (sub == 4), roll(tile["vm"], 4, 0), line)
    line = jnp.where(sub == 5, roll(tile["ns"], 6, 0), line)
    line = jnp.where(sub == 6, roll(tile["mix"], 7, 0), line)
    return line, first, pair_rows(tile["vm"], tile["ns"])


def merge_lines(north, south):
    sub = sublane(north.shape)
    return jnp.where((sub == 0) | (sub == 2) | (sub == 4), north, south)


def unpack_line(line):
    return {
        "s": line,
        "base": roll(line, 6, 0),
        "vm": roll(line, 4, 0),
        "ns": roll(line, 2, 0),
        "mix": roll(line, 1, 0),
    }


def unpack_rows(first, second):
    return {
        "s": first,
        "base": roll(first, 6, 0),
        "es": roll(first, 4, 0),
        "mix": roll(first, 2, 0),
        "vm": second,
        "ns": roll(second, 6, 0),
    }


def two_levels(x, y):
    sub = sublane(x.shape)
    return jnp.where((sub >= 3) & (sub <= 6), roll(y, 4, 0), x)


def shift_up(x, axis):
    return roll(x, -1, axis)


def shift_down(x, axis):
    return roll(x, 1, axis)


def rim_kernel(*args):
    fields = args[:10]
    s, es, ns, mix, relax, vm, obs, count, *_ = kept = args[10:20]
    corners, arrived = args[20:]
    copies = [pltpu.make_async_copy(fields[i], kept[i], arrived.at[i]) for i in range(10)]
    first = (7, 0, 1, 2, 3, 4, 5)
    rest = (6, 8, 9)
    for i in first + rest:
        copies[i].start()
    for i in first:
        copies[i].wait()
    refs = dict(zip(NAMES, (s, es, ns, mix, relax, vm, obs)))
    levels = s.shape[0]
    per_plane = 128 // GROUP
    small = (8, s.shape[2])
    group = iota(small, 1) // GROUP
    half = per_plane // 2
    plane_count = levels // per_plane
    counts = edge_rows(count[...].astype(F32))
    sub = sublane(small)

    def rims(p, carry):
        acc = jnp.zeros(small, F32)
        late = jnp.zeros(small, F32)
        for g in range(half):
            t = p * half + g
            for j, (k, link) in enumerate(level_pair(levels, t)):
                _, first, second = pack_rows(
                    lambda name: level_of(refs[name], name, link if name == "vm" else k),
                    counts,
                    k.astype(F32),
                )
                place = 2 * g + j
                acc = jnp.where(group == place, roll(first, GROUP * place + 4, 1), acc)
                second = jnp.where((sub == 3) | (sub == 4), roll(counts, 4, 0), second)
                late = jnp.where(group == place, roll(second, GROUP * place + 4, 1), late)
        corners[p] = acc
        corners[plane_count + p] = late
        return carry

    lax.fori_loop(0, plane_count, rims, 0)
    for i in rest:
        copies[i].wait()


def column_kernel(s, es, ns, mix, relax, vm, obs, count, planes, rows):
    refs = dict(zip(NAMES, (s, es, ns, mix, relax, vm, obs)))
    levels = s.shape[0]
    per_plane = 128 // GROUP
    plane_count = levels // per_plane
    shape = s.shape[1:]
    group = iota(shape, 1) // GROUP

    place = iota(shape, 1) % GROUP
    counts = edge_rows(count[...].astype(F32))
    rows[levels] = counts

    def lines(t, carry):
        for j, (k, link) in enumerate(level_pair(levels, t)):
            rows[2 * t + j], _, _ = pack_rows(
                lambda name: level_of(refs[name], name, link if name == "vm" else k),
                counts,
                k.astype(F32),
            )
        return carry

    lax.fori_loop(0, levels // 2, lines, 0, unroll=UNROLL)

    def columns(p, carry):
        packed = []
        for name in NAMES:
            acc = jnp.zeros(shape, F32)
            for g in range(per_plane):
                pair = level_pair(levels, p * (per_plane // 2) + g // 2)
                x = refs[name][pair[g % 2][name == "vm"]].astype(F32)
                acc = jnp.where(group == g, roll(x, GROUP * g + 4, 1), acc)
            packed.append(acc)
        seen = packed.pop()
        for name, distance in (("ns", 2), ("relax", 3)):
            i = NAMES.index(name)
            x = jnp.where(place == 0, roll(seen, -distance, 1), packed[i])
            packed[i] = jnp.where(place == GROUP - 1, roll(seen, distance, 1), x)
        for a, x in enumerate(packed):
            planes[a * plane_count + p] = x
        return carry

    lax.fori_loop(0, plane_count, columns, 0)
    total = len(NAMES[:6]) * plane_count
    planes[total] = in_all_groups(count[...].astype(F32))
    for p in range(total + 1, planes.shape[0]):
        planes[p] = jnp.zeros(shape, F32)


def merge_rows(north, south):
    return jnp.where(sublane(north.shape) % 2 == 0, north, south)


def halves_kernel(planes, corners_n, corners_s, one, two, kept):
    odd = odd_column()
    pairs = planes.shape[0] // 2
    ny = planes.shape[1]

    def put(place, x, y):
        low = iota(x.shape, 1) % GROUP < 4
        to_east = jnp.where(low, x, roll(y, 4, 1))
        to_west = jnp.where(low, roll(x, -4, 1), y)
        one[place] = jnp.where(odd, to_west, to_east)
        two[place] = jnp.where(odd, to_east, to_west)

    for h in range(pairs):
        put(pl.ds(h * ny, ny), planes[2 * h], planes[2 * h + 1])

    count = corners_n.shape[0]
    def corner(p):
        return merge_rows(corners_n[p], corners_s[p])

    for h in range(count // 2):
        x, y = corner(2 * h), corner(2 * h + 1)
        kept[2 * h] = x
        kept[2 * h + 1] = y
        put(pl.ds(pairs * ny + h * 8, 8), x, y)


def halves(x):
    nx = x.shape[1] // 2
    return x[:, :nx], x[:, nx:]


def east(x):
    main, side = halves(x)
    lane = iota(main.shape, 1)
    return jnp.concatenate(
        [
            jnp.where(lane == lane.shape[1] - 1, side, roll(main, -1, 1)),
            jnp.where(lane == 0, main, roll(side, 1, 1)),
        ],
        axis=1,
    )


def west(x):
    main, side = halves(x)
    lane = iota(main.shape, 1)
    return jnp.concatenate(
        [
            jnp.where(lane == 0, side, roll(main, 1, 1)),
            jnp.where(lane == lane.shape[1] - 1, main, roll(side, -1, 1)),
        ],
        axis=1,
    )


def pull_x(main, side, ep, em, em_side):
    lane = iota(main.shape, 1)
    ge = jnp.where(lane == lane.shape[1] - 1, side, roll(main, -1, 1)) - main
    return ep * ge + jnp.where(lane == 0, em_side * (main - side), roll(em * ge, 1, 1)), ge


def extend(main, side, rows=None, corners=None):
    top = jnp.concatenate([main, side], axis=1)
    if rows is None:
        return top
    return jnp.concatenate([top, jnp.concatenate([rows, corners], axis=1)], axis=0)


def solve_inward(levels, get, inv_q, carries):
    half = levels // 2
    inv, q = inv_q

    def step(t, carry):
        new = []
        for k, last in ((t, carry[0]), (levels - 1 - t, carry[1])):
            c = get(k) * inv(k) + q(k) * last
            carries[k] = c
            new.append(c)
        return tuple(new)

    zero = jnp.zeros(carries.shape[1:], F32)
    return lax.fori_loop(0, half, step, (zero, zero), unroll=UNROLL)


def solve_outward(levels, ends, ratio, join, carries, use):
    half = levels // 2
    high, low = ends
    upper = (high + ratio(half - 1) * low) * join
    lower = (low + ratio(half) * high) * join

    def block(i, last):
        m = half // STEPS - 1 - i
        for u in range(STEPS - 1, -1, -1):
            t = m * STEPS + u
            new = []
            for k, x in ((t, last[0]), (levels - 1 - t, last[1])):
                new.append(carries[k] + ratio(k) * x)
            use(t, m, u, *new)
            last = tuple(new)
        return last

    lax.fori_loop(0, half // STEPS, block, (lower, upper), unroll=2)


def merge_halos(odd, from_one, from_two, planes, start):
    size = planes.shape[1]
    low = iota(planes.shape[1:], 1) % GROUP < 4
    for h in range(planes.shape[0] // 2):
        place = pl.ds(start + h * size, size)
        a, b = from_one[place], from_two[place]
        west = jnp.where(odd, a, b)
        east = jnp.where(odd, b, a)
        planes[2 * h] = jnp.where(low, west, roll(east, 4, 1))
        planes[2 * h + 1] = jnp.where(low, roll(west, -4, 1), east)


def part_of_pull(x, ep, em, damp):
    ge = east(x) - x
    return x * damp + ep * ge + west(em * ge), ge


def local_kernel(
    s, es, ns, mix, relax, vm, count, east, north, after,
    ep_out, em_out, np_out, nm_out, sink_out, damp_out, local_out, inv_out, q_out, r_out,
    moves_out,
):
    levels, ny, nx = s.shape
    half = levels // 2
    counts = count[...].astype(F32)
    east_count = east[...].astype(F32)
    north_count = north[...].astype(F32)
    lane = iota((ny, nx), 1)
    sub = sublane((ny, nx))

    def prepare(k):
        level = k.astype(F32)
        state = s[k]
        diffusion = mix[k].astype(F32)
        speed_east = 0.5 * es[k].astype(F32)
        speed_north = 0.5 * ns[k].astype(F32)
        open_east = level < east_count
        open_north = level < north_count
        ep = jnp.where(open_east, speed_east + diffusion, 0.0)
        em = jnp.where(open_east, speed_east - diffusion, 0.0)
        np_ = jnp.where(open_north, speed_north + diffusion, 0.0)
        nm = jnp.where(open_north, speed_north - diffusion, 0.0)
        sink = jnp.where(level < counts, relax[k].astype(F32), 0.0)
        squeeze = jnp.tanh(state)
        ep_out[k] = ep
        em_out[k] = em
        np_out[k] = np_
        nm_out[k] = nm
        sink_out[k] = sink
        damp_out[k] = 1.0 - sink * (1.0 - squeeze * squeeze)
        fe = ep * state + em * shift_up(state, 1)
        fe = jnp.where(lane == nx - 1, 0.0, fe)
        fn = np_ * state + nm * jnp.where(sub == ny - 1, 0.0, shift_up(state, 0))
        flow = fe - shift_down(fe, 1)
        flow = flow + (fn - jnp.where(sub == 0, 0.0, shift_down(fn, 0)))
        local_out[k] = state - sink * squeeze - flow

    def factor(t, carry):
        new = []
        for (k, link_level), (ratio, outer) in zip(level_pair(levels, t), carry):
            prepare(k)
            link = jnp.where(
                link_level.astype(F32) + 1.0 < counts, vm[link_level].astype(F32), 0.0
            )
            inv = 1.0 / (1.0 + outer + link - outer * ratio)
            ratio = link * inv
            inv_out[k] = inv
            q_out[k] = outer * inv
            r_out[k] = ratio
            new.append((ratio, link))
        return tuple(new)

    zero = jnp.zeros((ny, nx), F32)
    lax.fori_loop(0, half, factor, ((zero, zero), (zero, zero)), unroll=UNROLL)

    source = iota((2 * nx, 2 * nx), 0) % nx
    target = iota((2 * nx, 2 * nx), 1)
    for u in range(STEPS):
        group = 2 * u + target // nx
        lane = target % nx
        column = jnp.where(lane < 4, 3 - lane, jnp.where(lane >= nx - 4, nx + 3 - lane, -nx))
        hit = source == GROUP * group + column
        moves_out[u] = jnp.where(hit, 1.0, 0.0).astype(jnp.bfloat16)


def whole(own, halo):
    ny = own.shape[0]
    return extend(own, halo[:ny], halo[ny + 8 :], halo[ny : ny + 8])


def forward_kernel(
    s, obs, count, from_one, from_two, own_planes, own_corners, rows_n, rows_s,
    ep, em, np_, nm, sink, local, inv, q, r, moves,
    ep_halo, em_halo, np_halo, nm_halo, sink_halo, inv_halo, q_halo, r_halo, s_halo,
    middle_out, damp_out, solved_out, counts_out, join_out, send,
    planes, corners, rhs, carries, packed, moved, moved_rows, sides,
):
    levels, ny, nx = s.shape
    half = levels // 2
    per_plane = 128 // GROUP
    plane_count = levels // per_plane
    odd = odd_column()
    merge_halos(odd, from_one, from_two, planes, 0)
    merge_halos(odd, from_one, from_two, corners, planes.shape[0] // 2 * planes.shape[1])

    def rim(index):
        return merge_lines(rows_n[index], rows_s[index])

    count_plane = len(NAMES[:6]) * plane_count
    side_counts = jnp.dot(
        jnp.concatenate([planes[count_plane]] + [roll(corners[plane_count], 4, 0)] * 2, axis=0).astype(
            jnp.bfloat16
        ),
        moves[0, :nx, :nx],
        preferred_element_type=F32,
    )
    count_ext = extend(
        count[...].astype(F32),
        side_counts[:ny],
        rim(levels),
        side_counts[ny : ny + 8],
    )
    east_ext = jnp.minimum(count_ext, east(count_ext))
    counts_out[0] = count_ext
    counts_out[1] = east_ext
    counts_out[2] = step_count(count_ext, 0)
    count_halo = jnp.concatenate(
        [count_ext[:ny, nx:], count_ext[ny:, nx:], count_ext[ny:, :nx]], axis=0
    )
    small_sub = sublane((8, nx))
    north_rows = jnp.where(small_sub == 7, counts_out[2, ny:, :nx], 0.0)
    lane = iota((ny, nx), 1)
    per_half = per_plane // 2

    strip = (ny + 8, nx)
    place = iota(strip, 1) % GROUP
    low = place < 4
    groups = iota(strip, 1) // GROUP
    from_top = groups % 2 == 0
    strip_sub = sublane(strip)

    def columns(p, carry):
        t = p * per_half + groups // 2
        level = jnp.where(from_top, t, levels - 1 - t).astype(F32)
        link_level = jnp.where(from_top, t, levels - 2 - t).astype(F32)

        def side_and_corner(a, c):
            return jnp.concatenate([a, c], axis=0)

        def strips(west):
            def pick(halo, own):
                near_side = low[: halo.shape[0]]
                return jnp.where(near_side, halo, own) if west else jnp.where(near_side, own, halo)

            x = unpack_rows(
                pick(corners[p], own_corners[p]),
                pick(corners[plane_count + p], own_corners[plane_count + p]),
            )
            side = {}
            for a, name in enumerate(NAMES[:6]):
                at = a * plane_count + p
                side[name] = pick(planes[at], own_planes[at])
            for name in NAMES[:4] + NAMES[5:6]:
                x[name] = side_and_corner(side[name], x[name])
            counts = side_and_corner(
                pick(planes[count_plane], own_planes[count_plane]),
                roll(pick(corners[plane_count + p], own_corners[plane_count + p]), 4, 0),
            )
            state = x["s"]
            open_east = level < step_count(counts, 1)
            open_north = (level < step_count(counts, 0)) & (
                (strip_sub < ny) | (strip_sub == ny + 7)
            )
            ep_s = jnp.where(open_east, 0.5 * x["es"] + x["mix"], 0.0)
            em_s = jnp.where(open_east, 0.5 * x["es"] - x["mix"], 0.0)
            np_s = jnp.where(open_north, 0.5 * x["ns"] + x["mix"], 0.0)
            nm_s = jnp.where(open_north, 0.5 * x["ns"] - x["mix"], 0.0)
            sink_s = jnp.where(level[:ny] < counts[:ny], side["relax"], 0.0)
            link = jnp.where(link_level + 1.0 < counts, x["vm"], 0.0)
            fe = ep_s * state + em_s * shift_up(state, 1)
            fe_west = shift_down(fe, 1)
            fn = np_s * state + nm_s * shift_up(state, 0)
            base = side_and_corner(side["s"] - sink_s * jnp.tanh(side["s"]), x["base"])
            right = base - (fe - fe_west) - (fn - shift_down(fn, 0))
            return (right, link, np_s, nm_s, ep_s, em_s, sink_s, state), fe, fe_west

        western, through_west, _ = strips(True)
        eastern, _, through_east = strips(False)
        seam = jnp.where(place == 3, through_west, through_east)
        seam = jnp.where(place == 5, roll(eastern[7], 1, 1), seam)
        both = [jnp.where(low[: a.shape[0]], a, b) for a, b in zip(western, eastern)]
        right, link, np_c, nm_c = (x[ny:] for x in both[:4])
        corner = pair_rows(right, link)
        corner = jnp.where((small_sub == 3) | (small_sub == 4), roll(seam[ny:], 4, 0), corner)
        corner = jnp.where(small_sub == 5, roll(np_c, 6, 0), corner)
        corner = jnp.where(small_sub == 6, roll(nm_c, 7, 0), corner)
        both = [x[:ny] for x in both]
        near_seam = planes[NAMES.index("relax") * plane_count + p]
        further = planes[NAMES.index("ns") * plane_count + p]
        side_place = place[:ny]
        seen = jnp.where(side_place < 3, roll(further, 2, 1), roll(near_seam, 3, 1))
        beyond = jnp.where(side_place > 4, roll(further, -2, 1), roll(near_seam, -3, 1))
        seen = jnp.where(side_place < 4, seen, beyond)
        both = both[:2] + [seen, seam[:ny]] + both[2:7] + [jnp.concatenate([corner] * 2, axis=0)]
        for i, x in enumerate(both):
            split(p, i * ny, x)
        return carry

    def split(p, at, x):
        for h, y in enumerate((x, roll(x, nx // 2, 1))):
            high = y.astype(jnp.bfloat16)
            packed[2 * p + h, at : at + ny, :nx] = high
            packed[2 * p + h, at : at + ny, nx:] = (y - high.astype(F32)).astype(jnp.bfloat16)

    lax.fori_loop(0, plane_count, columns, 0, unroll=plane_count)

    def unpack(u):
        move = moves[u]

        def place_both(m, carry):
            out = jnp.dot(packed[m], move, preferred_element_type=F32)
            t = m * STEPS + u
            for j, k in enumerate((t, levels - 1 - t)):
                x = out[:, j * nx : (j + 1) * nx]
                seam_x, np_x, nm_x, ep_x, em_x, sink_x, corner = (
                    x[i * ny : (i + 1) * ny] for i in range(3, 10)
                )
                corner = corner[:8]
                moved[k] = x[: 3 * ny]
                moved_rows[k] = corner
                ep_halo[k, :ny] = ep_x
                em_halo[k, :ny] = em_x
                np_halo[k, :ny] = np_x
                nm_halo[k, :ny] = nm_x
                np_halo[k, ny : ny + 8] = roll(corner, 2, 0)
                nm_halo[k, ny : ny + 8] = roll(corner, 1, 0)
                sink_halo[k] = sink_x
                s_halo[k, :ny] = seam_x
            return carry

        lax.fori_loop(0, 2 * plane_count, place_both, 0, unroll=2 * plane_count)

    for u in range(STEPS):
        unpack(u)

    def prepare(m, u, j, k, link_level):
        t = m * STEPS + u
        x = unpack_line(rim(2 * t + j))
        level = k.astype(F32)
        row = x["s"]
        open_north = level < north_rows
        np_r = jnp.where(open_north, 0.5 * x["ns"] + x["mix"], 0.0)
        nm_r = jnp.where(open_north, 0.5 * x["ns"] - x["mix"], 0.0)
        link_r = jnp.where(link_level.astype(F32) + 1.0 < count_halo[ny + 8 :], x["vm"], 0.0)
        corner = moved_rows[k]
        right, link = moved[k, :ny], moved[k, ny : 2 * ny]
        seam = s_halo[k, :ny]
        seam_rows = roll(corner, 4, 0)
        np_halo[k, ny + 8 :] = np_r
        nm_halo[k, ny + 8 :] = nm_r
        s_halo[k, ny + 8 :] = row

        own = s[k]
        last, first = lane == nx - 1, lane == 0
        through = jnp.where(first[:8], seam_rows, jnp.where(last[:8], -seam_rows, 0.0))
        fn = np_r * row + nm_r * shift_up(own[:8], 0)
        top = np_[k, ny - 8 :] * own[ny - 8 :]
        cross = nm[k, ny - 8 :] * shift_up(row, 0)
        from_block = jnp.where(small_sub == 0, shift_down(top + cross, 0), 0.0)
        right_r = x["base"] + through - (fn - from_block)

        inner = local[k] + jnp.where(first, seam, jnp.where(last, -seam, 0.0))
        low_rows = inner[:8] + jnp.where(small_sub == 0, shift_down(fn, 0), 0.0)
        high_rows = inner[ny - 8 :] - jnp.where(small_sub == 7, cross, 0.0)
        between = [inner[8 : ny - 8]] if ny > 16 else []
        inner = jnp.concatenate([low_rows] + between + [high_rows], axis=0)
        halo = jnp.concatenate([right, corner, right_r], axis=0)
        return inner, halo, jnp.concatenate([link, roll(corner, 6, 0), link_r], axis=0)

    def factor(m, carry):
        for u in range(STEPS):
            carry = factor_step(m, u, carry)
        return carry

    def factor_step(m, u, carry):
        t = m * STEPS + u
        new = []
        for j, (k, link_level) in enumerate(level_pair(levels, t)):
            ratio, c_own, c_halo, outer = carry[j]
            own, halo, link = prepare(m, u, j, k, link_level)
            inv_h = 1.0 / (1.0 + outer + link - outer * ratio)
            q_h = outer * inv_h
            ratio = link * inv_h
            c_own = own * inv[k] + q[k] * c_own
            c_halo = halo * inv_h + q_h * c_halo
            inv_halo[k] = inv_h
            q_halo[k] = q_h
            r_halo[k] = ratio
            carries[k] = whole(c_own, c_halo)
            new.append((ratio, c_own, c_halo, link))
        return tuple(new)

    zero = jnp.zeros(count_halo.shape, F32)
    begin = (zero, jnp.zeros((ny, nx), F32), zero, zero)
    (r_top, top_own, top_halo, _), (r_low, low_own, low_halo, _) = lax.fori_loop(
        0, half // STEPS, factor, (begin, begin), unroll=2
    )
    c_top, c_low = whole(top_own, top_halo), whole(low_own, low_halo)
    join = 1.0 / (1.0 - whole(r[half - 1], r_top) * whole(r[half], r_low))
    join_out[...] = join

    def ext(own, halo):
        return lambda k: whole(own[k], halo[k])

    def inner(own, halo):
        return lambda k: extend(own[k], halo[k, :ny])

    def spread(state, ep, em, np_, nm):
        fe = ep * state + em * east(state)
        fn = np_ * state + nm * shift_up(state, 0)
        return (fe - west(fe)) + (fn - shift_down(fn, 0))

    def both(one):
        def use(t, m, u, top, low):
            one(t, top, m, u, 0)
            one(levels - 1 - t, low, m, u, 1)

        return use

    def to_second(k, x, m, u, j):
        middle_out[k] = x
        state = x[:ny]
        squeeze = jnp.tanh(state)
        loss = inner(sink, sink_halo)(k)
        damp_out[k] = 1.0 - loss * (1.0 - squeeze * squeeze)
        fields = (ext(ep, ep_halo), ext(em, em_halo), ext(np_, np_halo), ext(nm, nm_halo))
        flow = spread(x, *(field(k) for field in fields))
        rhs[k] = state - flow[:ny] - loss * squeeze

    solve_outward(levels, (c_top, c_low), ext(r, r_halo), join, carries, both(to_second))

    main = carries.at[:, :ny]
    inv_q = inner(inv, inv_halo), inner(q, q_halo)
    ratio = inner(r, r_halo)
    ends = solve_inward(levels, lambda k: rhs[k], inv_q, main)

    def to_adjoint(k, x, m, u, j):
        seen = extend(obs[k].astype(F32), moved[k, 2 * ny :])
        rhs[k] = jnp.where(k.astype(F32) < count_ext[:ny], x - seen, 0.0)

    solve_outward(levels, ends, ratio, join[:ny], main, both(to_adjoint))
    ends = solve_inward(levels, lambda k: rhs[k], inv_q, main)

    def rim_part(k, solved):
        solved_out[k] = solved
        x = edge_rows(solved)
        main, side = halves(x)
        rows_of = lambda ref: edge_rows(ref[k])
        part, _ = pull_x(main, side, rows_of(ep), rows_of(em), edge_rows(em_halo[k, :ny]))
        part = part + main * edge_rows(damp_out[k, :, :nx])
        gn = shift_up(main, 0) - main
        sub = sublane(main.shape)
        part = part + jnp.where(
            sub == 0,
            rows_of(np_) * gn,
            jnp.where(sub == 7, shift_down(rows_of(nm) * gn, 0), 0.0),
        )
        return jnp.concatenate([pair_rows(main, part), side], axis=1)

    lane8 = iota((8, nx), 1)

    def to_send(t, m, u, top, low):
        pair = two_levels(rim_part(t, top), rim_part(levels - 1 - t, low))
        send[t] = pair[:, :nx]
        before = jnp.zeros((8, nx), F32) if u == STEPS - 1 else sides[m]
        moved = roll(pair[:, nx:], 2 * u + 1, 1)
        sides[m] = jnp.where(lane8 // 2 == u, moved, before)

    solve_outward(levels, ends, ratio, join[:ny], main, to_send)
    both_sides = sides[0]
    for m in range(1, half // STEPS):
        place = m * 2 * STEPS
        both_sides = jnp.where(lane8 < place, both_sides, roll(sides[m], place, 1))
    send[half] = both_sides


def inner_kernel(
    ep, em, np_, nm, ep_halo, em_halo, np_halo, nm_halo, damp, middle, solved, counts,
    s, s_halo, part_out, late_out, run_out, rise_out,
):
    levels, ny, width = solved.shape
    nx = width // 2
    sub = sublane((ny, width))
    inside = sub < ny - 1
    lane = iota((ny, nx), 1)

    def inner(k, carry):
        x = solved[k]
        state = middle[k]
        field = lambda own, halo: extend(own[k], halo[k, :ny])
        part, ge = part_of_pull(x, field(ep, ep_halo), field(em, em_halo), damp[k])
        gn = jnp.where(inside, shift_up(x, 0) - x, 0.0)
        part_out[k] = (
            part + field(np_, np_halo) * gn + shift_down(field(nm, nm_halo) * gn, 0)
        )
        level = k.astype(F32)
        open_east = level < counts[1, :ny, :nx]
        open_north = level < counts[2, :ny, :nx]

        def slopes(main, next_column, rows):
            run = jnp.where(lane == nx - 1, next_column, roll(main, -1, 1)) - main
            rise = shift_up(jnp.concatenate([main, rows], axis=0), 0)[:ny] - main
            return jnp.where(open_east, run, 0.0), jnp.where(open_north, rise, 0.0)

        run, rise = slopes(state[:ny, :nx], state[:ny, nx:], state[ny:, :nx])
        late_out[k] = ge[:, :nx] * run + gn[:, :nx] * rise
        run_out[k], rise_out[k] = slopes(
            s[k], roll(s_halo[k, :ny], 1, 1), s_halo[k, ny + 8 :]
        )
        return carry

    lax.fori_loop(0, levels, inner, 0, unroll=UNROLL)


def backward_kernel(
    ep, em, np_, nm, inv, q, r, ep_halo, em_halo, np_halo, nm_halo, inv_halo, q_halo, r_halo,
    middle, damp, solved, counts, join, part, late, run, rise, rows_n, rows_s,
    adjoint_out, gradient_out, carries, adjoint, gradient, sides, sent,
):
    levels, ny, width = solved.shape
    nx = width // 2
    half = levels // 2
    sub = sublane((8, width))

    side = merge_rows(rows_n[half], rows_s[half])
    for m in range(half // STEPS):
        sides[m] = roll(side, -2 * STEPS * m, 1)

    def rims(m, u):
        t = m * STEPS + u
        line = merge_rows(rows_n[t], rows_s[t])
        corner = roll(sides[m], -1 - 2 * u, 1)
        both = jnp.concatenate([line, corner], axis=1)
        return both, roll(both, 4, 0)

    def across(k, rim):
        inner = part[k]
        near_part = roll(rim, 6, 0)
        south = solved[k, :8] - shift_down(rim, 0)
        north = shift_up(rim, 0) - solved[k, ny - 8 :]
        north_plus = whole(np_[k], np_halo[k])
        north_minus = whole(nm[k], nm_halo[k])
        np_rim, nm_rim = north_plus[ny:], north_minus[ny:]
        np_top, nm_top = north_plus[ny - 8 : ny], north_minus[ny - 8 : ny]
        low = inner[:8] + jnp.where(sub == 0, shift_down(nm_rim, 0) * south, 0.0)
        high = inner[ny - 8 :] + jnp.where(sub == 7, np_top * north, 0.0)
        outer = near_part + jnp.where(
            sub == 0, shift_down(nm_top * north, 0), np_rim * shift_up(south, 0)
        )
        rise = (shift_up(middle[k, ny:], 0) - middle[k, ny - 8 : ny])[:, :nx]
        open_north = (sub[:, :nx] == 7) & (k.astype(F32) < counts[2, ny - 8 : ny, :nx])
        extra = jnp.where(open_north, north[:, :nx] * rise, 0.0)
        gradient[k, : ny - 8] = late[k, : ny - 8]
        gradient[k, ny - 8 :] = late[k, ny - 8 :] + extra
        middle_rows = [inner[8 : ny - 8]] if ny > 16 else []
        return jnp.concatenate([low, *middle_rows, high, outer], axis=0)

    def late_steps(m, carry):
        for u in range(STEPS):
            t = m * STEPS + u
            new = []
            for k, rim, last in zip((t, levels - 1 - t), rims(m, u), carry):
                c = across(k, rim) * whole(inv[k], inv_halo[k])
                c = c + whole(q[k], q_halo[k]) * last
                carries[k] = c
                new.append(c)
            carry = tuple(new)
        return carry

    zero = jnp.zeros(carries.shape[1:], F32)
    ends = lax.fori_loop(0, half // STEPS, late_steps, (zero, zero), unroll=2)

    def early(k, x):
        main, side = halves(x[:ny])
        flow, ge = pull_x(main, side, ep[k], em[k], em_halo[k, :ny])
        result = main * damp[k] + flow
        column = x[:, :nx]
        gn = shift_up(column, 0) - column
        minus = jnp.concatenate([nm[k], nm_halo[k, ny + 8 :]], axis=0)
        result = result + np_[k] * gn[:ny] + shift_down(minus * gn, 0)[:ny]
        adjoint[k] = result
        gradient[k] = -(gradient[k] + ge * run[k] + gn[:ny] * rise[k])

    def copies(p):
        out = []
        for i, begin in enumerate((p * UNROLL, levels - (p + 1) * UNROLL)):
            place = pl.ds(begin, UNROLL)
            for j, (source, target) in enumerate(
                ((adjoint, adjoint_out), (gradient, gradient_out))
            ):
                out.append(
                    pltpu.make_async_copy(
                        source.at[place], target.at[place], sent.at[p, 2 * i + j]
                    )
                )
        return out

    high, low = ends
    steps = half // UNROLL
    ratio = lambda k: whole(r[k], r_halo[k])
    last = (low + ratio(half) * high) * join[...], (high + ratio(half - 1) * low) * join[...]

    def block(i, last):
        p = steps - 1 - i
        for g in range(UNROLL - 1, -1, -1):
            t = p * UNROLL + g
            new = []
            for k, x in ((t, last[0]), (levels - 1 - t, last[1])):
                x = carries[k] + ratio(k) * x
                early(k, x)
                new.append(x)
            last = tuple(new)
        for copy in copies(p):
            copy.start()
        return last

    lax.fori_loop(0, steps, block, last)
    for p in range(steps):
        for copy in copies(p):
            copy.wait()


def ring(axis, distance):
    count = lax.axis_size(axis)
    return [(i, (i + distance) % count) for i in range(count)]


def both_ways(x):
    from_north = lax.ppermute(x, "ty", ring("ty", -1))
    if lax.axis_size("ty") == 2:
        return from_north, from_north
    return from_north, lax.ppermute(x, "ty", ring("ty", 1))


def swap(x, phase):
    nx = lax.axis_size("tx")
    return lax.ppermute(
        x, "tx", [(i, (i + 1) % nx if i % 2 == phase else (i - 1) % nx) for i in range(nx)]
    )


def per_device(
    tracer_start,
    observed,
    east_speed,
    north_speed,
    mixing,
    vertical_mixing,
    relax_rate,
    level_count,
    face_east,
    face_north,
):
    levels, ny, nx = tracer_start.shape
    per_plane = 128 // GROUP
    plane_count = levels // per_plane
    pairs = (len(NAMES[:6]) * plane_count + 2) // 2
    fields = (
        tracer_start, east_speed, north_speed, mixing, relax_rate, vertical_mixing, observed,
        level_count, face_east, face_north,
    )
    half = levels // 2
    corner_planes = 2 * plane_count
    *fields, corners = call(
        rim_kernel,
        [jax.ShapeDtypeStruct(x.shape, x.dtype) for x in fields]
        + [(corner_planes, 8, nx)],
        [pltpu.SemaphoreType.DMA((10,))],
        *[pltpu.with_memory_space_constraint(x, pltpu.HBM) for x in fields],
        space=HBM,
    )
    corners_n, corners_s = both_ways(corners)
    planes, rows = call(
        column_kernel, [(2 * pairs, ny, nx), (levels + 1, 8, nx)], [], *fields[:8]
    )
    rows_n, rows_s = both_ways(rows)
    packed = (pairs * ny + corner_planes // 2 * 8, nx)
    one, two, own_corners = call(
        halves_kernel, [packed, packed, corners.shape], [],
        planes, corners_n, corners_s,
        cost=pl.CostEstimate(flops=10**10, bytes_accessed=0, transcendentals=0),
    )
    from_two = swap(two, 1)
    from_one = swap(one, 0)
    ext = (levels, ny + 8, 2 * nx)
    block = (levels, ny, 2 * nx)
    own = (levels, ny, nx)
    halo = (levels, ny + 16, nx)
    s, es, ns, mix, relax, vm, obs, count, east, north = fields
    *coefficients, damp, local, inv, q, r, moves = call(
        local_kernel,
        [own] * 10 + [jax.ShapeDtypeStruct((STEPS, 2 * nx, 2 * nx), jnp.bfloat16)],
        [],
        s, es, ns, mix, relax, vm, count, east, north, one,
        cost=pl.CostEstimate(flops=10**9, bytes_accessed=0, transcendentals=0),
    )
    ep, em, np_, nm, sink = coefficients
    outs = call(
        forward_kernel,
        [halo] * 4 + [own] + [halo] * 4 + [ext, block, block, (3,) + ext[1:], ext[1:]]
        + [(half + 1, 8, nx)],
        [
            planes.shape,
            corners.shape,
            block,
            ext,
            pltpu.VMEM((2 * plane_count, 10 * ny, 2 * nx), jnp.bfloat16),
            (levels, 3 * ny, nx),
            (levels, 8, nx),
            (2 * plane_count, 8, nx),
        ],
        s, obs, count, from_one, from_two, planes, own_corners, rows_n, rows_s,
        ep, em, np_, nm, sink, local, inv, q, r, moves,
    )
    ep_h, em_h, np_h, nm_h, _, inv_h, q_h, r_h, s_h, *outs = outs
    middle, late_damp, solved, counts, join, send = outs
    sent_n, sent_s = both_ways(send)
    faces = ep, em, np_, nm
    halo_faces = ep_h, em_h, np_h, nm_h
    part, late, run, rise = call(
        inner_kernel,
        [block] + [own] * 3,
        [],
        *faces, *halo_faces, late_damp, middle, solved, counts, s, s_h,
        cost=pl.CostEstimate(flops=0, bytes_accessed=8 << 20, transcendentals=0),
    )
    adjoint, gradient = call(
        backward_kernel,
        [own] * 2,
        [ext, own, own, (2 * plane_count, 8, nx), pltpu.SemaphoreType.DMA((half // UNROLL, 4))],
        *faces, inv, q, r, *halo_faces, inv_h, q_h, r_h,
        middle, damp, solved, counts, join, part, late, run, rise, sent_n, sent_s,
        out_space=HBM,
    )
    return adjoint, gradient


def solution(mesh):
    block = P(None, "ty", "tx")
    plane = P("ty", "tx")
    return jax.shard_map(
        per_device,
        mesh=mesh,
        in_specs=(block,) * 7 + (plane,) * 3,
        out_specs=(block, block),
        check_vma=False,
    )
```

```python
import functools

import jax
import jax.numpy as jnp
from jax import lax
from jax.experimental import pallas as pl
from jax.experimental.pallas import tpu as pltpu
from jax.sharding import PartitionSpec as P

F32 = jnp.float32
VMEM = pl.BlockSpec(memory_space=pltpu.VMEM)
HBM = pl.BlockSpec(memory_space=pltpu.HBM)
UNROLL = 8
STEPS = 4
GROUP = 8
NAMES = ("s", "es", "ns", "mix", "relax", "vm", "obs")


def call(kernel, outs, scratch, *args, space=VMEM, out_space=VMEM, cost=None):
    def typed(x):
        return x if isinstance(x, jax.ShapeDtypeStruct) else jax.ShapeDtypeStruct(x, F32)

    return pl.pallas_call(
        kernel,
        out_shape=[typed(x) for x in outs],
        in_specs=[space] * len(args),
        out_specs=[out_space] * len(outs),
        scratch_shapes=[pltpu.VMEM(x, F32) if isinstance(x, tuple) else x for x in scratch],
        compiler_params=pltpu.CompilerParams(vmem_limit_bytes=16 << 20),
        cost_estimate=cost,
    )(*args)


def iota(shape, dim):
    return lax.broadcasted_iota(jnp.int32, shape, dim)


def roll(x, shift, axis):
    if isinstance(shift, int):
        shift = shift % x.shape[axis]
        if shift == 0:
            return x
    return pltpu.roll(x, shift, axis)


def odd_column():
    return lax.rem(lax.axis_index("tx"), 2) == 1


def level_of(ref, name, level):
    if name == "vm":
        level = jnp.minimum(level, ref.shape[0] - 1)
    return ref[level].astype(F32)


def edge_rows(block):
    return jnp.where(iota((8, block.shape[1]), 0) < 4, block[:8], block[-8:])


def sublane(shape):
    return iota(shape, 0)


def step_count(counts, axis):
    return jnp.minimum(counts, shift_up(counts, axis))


def pair_rows(first, second):
    sub = sublane(first.shape)
    return jnp.where((sub == 1) | (sub == 2), roll(second, 2, 0), first)


def level_pair(levels, t):
    return (t, t), (levels - 1 - t, levels - 2 - t)


def in_all_groups(x):
    group = iota(x.shape, 1) // GROUP
    out = jnp.zeros(x.shape, F32)
    for g in range(x.shape[1] // GROUP):
        out = jnp.where(group == g, roll(x, GROUP * g + 4, 1), out)
    return out


def pack_rows(get, counts, level):
    tile = {name: edge_rows(get(name)) for name in NAMES[:6]}
    s = tile["s"]
    sub = sublane(s.shape)
    open_north = level < step_count(counts, 0)
    fn = jnp.where(
        open_north,
        (0.5 * tile["ns"] + tile["mix"]) * s + (0.5 * tile["ns"] - tile["mix"]) * shift_up(s, 0),
        0.0,
    )
    sink = jnp.where(level < counts, tile["relax"], 0.0)
    inner = jnp.where(sub == 0, -fn, jnp.where(sub == 7, shift_down(fn, 0), 0.0))
    base = s - sink * jnp.tanh(s) + inner
    first = pair_rows(s, base)
    first = jnp.where((sub == 3) | (sub == 4), roll(tile["es"], 4, 0), first)
    first = jnp.where((sub == 5) | (sub == 6), roll(tile["mix"], 6, 0), first)
    lane = iota(s.shape, 1)
    fe = (0.5 * tile["es"] + tile["mix"]) * s
    fe = fe + (0.5 * tile["es"] - tile["mix"]) * shift_up(s, 1)
    fe = jnp.where((level < step_count(counts, 1)) & (lane < s.shape[1] - 1), fe, 0.0)
    line = pair_rows(s, base - (fe - shift_down(fe, 1)))
    line = jnp.where((sub == 3) | (sub == 4), roll(tile["vm"], 4, 0), line)
    line = jnp.where(sub == 5, roll(tile["ns"], 6, 0), line)
    line = jnp.where(sub == 6, roll(tile["mix"], 7, 0), line)
    return line, first, pair_rows(tile["vm"], tile["ns"])


def merge_lines(north, south):
    sub = sublane(north.shape)
    return jnp.where((sub == 0) | (sub == 2) | (sub == 4), north, south)


def unpack_line(line):
    return {
        "s": line,
        "base": roll(line, 6, 0),
        "vm": roll(line, 4, 0),
        "ns": roll(line, 2, 0),
        "mix": roll(line, 1, 0),
    }


def unpack_rows(first, second):
    return {
        "s": first,
        "base": roll(first, 6, 0),
        "es": roll(first, 4, 0),
        "mix": roll(first, 2, 0),
        "vm": second,
        "ns": roll(second, 6, 0),
    }


def two_levels(x, y):
    sub = sublane(x.shape)
    return jnp.where((sub >= 3) & (sub <= 6), roll(y, 4, 0), x)


def shift_up(x, axis):
    return roll(x, -1, axis)


def shift_down(x, axis):
    return roll(x, 1, axis)


def rim_kernel(*args):
    fields = args[:10]
    s, es, ns, mix, relax, vm, obs, count, *_ = kept = args[10:20]
    corners, arrived = args[20:]
    copies = [pltpu.make_async_copy(fields[i], kept[i], arrived.at[i]) for i in range(10)]
    first = (7, 0, 1, 2, 3, 4, 5)
    rest = (6, 8, 9)
    for i in first + rest:
        copies[i].start()
    for i in first:
        copies[i].wait()
    refs = dict(zip(NAMES, (s, es, ns, mix, relax, vm, obs)))
    levels = s.shape[0]
    per_plane = 128 // GROUP
    small = (8, s.shape[2])
    group = iota(small, 1) // GROUP
    half = per_plane // 2
    plane_count = levels // per_plane
    counts = edge_rows(count[...].astype(F32))
    sub = sublane(small)

    def rims(p, carry):
        acc = jnp.zeros(small, F32)
        late = jnp.zeros(small, F32)
        for g in range(half):
            t = p * half + g
            for j, (k, link) in enumerate(level_pair(levels, t)):
                _, first, second = pack_rows(
                    lambda name: level_of(refs[name], name, link if name == "vm" else k),
                    counts,
                    k.astype(F32),
                )
                place = 2 * g + j
                acc = jnp.where(group == place, roll(first, GROUP * place + 4, 1), acc)
                second = jnp.where((sub == 3) | (sub == 4), roll(counts, 4, 0), second)
                late = jnp.where(group == place, roll(second, GROUP * place + 4, 1), late)
        corners[p] = acc
        corners[plane_count + p] = late
        return carry

    lax.fori_loop(0, plane_count, rims, 0)
    for i in rest:
        copies[i].wait()


def column_kernel(s, es, ns, mix, relax, vm, obs, count, planes, rows):
    refs = dict(zip(NAMES, (s, es, ns, mix, relax, vm, obs)))
    levels = s.shape[0]
    per_plane = 128 // GROUP
    plane_count = levels // per_plane
    shape = s.shape[1:]
    group = iota(shape, 1) // GROUP

    place = iota(shape, 1) % GROUP
    counts = edge_rows(count[...].astype(F32))
    rows[levels] = counts

    def lines(t, carry):
        for j, (k, link) in enumerate(level_pair(levels, t)):
            rows[2 * t + j], _, _ = pack_rows(
                lambda name: level_of(refs[name], name, link if name == "vm" else k),
                counts,
                k.astype(F32),
            )
        return carry

    lax.fori_loop(0, levels // 2, lines, 0, unroll=UNROLL)

    def columns(p, carry):
        packed = []
        for name in NAMES:
            acc = jnp.zeros(shape, F32)
            for g in range(per_plane):
                pair = level_pair(levels, p * (per_plane // 2) + g // 2)
                x = refs[name][pair[g % 2][name == "vm"]].astype(F32)
                acc = jnp.where(group == g, roll(x, GROUP * g + 4, 1), acc)
            packed.append(acc)
        seen = packed.pop()
        for name, distance in (("ns", 2), ("relax", 3)):
            i = NAMES.index(name)
            x = jnp.where(place == 0, roll(seen, -distance, 1), packed[i])
            packed[i] = jnp.where(place == GROUP - 1, roll(seen, distance, 1), x)
        for a, x in enumerate(packed):
            planes[a * plane_count + p] = x
        return carry

    lax.fori_loop(0, plane_count, columns, 0)
    total = len(NAMES[:6]) * plane_count
    planes[total] = in_all_groups(count[...].astype(F32))
    for p in range(total + 1, planes.shape[0]):
        planes[p] = jnp.zeros(shape, F32)


def merge_rows(north, south):
    return jnp.where(sublane(north.shape) % 2 == 0, north, south)


def halves_kernel(planes, corners_n, corners_s, one, two, kept):
    odd = odd_column()
    pairs = planes.shape[0] // 2
    ny = planes.shape[1]

    def put(place, x, y):
        low = iota(x.shape, 1) % GROUP < 4
        to_east = jnp.where(low, x, roll(y, 4, 1))
        to_west = jnp.where(low, roll(x, -4, 1), y)
        one[place] = jnp.where(odd, to_west, to_east)
        two[place] = jnp.where(odd, to_east, to_west)

    for h in range(pairs):
        put(pl.ds(h * ny, ny), planes[2 * h], planes[2 * h + 1])

    count = corners_n.shape[0]
    def corner(p):
        return merge_rows(corners_n[p], corners_s[p])

    for h in range(count // 2):
        x, y = corner(2 * h), corner(2 * h + 1)
        kept[2 * h] = x
        kept[2 * h + 1] = y
        put(pl.ds(pairs * ny + h * 8, 8), x, y)


def halves(x):
    nx = x.shape[1] // 2
    return x[:, :nx], x[:, nx:]


def east(x):
    main, side = halves(x)
    lane = iota(main.shape, 1)
    return jnp.concatenate(
        [
            jnp.where(lane == lane.shape[1] - 1, side, roll(main, -1, 1)),
            jnp.where(lane == 0, main, roll(side, 1, 1)),
        ],
        axis=1,
    )


def west(x):
    main, side = halves(x)
    lane = iota(main.shape, 1)
    return jnp.concatenate(
        [
            jnp.where(lane == 0, side, roll(main, 1, 1)),
            jnp.where(lane == lane.shape[1] - 1, main, roll(side, -1, 1)),
        ],
        axis=1,
    )


def pull_x(main, side, ep, em, em_side):
    lane = iota(main.shape, 1)
    ge = jnp.where(lane == lane.shape[1] - 1, side, roll(main, -1, 1)) - main
    return ep * ge + jnp.where(lane == 0, em_side * (main - side), roll(em * ge, 1, 1)), ge


def extend(main, side, rows=None, corners=None):
    top = jnp.concatenate([main, side], axis=1)
    if rows is None:
        return top
    return jnp.concatenate([top, jnp.concatenate([rows, corners], axis=1)], axis=0)


def solve_inward(levels, get, inv_q, carries):
    half = levels // 2
    inv, q = inv_q

    def step(t, carry):
        new = []
        for k, last in ((t, carry[0]), (levels - 1 - t, carry[1])):
            c = get(k) * inv(k) + q(k) * last
            carries[k] = c
            new.append(c)
        return tuple(new)

    zero = jnp.zeros(carries.shape[1:], F32)
    return lax.fori_loop(0, half, step, (zero, zero), unroll=UNROLL)


def solve_outward(levels, ends, ratio, join, carries, use, unroll=2):
    half = levels // 2
    high, low = ends
    upper = (high + ratio(half - 1) * low) * join
    lower = (low + ratio(half) * high) * join

    def block(i, last):
        m = half // STEPS - 1 - i
        for u in range(STEPS - 1, -1, -1):
            t = m * STEPS + u
            new = []
            for k, x in ((t, last[0]), (levels - 1 - t, last[1])):
                new.append(carries[k] + ratio(k) * x)
            use(t, m, u, *new)
            last = tuple(new)
        return last

    lax.fori_loop(0, half // STEPS, block, (lower, upper), unroll=unroll)


def merge_halos(odd, from_one, from_two, planes, start):
    size = planes.shape[1]
    low = iota(planes.shape[1:], 1) % GROUP < 4
    for h in range(planes.shape[0] // 2):
        place = pl.ds(start + h * size, size)
        a, b = from_one[place], from_two[place]
        west = jnp.where(odd, a, b)
        east = jnp.where(odd, b, a)
        planes[2 * h] = jnp.where(low, west, roll(east, 4, 1))
        planes[2 * h + 1] = jnp.where(low, roll(west, -4, 1), east)


def part_of_pull(x, ep, em, damp):
    ge = east(x) - x
    return x * damp + ep * ge + west(em * ge), ge


def local_kernel(
    s, es, ns, mix, relax, vm, count, east, north, after,
    ep_out, em_out, np_out, nm_out, sink_out, damp_out, local_out, inv_out, q_out, r_out,
    moves_out,
):
    levels, ny, nx = s.shape
    half = levels // 2
    counts = count[...].astype(F32)
    east_count = east[...].astype(F32)
    north_count = north[...].astype(F32)
    lane = iota((ny, nx), 1)
    sub = sublane((ny, nx))

    def prepare(k):
        level = k.astype(F32)
        state = s[k]
        diffusion = mix[k].astype(F32)
        speed_east = 0.5 * es[k].astype(F32)
        speed_north = 0.5 * ns[k].astype(F32)
        open_east = level < east_count
        open_north = level < north_count
        ep = jnp.where(open_east, speed_east + diffusion, 0.0)
        em = jnp.where(open_east, speed_east - diffusion, 0.0)
        np_ = jnp.where(open_north, speed_north + diffusion, 0.0)
        nm = jnp.where(open_north, speed_north - diffusion, 0.0)
        sink = jnp.where(level < counts, relax[k].astype(F32), 0.0)
        squeeze = jnp.tanh(state)
        ep_out[k] = ep
        em_out[k] = em
        np_out[k] = np_
        nm_out[k] = nm
        sink_out[k] = sink
        damp_out[k] = 1.0 - sink * (1.0 - squeeze * squeeze)
        fe = ep * state + em * shift_up(state, 1)
        fe = jnp.where(lane == nx - 1, 0.0, fe)
        fn = np_ * state + nm * jnp.where(sub == ny - 1, 0.0, shift_up(state, 0))
        flow = fe - shift_down(fe, 1)
        flow = flow + (fn - jnp.where(sub == 0, 0.0, shift_down(fn, 0)))
        local_out[k] = state - sink * squeeze - flow

    def factor(t, carry):
        new = []
        for (k, link_level), (ratio, outer) in zip(level_pair(levels, t), carry):
            prepare(k)
            link = jnp.where(
                link_level.astype(F32) + 1.0 < counts, vm[link_level].astype(F32), 0.0
            )
            inv = 1.0 / (1.0 + outer + link - outer * ratio)
            ratio = link * inv
            inv_out[k] = inv
            q_out[k] = outer * inv
            r_out[k] = ratio
            new.append((ratio, link))
        return tuple(new)

    zero = jnp.zeros((ny, nx), F32)
    lax.fori_loop(0, half, factor, ((zero, zero), (zero, zero)), unroll=UNROLL)

    source = iota((2 * nx, 2 * nx), 0) % nx
    target = iota((2 * nx, 2 * nx), 1)
    for u in range(STEPS):
        group = 2 * u + target // nx
        lane = target % nx
        column = jnp.where(lane < 4, 3 - lane, jnp.where(lane >= nx - 4, nx + 3 - lane, -nx))
        hit = source == GROUP * group + column
        moves_out[u] = jnp.where(hit, 1.0, 0.0).astype(jnp.bfloat16)


def whole(own, halo):
    ny = own.shape[0]
    return extend(own, halo[:ny], halo[ny + 8 :], halo[ny : ny + 8])


def forward_kernel(
    s, obs, count, from_one, from_two, own_planes, own_corners, rows_n, rows_s,
    ep, em, np_, nm, sink, local, inv, q, r, moves,
    ep_halo, em_halo, np_halo, nm_halo, sink_halo, inv_halo, q_halo, r_halo, s_halo,
    middle_out, damp_out, solved_out, counts_out, join_out, send,
    planes, corners, rhs, carries, packed, moved, moved_rows, sides,
):
    levels, ny, nx = s.shape
    half = levels // 2
    per_plane = 128 // GROUP
    plane_count = levels // per_plane
    odd = odd_column()
    merge_halos(odd, from_one, from_two, planes, 0)
    merge_halos(odd, from_one, from_two, corners, planes.shape[0] // 2 * planes.shape[1])

    def rim(index):
        return merge_lines(rows_n[index], rows_s[index])

    count_plane = len(NAMES[:6]) * plane_count
    side_counts = jnp.dot(
        jnp.concatenate([planes[count_plane]] + [roll(corners[plane_count], 4, 0)] * 2, axis=0).astype(
            jnp.bfloat16
        ),
        moves[0, :nx, :nx],
        preferred_element_type=F32,
    )
    count_ext = extend(
        count[...].astype(F32),
        side_counts[:ny],
        rim(levels),
        side_counts[ny : ny + 8],
    )
    east_ext = jnp.minimum(count_ext, east(count_ext))
    counts_out[0] = count_ext
    counts_out[1] = east_ext
    counts_out[2] = step_count(count_ext, 0)
    count_halo = jnp.concatenate(
        [count_ext[:ny, nx:], count_ext[ny:, nx:], count_ext[ny:, :nx]], axis=0
    )
    small_sub = sublane((8, nx))
    north_rows = jnp.where(small_sub == 7, counts_out[2, ny:, :nx], 0.0)
    lane = iota((ny, nx), 1)
    per_half = per_plane // 2

    strip = (ny + 8, nx)
    place = iota(strip, 1) % GROUP
    low = place < 4
    groups = iota(strip, 1) // GROUP
    from_top = groups % 2 == 0
    strip_sub = sublane(strip)

    def columns(p, carry):
        t = p * per_half + groups // 2
        level = jnp.where(from_top, t, levels - 1 - t).astype(F32)
        link_level = jnp.where(from_top, t, levels - 2 - t).astype(F32)

        def side_and_corner(a, c):
            return jnp.concatenate([a, c], axis=0)

        def strips(west):
            def pick(halo, own):
                near_side = low[: halo.shape[0]]
                return jnp.where(near_side, halo, own) if west else jnp.where(near_side, own, halo)

            x = unpack_rows(
                pick(corners[p], own_corners[p]),
                pick(corners[plane_count + p], own_corners[plane_count + p]),
            )
            side = {}
            for a, name in enumerate(NAMES[:6]):
                at = a * plane_count + p
                side[name] = pick(planes[at], own_planes[at])
            for name in NAMES[:4] + NAMES[5:6]:
                x[name] = side_and_corner(side[name], x[name])
            counts = side_and_corner(
                pick(planes[count_plane], own_planes[count_plane]),
                roll(pick(corners[plane_count + p], own_corners[plane_count + p]), 4, 0),
            )
            state = x["s"]
            open_east = level < step_count(counts, 1)
            open_north = (level < step_count(counts, 0)) & (
                (strip_sub < ny) | (strip_sub == ny + 7)
            )
            ep_s = jnp.where(open_east, 0.5 * x["es"] + x["mix"], 0.0)
            em_s = jnp.where(open_east, 0.5 * x["es"] - x["mix"], 0.0)
            np_s = jnp.where(open_north, 0.5 * x["ns"] + x["mix"], 0.0)
            nm_s = jnp.where(open_north, 0.5 * x["ns"] - x["mix"], 0.0)
            sink_s = jnp.where(level[:ny] < counts[:ny], side["relax"], 0.0)
            link = jnp.where(link_level + 1.0 < counts, x["vm"], 0.0)
            fe = ep_s * state + em_s * shift_up(state, 1)
            fe_west = shift_down(fe, 1)
            fn = np_s * state + nm_s * shift_up(state, 0)
            base = side_and_corner(side["s"] - sink_s * jnp.tanh(side["s"]), x["base"])
            right = base - (fe - fe_west) - (fn - shift_down(fn, 0))
            return (right, link, np_s, nm_s, ep_s, em_s, sink_s, state), fe, fe_west

        western, through_west, _ = strips(True)
        eastern, _, through_east = strips(False)
        seam = jnp.where(place == 3, through_west, through_east)
        seam = jnp.where(place == 5, roll(eastern[7], 1, 1), seam)
        both = [jnp.where(low[: a.shape[0]], a, b) for a, b in zip(western, eastern)]
        right, link, np_c, nm_c = (x[ny:] for x in both[:4])
        corner = pair_rows(right, link)
        corner = jnp.where((small_sub == 3) | (small_sub == 4), roll(seam[ny:], 4, 0), corner)
        corner = jnp.where(small_sub == 5, roll(np_c, 6, 0), corner)
        corner = jnp.where(small_sub == 6, roll(nm_c, 7, 0), corner)
        both = [x[:ny] for x in both]
        near_seam = planes[NAMES.index("relax") * plane_count + p]
        further = planes[NAMES.index("ns") * plane_count + p]
        side_place = place[:ny]
        seen = jnp.where(side_place < 3, roll(further, 2, 1), roll(near_seam, 3, 1))
        beyond = jnp.where(side_place > 4, roll(further, -2, 1), roll(near_seam, -3, 1))
        seen = jnp.where(side_place < 4, seen, beyond)
        both = both[:2] + [seen, seam[:ny]] + both[2:7] + [jnp.concatenate([corner] * 2, axis=0)]
        for i, x in enumerate(both):
            split(p, i * ny, x)
        return carry

    def split(p, at, x):
        for h, y in enumerate((x, roll(x, nx // 2, 1))):
            high = y.astype(jnp.bfloat16)
            packed[2 * p + h, at : at + ny, :nx] = high
            packed[2 * p + h, at : at + ny, nx:] = (y - high.astype(F32)).astype(jnp.bfloat16)

    lax.fori_loop(0, plane_count, columns, 0, unroll=plane_count)

    def unpack(u):
        move = moves[u]

        def place_both(m, carry):
            out = jnp.dot(packed[m], move, preferred_element_type=F32)
            t = m * STEPS + u
            for j, k in enumerate((t, levels - 1 - t)):
                x = out[:, j * nx : (j + 1) * nx]
                seam_x, np_x, nm_x, ep_x, em_x, sink_x, corner = (
                    x[i * ny : (i + 1) * ny] for i in range(3, 10)
                )
                corner = corner[:8]
                moved[k] = x[: 3 * ny]
                moved_rows[k] = corner
                ep_halo[k, :ny] = ep_x
                em_halo[k, :ny] = em_x
                np_halo[k, :ny] = np_x
                nm_halo[k, :ny] = nm_x
                np_halo[k, ny : ny + 8] = roll(corner, 2, 0)
                nm_halo[k, ny : ny + 8] = roll(corner, 1, 0)
                sink_halo[k] = sink_x
                s_halo[k, :ny] = seam_x
            return carry

        lax.fori_loop(0, 2 * plane_count, place_both, 0, unroll=2 * plane_count)

    for u in range(STEPS):
        unpack(u)

    def prepare(m, u, j, k, link_level):
        t = m * STEPS + u
        x = unpack_line(rim(2 * t + j))
        level = k.astype(F32)
        row = x["s"]
        open_north = level < north_rows
        np_r = jnp.where(open_north, 0.5 * x["ns"] + x["mix"], 0.0)
        nm_r = jnp.where(open_north, 0.5 * x["ns"] - x["mix"], 0.0)
        link_r = jnp.where(link_level.astype(F32) + 1.0 < count_halo[ny + 8 :], x["vm"], 0.0)
        corner = moved_rows[k]
        right, link = moved[k, :ny], moved[k, ny : 2 * ny]
        seam = s_halo[k, :ny]
        seam_rows = roll(corner, 4, 0)
        np_halo[k, ny + 8 :] = np_r
        nm_halo[k, ny + 8 :] = nm_r
        s_halo[k, ny + 8 :] = row

        own = s[k]
        last, first = lane == nx - 1, lane == 0
        through = jnp.where(first[:8], seam_rows, jnp.where(last[:8], -seam_rows, 0.0))
        fn = np_r * row + nm_r * shift_up(own[:8], 0)
        top = np_[k, ny - 8 :] * own[ny - 8 :]
        cross = nm[k, ny - 8 :] * shift_up(row, 0)
        from_block = jnp.where(small_sub == 0, shift_down(top + cross, 0), 0.0)
        right_r = x["base"] + through - (fn - from_block)

        inner = local[k] + jnp.where(first, seam, jnp.where(last, -seam, 0.0))
        low_rows = inner[:8] + jnp.where(small_sub == 0, shift_down(fn, 0), 0.0)
        high_rows = inner[ny - 8 :] - jnp.where(small_sub == 7, cross, 0.0)
        between = [inner[8 : ny - 8]] if ny > 16 else []
        inner = jnp.concatenate([low_rows] + between + [high_rows], axis=0)
        halo = jnp.concatenate([right, corner, right_r], axis=0)
        return inner, halo, jnp.concatenate([link, roll(corner, 6, 0), link_r], axis=0)

    def factor(m, carry):
        for u in range(STEPS):
            carry = factor_step(m, u, carry)
        return carry

    def factor_step(m, u, carry):
        t = m * STEPS + u
        new = []
        for j, (k, link_level) in enumerate(level_pair(levels, t)):
            ratio, c_own, c_halo, outer = carry[j]
            own, halo, link = prepare(m, u, j, k, link_level)
            inv_h = 1.0 / (1.0 + outer + link - outer * ratio)
            q_h = outer * inv_h
            ratio = link * inv_h
            c_own = own * inv[k] + q[k] * c_own
            c_halo = halo * inv_h + q_h * c_halo
            inv_halo[k] = inv_h
            q_halo[k] = q_h
            r_halo[k] = ratio
            carries[k] = whole(c_own, c_halo)
            new.append((ratio, c_own, c_halo, link))
        return tuple(new)

    zero = jnp.zeros(count_halo.shape, F32)
    begin = (zero, jnp.zeros((ny, nx), F32), zero, zero)
    (r_top, top_own, top_halo, _), (r_low, low_own, low_halo, _) = lax.fori_loop(
        0, half // STEPS, factor, (begin, begin), unroll=2
    )
    c_top, c_low = whole(top_own, top_halo), whole(low_own, low_halo)
    join = 1.0 / (1.0 - whole(r[half - 1], r_top) * whole(r[half], r_low))
    join_out[...] = join

    def ext(own, halo):
        return lambda k: whole(own[k], halo[k])

    def inner(own, halo):
        return lambda k: extend(own[k], halo[k, :ny])

    def spread(state, ep, em, np_, nm):
        fe = ep * state + em * east(state)
        fn = np_ * state + nm * shift_up(state, 0)
        return (fe - west(fe)) + (fn - shift_down(fn, 0))

    def both(one):
        def use(t, m, u, top, low):
            one(t, top, m, u, 0)
            one(levels - 1 - t, low, m, u, 1)

        return use

    def to_second(k, x, m, u, j):
        middle_out[k] = x
        state = x[:ny]
        squeeze = jnp.tanh(state)
        loss = inner(sink, sink_halo)(k)
        damp_out[k] = 1.0 - loss * (1.0 - squeeze * squeeze)
        fields = (ext(ep, ep_halo), ext(em, em_halo), ext(np_, np_halo), ext(nm, nm_halo))
        flow = spread(x, *(field(k) for field in fields))
        rhs[k] = state - flow[:ny] - loss * squeeze

    solve_outward(levels, (c_top, c_low), ext(r, r_halo), join, carries, both(to_second))

    main = carries.at[:, :ny]
    inv_q = inner(inv, inv_halo), inner(q, q_halo)
    ratio = inner(r, r_halo)
    ends = solve_inward(levels, lambda k: rhs[k], inv_q, main)

    def to_adjoint(k, x, m, u, j):
        seen = extend(obs[k].astype(F32), moved[k, 2 * ny :])
        rhs[k] = jnp.where(k.astype(F32) < count_ext[:ny], x - seen, 0.0)

    solve_outward(levels, ends, ratio, join[:ny], main, both(to_adjoint))
    ends = solve_inward(levels, lambda k: rhs[k], inv_q, main)

    def rim_part(k, solved):
        solved_out[k] = solved
        x = edge_rows(solved)
        main, side = halves(x)
        rows_of = lambda ref: edge_rows(ref[k])
        part, _ = pull_x(main, side, rows_of(ep), rows_of(em), edge_rows(em_halo[k, :ny]))
        part = part + main * edge_rows(damp_out[k, :, :nx])
        gn = shift_up(main, 0) - main
        sub = sublane(main.shape)
        part = part + jnp.where(
            sub == 0,
            rows_of(np_) * gn,
            jnp.where(sub == 7, shift_down(rows_of(nm) * gn, 0), 0.0),
        )
        return jnp.concatenate([pair_rows(main, part), side], axis=1)

    lane8 = iota((8, nx), 1)

    def to_send(t, m, u, top, low):
        pair = two_levels(rim_part(t, top), rim_part(levels - 1 - t, low))
        send[t] = pair[:, :nx]
        before = jnp.zeros((8, nx), F32) if u == STEPS - 1 else sides[m]
        moved = roll(pair[:, nx:], 2 * u + 1, 1)
        sides[m] = jnp.where(lane8 // 2 == u, moved, before)

    solve_outward(levels, ends, ratio, join[:ny], main, to_send, 3)
    both_sides = sides[0]
    for m in range(1, half // STEPS):
        place = m * 2 * STEPS
        both_sides = jnp.where(lane8 < place, both_sides, roll(sides[m], place, 1))
    send[half] = both_sides


def inner_kernel(
    ep, em, np_, nm, ep_halo, em_halo, np_halo, nm_halo, damp, middle, solved, counts,
    s, s_halo, part_out, late_out, run_out, rise_out,
):
    levels, ny, width = solved.shape
    nx = width // 2
    sub = sublane((ny, width))
    inside = sub < ny - 1
    lane = iota((ny, nx), 1)

    def inner(k, carry):
        x = solved[k]
        state = middle[k]
        field = lambda own, halo: extend(own[k], halo[k, :ny])
        part, ge = part_of_pull(x, field(ep, ep_halo), field(em, em_halo), damp[k])
        gn = jnp.where(inside, shift_up(x, 0) - x, 0.0)
        part_out[k] = (
            part + field(np_, np_halo) * gn + shift_down(field(nm, nm_halo) * gn, 0)
        )
        level = k.astype(F32)
        open_east = level < counts[1, :ny, :nx]
        open_north = level < counts[2, :ny, :nx]

        def slopes(main, next_column, rows):
            run = jnp.where(lane == nx - 1, next_column, roll(main, -1, 1)) - main
            rise = shift_up(jnp.concatenate([main, rows], axis=0), 0)[:ny] - main
            return jnp.where(open_east, run, 0.0), jnp.where(open_north, rise, 0.0)

        run, rise = slopes(state[:ny, :nx], state[:ny, nx:], state[ny:, :nx])
        late_out[k] = ge[:, :nx] * run + gn[:, :nx] * rise
        run_out[k], rise_out[k] = slopes(
            s[k], roll(s_halo[k, :ny], 1, 1), s_halo[k, ny + 8 :]
        )
        return carry

    lax.fori_loop(0, levels, inner, 0, unroll=UNROLL)


def backward_kernel(
    ep, em, np_, nm, inv, q, r, ep_halo, em_halo, np_halo, nm_halo, inv_halo, q_halo, r_halo,
    middle, damp, solved, counts, join, part, late, run, rise, rows_n, rows_s,
    adjoint_out, gradient_out, carries, adjoint, gradient, sides, sent,
):
    levels, ny, width = solved.shape
    nx = width // 2
    half = levels // 2
    sub = sublane((8, width))

    side = merge_rows(rows_n[half], rows_s[half])
    for m in range(half // STEPS):
        sides[m] = roll(side, -2 * STEPS * m, 1)

    def rims(m, u):
        t = m * STEPS + u
        line = merge_rows(rows_n[t], rows_s[t])
        corner = roll(sides[m], -1 - 2 * u, 1)
        both = jnp.concatenate([line, corner], axis=1)
        return both, roll(both, 4, 0)

    def across(k, rim):
        inner = part[k]
        near_part = roll(rim, 6, 0)
        south = solved[k, :8] - shift_down(rim, 0)
        north = shift_up(rim, 0) - solved[k, ny - 8 :]
        north_plus = whole(np_[k], np_halo[k])
        north_minus = whole(nm[k], nm_halo[k])
        np_rim, nm_rim = north_plus[ny:], north_minus[ny:]
        np_top, nm_top = north_plus[ny - 8 : ny], north_minus[ny - 8 : ny]
        low = inner[:8] + jnp.where(sub == 0, shift_down(nm_rim, 0) * south, 0.0)
        high = inner[ny - 8 :] + jnp.where(sub == 7, np_top * north, 0.0)
        outer = near_part + jnp.where(
            sub == 0, shift_down(nm_top * north, 0), np_rim * shift_up(south, 0)
        )
        rise = (shift_up(middle[k, ny:], 0) - middle[k, ny - 8 : ny])[:, :nx]
        open_north = (sub[:, :nx] == 7) & (k.astype(F32) < counts[2, ny - 8 : ny, :nx])
        extra = jnp.where(open_north, north[:, :nx] * rise, 0.0)
        gradient[k, : ny - 8] = late[k, : ny - 8]
        gradient[k, ny - 8 :] = late[k, ny - 8 :] + extra
        middle_rows = [inner[8 : ny - 8]] if ny > 16 else []
        return jnp.concatenate([low, *middle_rows, high, outer], axis=0)

    def late_steps(m, carry):
        for u in range(STEPS):
            t = m * STEPS + u
            new = []
            for k, rim, last in zip((t, levels - 1 - t), rims(m, u), carry):
                c = across(k, rim) * whole(inv[k], inv_halo[k])
                c = c + whole(q[k], q_halo[k]) * last
                carries[k] = c
                new.append(c)
            carry = tuple(new)
        return carry

    zero = jnp.zeros(carries.shape[1:], F32)
    ends = lax.fori_loop(0, half // STEPS, late_steps, (zero, zero), unroll=2)

    def early(k, x):
        main, side = halves(x[:ny])
        flow, ge = pull_x(main, side, ep[k], em[k], em_halo[k, :ny])
        result = main * damp[k] + flow
        column = x[:, :nx]
        gn = shift_up(column, 0) - column
        minus = jnp.concatenate([nm[k], nm_halo[k, ny + 8 :]], axis=0)
        result = result + np_[k] * gn[:ny] + shift_down(minus * gn, 0)[:ny]
        adjoint[k] = result
        gradient[k] = -(gradient[k] + ge * run[k] + gn[:ny] * rise[k])

    def copies(p):
        out = []
        for i, begin in enumerate((p * UNROLL, levels - (p + 1) * UNROLL)):
            place = pl.ds(begin, UNROLL)
            for j, (source, target) in enumerate(
                ((adjoint, adjoint_out), (gradient, gradient_out))
            ):
                out.append(
                    pltpu.make_async_copy(
                        source.at[place], target.at[place], sent.at[p, 2 * i + j]
                    )
                )
        return out

    high, low = ends
    steps = half // UNROLL
    ratio = lambda k: whole(r[k], r_halo[k])
    last = (low + ratio(half) * high) * join[...], (high + ratio(half - 1) * low) * join[...]

    def block(i, last):
        p = steps - 1 - i
        for g in range(UNROLL - 1, -1, -1):
            t = p * UNROLL + g
            new = []
            for k, x in ((t, last[0]), (levels - 1 - t, last[1])):
                x = carries[k] + ratio(k) * x
                early(k, x)
                new.append(x)
            last = tuple(new)
        for copy in copies(p):
            copy.start()
        return last

    lax.fori_loop(0, steps, block, last)
    for p in range(steps):
        for copy in copies(p):
            copy.wait()


def ring(axis, distance):
    count = lax.axis_size(axis)
    return [(i, (i + distance) % count) for i in range(count)]


def both_ways(x):
    from_north = lax.ppermute(x, "ty", ring("ty", -1))
    if lax.axis_size("ty") == 2:
        return from_north, from_north
    return from_north, lax.ppermute(x, "ty", ring("ty", 1))


def swap(x, phase):
    nx = lax.axis_size("tx")
    return lax.ppermute(
        x, "tx", [(i, (i + 1) % nx if i % 2 == phase else (i - 1) % nx) for i in range(nx)]
    )


def per_device(
    tracer_start,
    observed,
    east_speed,
    north_speed,
    mixing,
    vertical_mixing,
    relax_rate,
    level_count,
    face_east,
    face_north,
):
    levels, ny, nx = tracer_start.shape
    per_plane = 128 // GROUP
    plane_count = levels // per_plane
    pairs = (len(NAMES[:6]) * plane_count + 2) // 2
    fields = (
        tracer_start, east_speed, north_speed, mixing, relax_rate, vertical_mixing, observed,
        level_count, face_east, face_north,
    )
    half = levels // 2
    corner_planes = 2 * plane_count
    *fields, corners = call(
        rim_kernel,
        [jax.ShapeDtypeStruct(x.shape, x.dtype) for x in fields]
        + [(corner_planes, 8, nx)],
        [pltpu.SemaphoreType.DMA((10,))],
        *[pltpu.with_memory_space_constraint(x, pltpu.HBM) for x in fields],
        space=HBM,
    )
    corners_n, corners_s = both_ways(corners)
    planes, rows = call(
        column_kernel, [(2 * pairs, ny, nx), (levels + 1, 8, nx)], [], *fields[:8]
    )
    rows_n, rows_s = both_ways(rows)
    packed = (pairs * ny + corner_planes // 2 * 8, nx)
    one, two, own_corners = call(
        halves_kernel, [packed, packed, corners.shape], [],
        planes, corners_n, corners_s,
        cost=pl.CostEstimate(flops=10**10, bytes_accessed=0, transcendentals=0),
    )
    from_two = swap(two, 1)
    from_one = swap(one, 0)
    ext = (levels, ny + 8, 2 * nx)
    block = (levels, ny, 2 * nx)
    own = (levels, ny, nx)
    halo = (levels, ny + 16, nx)
    s, es, ns, mix, relax, vm, obs, count, east, north = fields
    *coefficients, damp, local, inv, q, r, moves = call(
        local_kernel,
        [own] * 10 + [jax.ShapeDtypeStruct((STEPS, 2 * nx, 2 * nx), jnp.bfloat16)],
        [],
        s, es, ns, mix, relax, vm, count, east, north, one,
        cost=pl.CostEstimate(flops=10**9, bytes_accessed=0, transcendentals=0),
    )
    ep, em, np_, nm, sink = coefficients
    outs = call(
        forward_kernel,
        [halo] * 4 + [own] + [halo] * 4 + [ext, block, block, (3,) + ext[1:], ext[1:]]
        + [(half + 1, 8, nx)],
        [
            planes.shape,
            corners.shape,
            block,
            ext,
            pltpu.VMEM((2 * plane_count, 10 * ny, 2 * nx), jnp.bfloat16),
            (levels, 3 * ny, nx),
            (levels, 8, nx),
            (2 * plane_count, 8, nx),
        ],
        s, obs, count, from_one, from_two, planes, own_corners, rows_n, rows_s,
        ep, em, np_, nm, sink, local, inv, q, r, moves,
    )
    ep_h, em_h, np_h, nm_h, _, inv_h, q_h, r_h, s_h, *outs = outs
    middle, late_damp, solved, counts, join, send = outs
    sent_n, sent_s = both_ways(send)
    faces = ep, em, np_, nm
    halo_faces = ep_h, em_h, np_h, nm_h
    part, late, run, rise = call(
        inner_kernel,
        [block] + [own] * 3,
        [],
        *faces, *halo_faces, late_damp, middle, solved, counts, s, s_h,
        cost=pl.CostEstimate(flops=0, bytes_accessed=8 << 20, transcendentals=0),
    )
    adjoint, gradient = call(
        backward_kernel,
        [own] * 2,
        [ext, own, own, (2 * plane_count, 8, nx), pltpu.SemaphoreType.DMA((half // UNROLL, 4))],
        *faces, inv, q, r, *halo_faces, inv_h, q_h, r_h,
        middle, damp, solved, counts, join, part, late, run, rise, sent_n, sent_s,
        out_space=HBM,
    )
    return adjoint, gradient


def solution(mesh):
    block = P(None, "ty", "tx")
    plane = P("ty", "tx")
    return jax.shard_map(
        per_device,
        mesh=mesh,
        in_specs=(block,) * 7 + (plane,) * 3,
        out_specs=(block, block),
        check_vma=False,
    )
```

```python
import functools

import jax
import jax.numpy as jnp
from jax import lax
from jax.experimental import pallas as pl
from jax.experimental.pallas import tpu as pltpu
from jax.sharding import PartitionSpec as P

F32 = jnp.float32
VMEM = pl.BlockSpec(memory_space=pltpu.VMEM)
HBM = pl.BlockSpec(memory_space=pltpu.HBM)
UNROLL = 8
STEPS = 4
GROUP = 8
NAMES = ("s", "es", "ns", "mix", "relax", "vm", "obs")


def call(kernel, outs, scratch, *args, space=VMEM, out_space=VMEM, cost=None):
    def typed(x):
        return x if isinstance(x, jax.ShapeDtypeStruct) else jax.ShapeDtypeStruct(x, F32)

    return pl.pallas_call(
        kernel,
        out_shape=[typed(x) for x in outs],
        in_specs=[space] * len(args),
        out_specs=[out_space] * len(outs),
        scratch_shapes=[pltpu.VMEM(x, F32) if isinstance(x, tuple) else x for x in scratch],
        compiler_params=pltpu.CompilerParams(vmem_limit_bytes=16 << 20),
        cost_estimate=cost,
    )(*args)


def iota(shape, dim):
    return lax.broadcasted_iota(jnp.int32, shape, dim)


def roll(x, shift, axis):
    if isinstance(shift, int):
        shift = shift % x.shape[axis]
        if shift == 0:
            return x
    return pltpu.roll(x, shift, axis)


def odd_column():
    return lax.rem(lax.axis_index("tx"), 2) == 1


def level_of(ref, name, level):
    if name == "vm":
        level = jnp.minimum(level, ref.shape[0] - 1)
    return ref[level].astype(F32)


def edge_rows(block):
    return jnp.where(iota((8, block.shape[1]), 0) < 4, block[:8], block[-8:])


def sublane(shape):
    return iota(shape, 0)


def step_count(counts, axis):
    return jnp.minimum(counts, shift_up(counts, axis))


def pair_rows(first, second):
    sub = sublane(first.shape)
    return jnp.where((sub == 1) | (sub == 2), roll(second, 2, 0), first)


def level_pair(levels, t):
    return (t, t), (levels - 1 - t, levels - 2 - t)


def in_all_groups(x):
    group = iota(x.shape, 1) // GROUP
    out = jnp.zeros(x.shape, F32)
    for g in range(x.shape[1] // GROUP):
        out = jnp.where(group == g, roll(x, GROUP * g + 4, 1), out)
    return out


def pack_rows(get, counts, level):
    tile = {name: edge_rows(get(name)) for name in NAMES[:6]}
    s = tile["s"]
    sub = sublane(s.shape)
    open_north = level < step_count(counts, 0)
    fn = jnp.where(
        open_north,
        (0.5 * tile["ns"] + tile["mix"]) * s + (0.5 * tile["ns"] - tile["mix"]) * shift_up(s, 0),
        0.0,
    )
    sink = jnp.where(level < counts, tile["relax"], 0.0)
    inner = jnp.where(sub == 0, -fn, jnp.where(sub == 7, shift_down(fn, 0), 0.0))
    base = s - sink * jnp.tanh(s) + inner
    first = pair_rows(s, base)
    first = jnp.where((sub == 3) | (sub == 4), roll(tile["es"], 4, 0), first)
    first = jnp.where((sub == 5) | (sub == 6), roll(tile["mix"], 6, 0), first)
    lane = iota(s.shape, 1)
    fe = (0.5 * tile["es"] + tile["mix"]) * s
    fe = fe + (0.5 * tile["es"] - tile["mix"]) * shift_up(s, 1)
    fe = jnp.where((level < step_count(counts, 1)) & (lane < s.shape[1] - 1), fe, 0.0)
    line = pair_rows(s, base - (fe - shift_down(fe, 1)))
    line = jnp.where((sub == 3) | (sub == 4), roll(tile["vm"], 4, 0), line)
    line = jnp.where(sub == 5, roll(tile["ns"], 6, 0), line)
    line = jnp.where(sub == 6, roll(tile["mix"], 7, 0), line)
    return line, first, pair_rows(tile["vm"], tile["ns"])


def merge_lines(north, south):
    sub = sublane(north.shape)
    return jnp.where((sub == 0) | (sub == 2) | (sub == 4), north, south)


def unpack_line(line):
    return {
        "s": line,
        "base": roll(line, 6, 0),
        "vm": roll(line, 4, 0),
        "ns": roll(line, 2, 0),
        "mix": roll(line, 1, 0),
    }


def unpack_rows(first, second):
    return {
        "s": first,
        "base": roll(first, 6, 0),
        "es": roll(first, 4, 0),
        "mix": roll(first, 2, 0),
        "vm": second,
        "ns": roll(second, 6, 0),
    }


def two_levels(x, y):
    sub = sublane(x.shape)
    return jnp.where((sub >= 3) & (sub <= 6), roll(y, 4, 0), x)


def shift_up(x, axis):
    return roll(x, -1, axis)


def shift_down(x, axis):
    return roll(x, 1, axis)


def rim_kernel(*args):
    fields = args[:10]
    s, es, ns, mix, relax, vm, obs, count, *_ = kept = args[10:20]
    corners, arrived = args[20:]
    copies = [pltpu.make_async_copy(fields[i], kept[i], arrived.at[i]) for i in range(10)]
    first = (7, 0, 1, 2, 3, 4, 5)
    rest = (6, 8, 9)
    for i in first + rest:
        copies[i].start()
    for i in first:
        copies[i].wait()
    refs = dict(zip(NAMES, (s, es, ns, mix, relax, vm, obs)))
    levels = s.shape[0]
    per_plane = 128 // GROUP
    small = (8, s.shape[2])
    group = iota(small, 1) // GROUP
    half = per_plane // 2
    plane_count = levels // per_plane
    counts = edge_rows(count[...].astype(F32))
    sub = sublane(small)

    def rims(p, carry):
        acc = jnp.zeros(small, F32)
        late = jnp.zeros(small, F32)
        for g in range(half):
            t = p * half + g
            for j, (k, link) in enumerate(level_pair(levels, t)):
                _, first, second = pack_rows(
                    lambda name: level_of(refs[name], name, link if name == "vm" else k),
                    counts,
                    k.astype(F32),
                )
                place = 2 * g + j
                acc = jnp.where(group == place, roll(first, GROUP * place + 4, 1), acc)
                second = jnp.where((sub == 3) | (sub == 4), roll(counts, 4, 0), second)
                late = jnp.where(group == place, roll(second, GROUP * place + 4, 1), late)
        corners[p] = acc
        corners[plane_count + p] = late
        return carry

    lax.fori_loop(0, plane_count, rims, 0)
    for i in rest:
        copies[i].wait()


def column_kernel(s, es, ns, mix, relax, vm, obs, count, planes, rows):
    refs = dict(zip(NAMES, (s, es, ns, mix, relax, vm, obs)))
    levels = s.shape[0]
    per_plane = 128 // GROUP
    plane_count = levels // per_plane
    shape = s.shape[1:]
    group = iota(shape, 1) // GROUP

    place = iota(shape, 1) % GROUP
    counts = edge_rows(count[...].astype(F32))
    rows[levels] = counts

    def lines(t, carry):
        for j, (k, link) in enumerate(level_pair(levels, t)):
            rows[2 * t + j], _, _ = pack_rows(
                lambda name: level_of(refs[name], name, link if name == "vm" else k),
                counts,
                k.astype(F32),
            )
        return carry

    lax.fori_loop(0, levels // 2, lines, 0, unroll=UNROLL)

    def columns(p, carry):
        packed = []
        for name in NAMES:
            acc = jnp.zeros(shape, F32)
            for g in range(per_plane):
                pair = level_pair(levels, p * (per_plane // 2) + g // 2)
                x = refs[name][pair[g % 2][name == "vm"]].astype(F32)
                acc = jnp.where(group == g, roll(x, GROUP * g + 4, 1), acc)
            packed.append(acc)
        seen = packed.pop()
        for name, distance in (("ns", 2), ("relax", 3)):
            i = NAMES.index(name)
            x = jnp.where(place == 0, roll(seen, -distance, 1), packed[i])
            packed[i] = jnp.where(place == GROUP - 1, roll(seen, distance, 1), x)
        for a, x in enumerate(packed):
            planes[a * plane_count + p] = x
        return carry

    lax.fori_loop(0, plane_count, columns, 0)
    total = len(NAMES[:6]) * plane_count
    planes[total] = in_all_groups(count[...].astype(F32))
    for p in range(total + 1, planes.shape[0]):
        planes[p] = jnp.zeros(shape, F32)


def merge_rows(north, south):
    return jnp.where(sublane(north.shape) % 2 == 0, north, south)


def halves_kernel(planes, corners_n, corners_s, one, two, kept):
    odd = odd_column()
    pairs = planes.shape[0] // 2
    ny = planes.shape[1]

    def put(place, x, y):
        low = iota(x.shape, 1) % GROUP < 4
        to_east = jnp.where(low, x, roll(y, 4, 1))
        to_west = jnp.where(low, roll(x, -4, 1), y)
        one[place] = jnp.where(odd, to_west, to_east)
        two[place] = jnp.where(odd, to_east, to_west)

    for h in range(pairs):
        put(pl.ds(h * ny, ny), planes[2 * h], planes[2 * h + 1])

    count = corners_n.shape[0]
    def corner(p):
        return merge_rows(corners_n[p], corners_s[p])

    for h in range(count // 2):
        x, y = corner(2 * h), corner(2 * h + 1)
        kept[2 * h] = x
        kept[2 * h + 1] = y
        put(pl.ds(pairs * ny + h * 8, 8), x, y)


def halves(x):
    nx = x.shape[1] // 2
    return x[:, :nx], x[:, nx:]


def east(x):
    main, side = halves(x)
    lane = iota(main.shape, 1)
    return jnp.concatenate(
        [
            jnp.where(lane == lane.shape[1] - 1, side, roll(main, -1, 1)),
            jnp.where(lane == 0, main, roll(side, 1, 1)),
        ],
        axis=1,
    )


def west(x):
    main, side = halves(x)
    lane = iota(main.shape, 1)
    return jnp.concatenate(
        [
            jnp.where(lane == 0, side, roll(main, 1, 1)),
            jnp.where(lane == lane.shape[1] - 1, main, roll(side, -1, 1)),
        ],
        axis=1,
    )


def pull_x(main, side, ep, em, em_side):
    lane = iota(main.shape, 1)
    ge = jnp.where(lane == lane.shape[1] - 1, side, roll(main, -1, 1)) - main
    return ep * ge + jnp.where(lane == 0, em_side * (main - side), roll(em * ge, 1, 1)), ge


def extend(main, side, rows=None, corners=None):
    top = jnp.concatenate([main, side], axis=1)
    if rows is None:
        return top
    return jnp.concatenate([top, jnp.concatenate([rows, corners], axis=1)], axis=0)


def solve_inward(levels, get, inv_q, carries):
    half = levels // 2
    inv, q = inv_q

    def step(t, carry):
        new = []
        for k, last in ((t, carry[0]), (levels - 1 - t, carry[1])):
            c = get(k) * inv(k) + q(k) * last
            carries[k] = c
            new.append(c)
        return tuple(new)

    zero = jnp.zeros(carries.shape[1:], F32)
    return lax.fori_loop(0, half, step, (zero, zero), unroll=UNROLL)


def solve_outward(levels, ends, ratio, join, carries, use, unroll=2):
    half = levels // 2
    high, low = ends
    upper = (high + ratio(half - 1) * low) * join
    lower = (low + ratio(half) * high) * join

    def block(i, last):
        m = half // STEPS - 1 - i
        for u in range(STEPS - 1, -1, -1):
            t = m * STEPS + u
            new = []
            for k, x in ((t, last[0]), (levels - 1 - t, last[1])):
                new.append(carries[k] + ratio(k) * x)
            use(t, m, u, *new)
            last = tuple(new)
        return last

    lax.fori_loop(0, half // STEPS, block, (lower, upper), unroll=unroll)


def merge_halos(odd, from_one, from_two, planes, start):
    size = planes.shape[1]
    low = iota(planes.shape[1:], 1) % GROUP < 4
    for h in range(planes.shape[0] // 2):
        place = pl.ds(start + h * size, size)
        a, b = from_one[place], from_two[place]
        west = jnp.where(odd, a, b)
        east = jnp.where(odd, b, a)
        planes[2 * h] = jnp.where(low, west, roll(east, 4, 1))
        planes[2 * h + 1] = jnp.where(low, roll(west, -4, 1), east)


def part_of_pull(x, ep, em, damp):
    ge = east(x) - x
    return x * damp + ep * ge + west(em * ge), ge


def local_kernel(
    s, es, ns, mix, relax, vm, count, east, north, after,
    ep_out, em_out, np_out, nm_out, sink_out, damp_out, local_out, inv_out, q_out, r_out,
    moves_out,
):
    levels, ny, nx = s.shape
    half = levels // 2
    counts = count[...].astype(F32)
    east_count = east[...].astype(F32)
    north_count = north[...].astype(F32)
    lane = iota((ny, nx), 1)
    sub = sublane((ny, nx))

    def prepare(k):
        level = k.astype(F32)
        state = s[k]
        diffusion = mix[k].astype(F32)
        speed_east = 0.5 * es[k].astype(F32)
        speed_north = 0.5 * ns[k].astype(F32)
        open_east = level < east_count
        open_north = level < north_count
        ep = jnp.where(open_east, speed_east + diffusion, 0.0)
        em = jnp.where(open_east, speed_east - diffusion, 0.0)
        np_ = jnp.where(open_north, speed_north + diffusion, 0.0)
        nm = jnp.where(open_north, speed_north - diffusion, 0.0)
        sink = jnp.where(level < counts, relax[k].astype(F32), 0.0)
        squeeze = jnp.tanh(state)
        ep_out[k] = ep
        em_out[k] = em
        np_out[k] = np_
        nm_out[k] = nm
        sink_out[k] = sink
        damp_out[k] = 1.0 - sink * (1.0 - squeeze * squeeze)
        fe = ep * state + em * shift_up(state, 1)
        fe = jnp.where(lane == nx - 1, 0.0, fe)
        fn = np_ * state + nm * jnp.where(sub == ny - 1, 0.0, shift_up(state, 0))
        flow = fe - shift_down(fe, 1)
        flow = flow + (fn - jnp.where(sub == 0, 0.0, shift_down(fn, 0)))
        local_out[k] = state - sink * squeeze - flow

    def factor(t, carry):
        new = []
        for (k, link_level), (ratio, outer) in zip(level_pair(levels, t), carry):
            prepare(k)
            link = jnp.where(
                link_level.astype(F32) + 1.0 < counts, vm[link_level].astype(F32), 0.0
            )
            inv = 1.0 / (1.0 + outer + link - outer * ratio)
            ratio = link * inv
            inv_out[k] = inv
            q_out[k] = outer * inv
            r_out[k] = ratio
            new.append((ratio, link))
        return tuple(new)

    zero = jnp.zeros((ny, nx), F32)
    lax.fori_loop(0, half, factor, ((zero, zero), (zero, zero)), unroll=UNROLL)

    source = iota((2 * nx, 2 * nx), 0) % nx
    target = iota((2 * nx, 2 * nx), 1)
    for u in range(STEPS):
        group = 2 * u + target // nx
        lane = target % nx
        column = jnp.where(lane < 4, 3 - lane, jnp.where(lane >= nx - 4, nx + 3 - lane, -nx))
        hit = source == GROUP * group + column
        moves_out[u] = jnp.where(hit, 1.0, 0.0).astype(jnp.bfloat16)


def whole(own, halo):
    ny = own.shape[0]
    return extend(own, halo[:ny], halo[ny + 8 :], halo[ny : ny + 8])


def forward_kernel(
    s, obs, count, from_one, from_two, own_planes, own_corners, rows_n, rows_s,
    ep, em, np_, nm, sink, local, inv, q, r, moves,
    ep_halo, em_halo, np_halo, nm_halo, sink_halo, inv_halo, q_halo, r_halo, s_halo,
    middle_out, damp_out, solved_out, counts_out, join_out, send,
    planes, corners, rhs, carries, packed, moved, moved_rows, sides,
):
    levels, ny, nx = s.shape
    half = levels // 2
    per_plane = 128 // GROUP
    plane_count = levels // per_plane
    odd = odd_column()
    merge_halos(odd, from_one, from_two, planes, 0)
    merge_halos(odd, from_one, from_two, corners, planes.shape[0] // 2 * planes.shape[1])

    def rim(index):
        return merge_lines(rows_n[index], rows_s[index])

    count_plane = len(NAMES[:6]) * plane_count
    side_counts = jnp.dot(
        jnp.concatenate([planes[count_plane]] + [roll(corners[plane_count], 4, 0)] * 2, axis=0).astype(
            jnp.bfloat16
        ),
        moves[0, :nx, :nx],
        preferred_element_type=F32,
    )
    count_ext = extend(
        count[...].astype(F32),
        side_counts[:ny],
        rim(levels),
        side_counts[ny : ny + 8],
    )
    east_ext = jnp.minimum(count_ext, east(count_ext))
    counts_out[0] = count_ext
    counts_out[1] = east_ext
    counts_out[2] = step_count(count_ext, 0)
    count_halo = jnp.concatenate(
        [count_ext[:ny, nx:], count_ext[ny:, nx:], count_ext[ny:, :nx]], axis=0
    )
    small_sub = sublane((8, nx))
    north_rows = jnp.where(small_sub == 7, counts_out[2, ny:, :nx], 0.0)
    lane = iota((ny, nx), 1)
    per_half = per_plane // 2

    strip = (ny + 8, nx)
    place = iota(strip, 1) % GROUP
    low = place < 4
    groups = iota(strip, 1) // GROUP
    from_top = groups % 2 == 0
    strip_sub = sublane(strip)

    def columns(p, carry):
        t = p * per_half + groups // 2
        level = jnp.where(from_top, t, levels - 1 - t).astype(F32)
        link_level = jnp.where(from_top, t, levels - 2 - t).astype(F32)

        def side_and_corner(a, c):
            return jnp.concatenate([a, c], axis=0)

        def strips(west):
            def pick(halo, own):
                near_side = low[: halo.shape[0]]
                return jnp.where(near_side, halo, own) if west else jnp.where(near_side, own, halo)

            x = unpack_rows(
                pick(corners[p], own_corners[p]),
                pick(corners[plane_count + p], own_corners[plane_count + p]),
            )
            side = {}
            for a, name in enumerate(NAMES[:6]):
                at = a * plane_count + p
                side[name] = pick(planes[at], own_planes[at])
            for name in NAMES[:4] + NAMES[5:6]:
                x[name] = side_and_corner(side[name], x[name])
            counts = side_and_corner(
                pick(planes[count_plane], own_planes[count_plane]),
                roll(pick(corners[plane_count + p], own_corners[plane_count + p]), 4, 0),
            )
            state = x["s"]
            open_east = level < step_count(counts, 1)
            open_north = (level < step_count(counts, 0)) & (
                (strip_sub < ny) | (strip_sub == ny + 7)
            )
            ep_s = jnp.where(open_east, 0.5 * x["es"] + x["mix"], 0.0)
            em_s = jnp.where(open_east, 0.5 * x["es"] - x["mix"], 0.0)
            np_s = jnp.where(open_north, 0.5 * x["ns"] + x["mix"], 0.0)
            nm_s = jnp.where(open_north, 0.5 * x["ns"] - x["mix"], 0.0)
            sink_s = jnp.where(level[:ny] < counts[:ny], side["relax"], 0.0)
            link = jnp.where(link_level + 1.0 < counts, x["vm"], 0.0)
            fe = ep_s * state + em_s * shift_up(state, 1)
            fe_west = shift_down(fe, 1)
            fn = np_s * state + nm_s * shift_up(state, 0)
            base = side_and_corner(side["s"] - sink_s * jnp.tanh(side["s"]), x["base"])
            right = base - (fe - fe_west) - (fn - shift_down(fn, 0))
            return (right, link, np_s, nm_s, ep_s, em_s, sink_s, state), fe, fe_west

        western, through_west, _ = strips(True)
        eastern, _, through_east = strips(False)
        seam = jnp.where(place == 3, through_west, through_east)
        seam = jnp.where(place == 5, roll(eastern[7], 1, 1), seam)
        both = [jnp.where(low[: a.shape[0]], a, b) for a, b in zip(western, eastern)]
        right, link, np_c, nm_c = (x[ny:] for x in both[:4])
        corner = pair_rows(right, link)
        corner = jnp.where((small_sub == 3) | (small_sub == 4), roll(seam[ny:], 4, 0), corner)
        corner = jnp.where(small_sub == 5, roll(np_c, 6, 0), corner)
        corner = jnp.where(small_sub == 6, roll(nm_c, 7, 0), corner)
        both = [x[:ny] for x in both]
        near_seam = planes[NAMES.index("relax") * plane_count + p]
        further = planes[NAMES.index("ns") * plane_count + p]
        side_place = place[:ny]
        seen = jnp.where(side_place < 3, roll(further, 2, 1), roll(near_seam, 3, 1))
        beyond = jnp.where(side_place > 4, roll(further, -2, 1), roll(near_seam, -3, 1))
        seen = jnp.where(side_place < 4, seen, beyond)
        both = both[:2] + [seen, seam[:ny]] + both[2:7] + [jnp.concatenate([corner] * 2, axis=0)]
        for i, x in enumerate(both):
            split(p, i * ny, x)
        return carry

    def split(p, at, x):
        for h, y in enumerate((x, roll(x, nx // 2, 1))):
            high = y.astype(jnp.bfloat16)
            packed[2 * p + h, at : at + ny, :nx] = high
            packed[2 * p + h, at : at + ny, nx:] = (y - high.astype(F32)).astype(jnp.bfloat16)

    lax.fori_loop(0, plane_count, columns, 0, unroll=plane_count)

    def unpack(u):
        move = moves[u]

        def place_both(m, carry):
            out = jnp.dot(packed[m], move, preferred_element_type=F32)
            t = m * STEPS + u
            for j, k in enumerate((t, levels - 1 - t)):
                x = out[:, j * nx : (j + 1) * nx]
                seam_x, np_x, nm_x, ep_x, em_x, sink_x, corner = (
                    x[i * ny : (i + 1) * ny] for i in range(3, 10)
                )
                corner = corner[:8]
                moved[k] = x[: 3 * ny]
                moved_rows[k] = corner
                ep_halo[k, :ny] = ep_x
                em_halo[k, :ny] = em_x
                np_halo[k, :ny] = np_x
                nm_halo[k, :ny] = nm_x
                np_halo[k, ny : ny + 8] = roll(corner, 2, 0)
                nm_halo[k, ny : ny + 8] = roll(corner, 1, 0)
                sink_halo[k] = sink_x
                s_halo[k, :ny] = seam_x
            return carry

        lax.fori_loop(0, 2 * plane_count, place_both, 0, unroll=2 * plane_count)

    for u in range(STEPS):
        unpack(u)

    def prepare(m, u, j, k, link_level):
        t = m * STEPS + u
        x = unpack_line(rim(2 * t + j))
        level = k.astype(F32)
        row = x["s"]
        open_north = level < north_rows
        np_r = jnp.where(open_north, 0.5 * x["ns"] + x["mix"], 0.0)
        nm_r = jnp.where(open_north, 0.5 * x["ns"] - x["mix"], 0.0)
        link_r = jnp.where(link_level.astype(F32) + 1.0 < count_halo[ny + 8 :], x["vm"], 0.0)
        corner = moved_rows[k]
        right, link = moved[k, :ny], moved[k, ny : 2 * ny]
        seam = s_halo[k, :ny]
        seam_rows = roll(corner, 4, 0)
        np_halo[k, ny + 8 :] = np_r
        nm_halo[k, ny + 8 :] = nm_r
        s_halo[k, ny + 8 :] = row

        own = s[k]
        last, first = lane == nx - 1, lane == 0
        through = jnp.where(first[:8], seam_rows, jnp.where(last[:8], -seam_rows, 0.0))
        fn = np_r * row + nm_r * shift_up(own[:8], 0)
        top = np_[k, ny - 8 :] * own[ny - 8 :]
        cross = nm[k, ny - 8 :] * shift_up(row, 0)
        from_block = jnp.where(small_sub == 0, shift_down(top + cross, 0), 0.0)
        right_r = x["base"] + through - (fn - from_block)

        inner = local[k] + jnp.where(first, seam, jnp.where(last, -seam, 0.0))
        low_rows = inner[:8] + jnp.where(small_sub == 0, shift_down(fn, 0), 0.0)
        high_rows = inner[ny - 8 :] - jnp.where(small_sub == 7, cross, 0.0)
        between = [inner[8 : ny - 8]] if ny > 16 else []
        inner = jnp.concatenate([low_rows] + between + [high_rows], axis=0)
        halo = jnp.concatenate([right, corner, right_r], axis=0)
        return inner, halo, jnp.concatenate([link, roll(corner, 6, 0), link_r], axis=0)

    def factor(m, carry):
        for u in range(STEPS):
            carry = factor_step(m, u, carry)
        return carry

    def factor_step(m, u, carry):
        t = m * STEPS + u
        new = []
        for j, (k, link_level) in enumerate(level_pair(levels, t)):
            ratio, c_own, c_halo, outer = carry[j]
            own, halo, link = prepare(m, u, j, k, link_level)
            inv_h = 1.0 / (1.0 + outer + link - outer * ratio)
            q_h = outer * inv_h
            ratio = link * inv_h
            c_own = own * inv[k] + q[k] * c_own
            c_halo = halo * inv_h + q_h * c_halo
            inv_halo[k] = inv_h
            q_halo[k] = q_h
            r_halo[k] = ratio
            carries[k] = whole(c_own, c_halo)
            new.append((ratio, c_own, c_halo, link))
        return tuple(new)

    zero = jnp.zeros(count_halo.shape, F32)
    begin = (zero, jnp.zeros((ny, nx), F32), zero, zero)
    (r_top, top_own, top_halo, _), (r_low, low_own, low_halo, _) = lax.fori_loop(
        0, half // STEPS, factor, (begin, begin), unroll=2
    )
    c_top, c_low = whole(top_own, top_halo), whole(low_own, low_halo)
    join = 1.0 / (1.0 - whole(r[half - 1], r_top) * whole(r[half], r_low))
    join_out[...] = join

    def ext(own, halo):
        return lambda k: whole(own[k], halo[k])

    def inner(own, halo):
        return lambda k: extend(own[k], halo[k, :ny])

    def spread(state, ep, em, np_, nm):
        fe = ep * state + em * east(state)
        fn = np_ * state + nm * shift_up(state, 0)
        return (fe - west(fe)) + (fn - shift_down(fn, 0))

    def both(one):
        def use(t, m, u, top, low):
            one(t, top, m, u, 0)
            one(levels - 1 - t, low, m, u, 1)

        return use

    def to_second(k, x, m, u, j):
        middle_out[k] = x
        state = x[:ny]
        squeeze = jnp.tanh(state)
        loss = inner(sink, sink_halo)(k)
        damp_out[k] = 1.0 - loss * (1.0 - squeeze * squeeze)
        fields = (ext(ep, ep_halo), ext(em, em_halo), ext(np_, np_halo), ext(nm, nm_halo))
        flow = spread(x, *(field(k) for field in fields))
        rhs[k] = state - flow[:ny] - loss * squeeze

    solve_outward(levels, (c_top, c_low), ext(r, r_halo), join, carries, both(to_second))

    main = carries.at[:, :ny]
    inv_q = inner(inv, inv_halo), inner(q, q_halo)
    ratio = inner(r, r_halo)
    ends = solve_inward(levels, lambda k: rhs[k], inv_q, main)

    def to_adjoint(k, x, m, u, j):
        seen = extend(obs[k].astype(F32), moved[k, 2 * ny :])
        rhs[k] = jnp.where(k.astype(F32) < count_ext[:ny], x - seen, 0.0)

    solve_outward(levels, ends, ratio, join[:ny], main, both(to_adjoint))
    ends = solve_inward(levels, lambda k: rhs[k], inv_q, main)

    def rim_part(k, solved):
        solved_out[k] = solved
        x = edge_rows(solved)
        main, side = halves(x)
        rows_of = lambda ref: edge_rows(ref[k])
        part, _ = pull_x(main, side, rows_of(ep), rows_of(em), edge_rows(em_halo[k, :ny]))
        part = part + main * edge_rows(damp_out[k, :, :nx])
        gn = shift_up(main, 0) - main
        sub = sublane(main.shape)
        part = part + jnp.where(
            sub == 0,
            rows_of(np_) * gn,
            jnp.where(sub == 7, shift_down(rows_of(nm) * gn, 0), 0.0),
        )
        return jnp.concatenate([pair_rows(main, part), side], axis=1)

    lane8 = iota((8, nx), 1)

    def to_send(t, m, u, top, low):
        pair = two_levels(rim_part(t, top), rim_part(levels - 1 - t, low))
        send[t] = pair[:, :nx]
        before = jnp.zeros((8, nx), F32) if u == STEPS - 1 else sides[m]
        moved = roll(pair[:, nx:], 2 * u + 1, 1)
        sides[m] = jnp.where(lane8 // 2 == u, moved, before)

    solve_outward(levels, ends, ratio, join[:ny], main, to_send, 3)
    both_sides = sides[0]
    for m in range(1, half // STEPS):
        place = m * 2 * STEPS
        both_sides = jnp.where(lane8 < place, both_sides, roll(sides[m], place, 1))
    send[half] = both_sides


def inner_kernel(
    ep, em, np_, nm, ep_halo, em_halo, np_halo, nm_halo, damp, middle, solved, counts,
    s, s_halo, part_out, late_out, run_out, rise_out,
):
    levels, ny, width = solved.shape
    nx = width // 2
    sub = sublane((ny, width))
    inside = sub < ny - 1
    lane = iota((ny, nx), 1)

    def inner(k, carry):
        x = solved[k]
        state = middle[k]
        field = lambda own, halo: extend(own[k], halo[k, :ny])
        part, ge = part_of_pull(x, field(ep, ep_halo), field(em, em_halo), damp[k])
        gn = jnp.where(inside, shift_up(x, 0) - x, 0.0)
        part_out[k] = (
            part + field(np_, np_halo) * gn + shift_down(field(nm, nm_halo) * gn, 0)
        )
        level = k.astype(F32)
        open_east = level < counts[1, :ny, :nx]
        open_north = level < counts[2, :ny, :nx]

        def slopes(main, next_column, rows):
            run = jnp.where(lane == nx - 1, next_column, roll(main, -1, 1)) - main
            rise = shift_up(jnp.concatenate([main, rows], axis=0), 0)[:ny] - main
            return jnp.where(open_east, run, 0.0), jnp.where(open_north, rise, 0.0)

        run, rise = slopes(state[:ny, :nx], state[:ny, nx:], state[ny:, :nx])
        late_out[k] = ge[:, :nx] * run + gn[:, :nx] * rise
        run_out[k], rise_out[k] = slopes(
            s[k], roll(s_halo[k, :ny], 1, 1), s_halo[k, ny + 8 :]
        )
        return carry

    lax.fori_loop(0, levels, inner, 0, unroll=UNROLL)


def backward_kernel(
    ep, em, np_, nm, inv, q, r, ep_halo, em_halo, np_halo, nm_halo, inv_halo, q_halo, r_halo,
    middle, damp, solved, counts, join, part, late, run, rise, rows_n, rows_s,
    adjoint_out, gradient_out, carries, adjoint, gradient, sides, sent,
):
    levels, ny, width = solved.shape
    nx = width // 2
    half = levels // 2
    sub = sublane((8, width))

    side = merge_rows(rows_n[half], rows_s[half])
    for m in range(half // STEPS):
        sides[m] = roll(side, -2 * STEPS * m, 1)

    def rims(m, u):
        t = m * STEPS + u
        line = merge_rows(rows_n[t], rows_s[t])
        corner = roll(sides[m], -1 - 2 * u, 1)
        both = jnp.concatenate([line, corner], axis=1)
        return both, roll(both, 4, 0)

    def across(k, rim):
        inner = part[k]
        near_part = roll(rim, 6, 0)
        south = solved[k, :8] - shift_down(rim, 0)
        north = shift_up(rim, 0) - solved[k, ny - 8 :]
        north_plus = whole(np_[k], np_halo[k])
        north_minus = whole(nm[k], nm_halo[k])
        np_rim, nm_rim = north_plus[ny:], north_minus[ny:]
        np_top, nm_top = north_plus[ny - 8 : ny], north_minus[ny - 8 : ny]
        low = inner[:8] + jnp.where(sub == 0, shift_down(nm_rim, 0) * south, 0.0)
        high = inner[ny - 8 :] + jnp.where(sub == 7, np_top * north, 0.0)
        outer = near_part + jnp.where(
            sub == 0, shift_down(nm_top * north, 0), np_rim * shift_up(south, 0)
        )
        rise = (shift_up(middle[k, ny:], 0) - middle[k, ny - 8 : ny])[:, :nx]
        open_north = (sub[:, :nx] == 7) & (k.astype(F32) < counts[2, ny - 8 : ny, :nx])
        extra = jnp.where(open_north, north[:, :nx] * rise, 0.0)
        gradient[k, : ny - 8] = late[k, : ny - 8]
        gradient[k, ny - 8 :] = late[k, ny - 8 :] + extra
        middle_rows = [inner[8 : ny - 8]] if ny > 16 else []
        return jnp.concatenate([low, *middle_rows, high, outer], axis=0)

    def late_steps(m, carry):
        for u in range(STEPS):
            t = m * STEPS + u
            new = []
            for k, rim, last in zip((t, levels - 1 - t), rims(m, u), carry):
                c = across(k, rim) * whole(inv[k], inv_halo[k])
                c = c + whole(q[k], q_halo[k]) * last
                carries[k] = c
                new.append(c)
            carry = tuple(new)
        return carry

    zero = jnp.zeros(carries.shape[1:], F32)
    ends = lax.fori_loop(0, half // STEPS, late_steps, (zero, zero), unroll=3)

    def early(k, x):
        main, side = halves(x[:ny])
        flow, ge = pull_x(main, side, ep[k], em[k], em_halo[k, :ny])
        result = main * damp[k] + flow
        column = x[:, :nx]
        gn = shift_up(column, 0) - column
        minus = jnp.concatenate([nm[k], nm_halo[k, ny + 8 :]], axis=0)
        result = result + np_[k] * gn[:ny] + shift_down(minus * gn, 0)[:ny]
        adjoint[k] = result
        gradient[k] = -(gradient[k] + ge * run[k] + gn[:ny] * rise[k])

    def copies(p):
        out = []
        for i, begin in enumerate((p * UNROLL, levels - (p + 1) * UNROLL)):
            place = pl.ds(begin, UNROLL)
            for j, (source, target) in enumerate(
                ((adjoint, adjoint_out), (gradient, gradient_out))
            ):
                out.append(
                    pltpu.make_async_copy(
                        source.at[place], target.at[place], sent.at[p, 2 * i + j]
                    )
                )
        return out

    high, low = ends
    steps = half // UNROLL
    ratio = lambda k: whole(r[k], r_halo[k])
    last = (low + ratio(half) * high) * join[...], (high + ratio(half - 1) * low) * join[...]

    def block(i, last):
        p = steps - 1 - i
        for g in range(UNROLL - 1, -1, -1):
            t = p * UNROLL + g
            new = []
            for k, x in ((t, last[0]), (levels - 1 - t, last[1])):
                x = carries[k] + ratio(k) * x
                early(k, x)
                new.append(x)
            last = tuple(new)
        for copy in copies(p):
            copy.start()
        return last

    lax.fori_loop(0, steps, block, last)
    for p in range(steps):
        for copy in copies(p):
            copy.wait()


def ring(axis, distance):
    count = lax.axis_size(axis)
    return [(i, (i + distance) % count) for i in range(count)]


def both_ways(x):
    from_north = lax.ppermute(x, "ty", ring("ty", -1))
    if lax.axis_size("ty") == 2:
        return from_north, from_north
    return from_north, lax.ppermute(x, "ty", ring("ty", 1))


def swap(x, phase):
    nx = lax.axis_size("tx")
    return lax.ppermute(
        x, "tx", [(i, (i + 1) % nx if i % 2 == phase else (i - 1) % nx) for i in range(nx)]
    )


def per_device(
    tracer_start,
    observed,
    east_speed,
    north_speed,
    mixing,
    vertical_mixing,
    relax_rate,
    level_count,
    face_east,
    face_north,
):
    levels, ny, nx = tracer_start.shape
    per_plane = 128 // GROUP
    plane_count = levels // per_plane
    pairs = (len(NAMES[:6]) * plane_count + 2) // 2
    fields = (
        tracer_start, east_speed, north_speed, mixing, relax_rate, vertical_mixing, observed,
        level_count, face_east, face_north,
    )
    half = levels // 2
    corner_planes = 2 * plane_count
    *fields, corners = call(
        rim_kernel,
        [jax.ShapeDtypeStruct(x.shape, x.dtype) for x in fields]
        + [(corner_planes, 8, nx)],
        [pltpu.SemaphoreType.DMA((10,))],
        *[pltpu.with_memory_space_constraint(x, pltpu.HBM) for x in fields],
        space=HBM,
    )
    corners_n, corners_s = both_ways(corners)
    planes, rows = call(
        column_kernel, [(2 * pairs, ny, nx), (levels + 1, 8, nx)], [], *fields[:8]
    )
    rows_n, rows_s = both_ways(rows)
    packed = (pairs * ny + corner_planes // 2 * 8, nx)
    one, two, own_corners = call(
        halves_kernel, [packed, packed, corners.shape], [],
        planes, corners_n, corners_s,
        cost=pl.CostEstimate(flops=10**10, bytes_accessed=0, transcendentals=0),
    )
    from_two = swap(two, 1)
    from_one = swap(one, 0)
    ext = (levels, ny + 8, 2 * nx)
    block = (levels, ny, 2 * nx)
    own = (levels, ny, nx)
    halo = (levels, ny + 16, nx)
    s, es, ns, mix, relax, vm, obs, count, east, north = fields
    *coefficients, damp, local, inv, q, r, moves = call(
        local_kernel,
        [own] * 10 + [jax.ShapeDtypeStruct((STEPS, 2 * nx, 2 * nx), jnp.bfloat16)],
        [],
        s, es, ns, mix, relax, vm, count, east, north, one,
        cost=pl.CostEstimate(flops=10**9, bytes_accessed=0, transcendentals=0),
    )
    ep, em, np_, nm, sink = coefficients
    outs = call(
        forward_kernel,
        [halo] * 4 + [own] + [halo] * 4 + [ext, block, block, (3,) + ext[1:], ext[1:]]
        + [(half + 1, 8, nx)],
        [
            planes.shape,
            corners.shape,
            block,
            ext,
            pltpu.VMEM((2 * plane_count, 10 * ny, 2 * nx), jnp.bfloat16),
            (levels, 3 * ny, nx),
            (levels, 8, nx),
            (2 * plane_count, 8, nx),
        ],
        s, obs, count, from_one, from_two, planes, own_corners, rows_n, rows_s,
        ep, em, np_, nm, sink, local, inv, q, r, moves,
    )
    ep_h, em_h, np_h, nm_h, _, inv_h, q_h, r_h, s_h, *outs = outs
    middle, late_damp, solved, counts, join, send = outs
    sent_n, sent_s = both_ways(send)
    faces = ep, em, np_, nm
    halo_faces = ep_h, em_h, np_h, nm_h
    part, late, run, rise = call(
        inner_kernel,
        [block] + [own] * 3,
        [],
        *faces, *halo_faces, late_damp, middle, solved, counts, s, s_h,
        cost=pl.CostEstimate(flops=0, bytes_accessed=8 << 20, transcendentals=0),
    )
    adjoint, gradient = call(
        backward_kernel,
        [own] * 2,
        [ext, own, own, (2 * plane_count, 8, nx), pltpu.SemaphoreType.DMA((half // UNROLL, 4))],
        *faces, inv, q, r, *halo_faces, inv_h, q_h, r_h,
        middle, damp, solved, counts, join, part, late, run, rise, sent_n, sent_s,
        out_space=HBM,
    )
    return adjoint, gradient


def solution(mesh):
    block = P(None, "ty", "tx")
    plane = P("ty", "tx")
    return jax.shard_map(
        per_device,
        mesh=mesh,
        in_specs=(block,) * 7 + (plane,) * 3,
        out_specs=(block, block),
        check_vma=False,
    )
```
